256 devices in a mesh: ctx: 16 (over y, z_lo), head: 4 (over x), dp: 4 (over z_hi, core).
Axes of the slice: x: 4, y: 4, z: 8 (z_hi: 2, z_lo: 4; z = z_hi * 4 + z_lo), core: 2. Of those that a mesh axis runs over, the one named last changes fastest.
Arguments:
- query_states: bfloat16 [32768, 8192], P(('dp', 'ctx'), 'head'), parts along dimension 0, may hold values from -6 to 6
- key_states: bfloat16 [32768, 1024], P(('dp', 'ctx'), 'head'), parts along dimension 0, may hold values from -6 to 6
- value_state_rows: bfloat16 [32768, 1024], P(('dp', 'ctx'), 'head'), parts along dimension 0, may hold values from -6 to 6
- grad_out: bfloat16 [32768, 8192], P(('dp', 'ctx'), 'head'), parts along dimension 0, may hold values from -6 to 6
- vis_blocks: int32 [256, 6], P('dp'), parts along dimension 0, may hold values from 0 to 63, as said below
- vis_count: int32 [256], P('dp'), parts along dimension 0, may hold values from 1 to 6
- vis_len: int32 [256, 6], P('dp'), parts along dimension 0, may hold values from 1 to 128, as said below
Outputs:
- attention: bfloat16 [32768, 8192], P(('dp', 'ctx'), 'head'), parts along dimension 0
- grad_query: bfloat16 [32768, 8192], P(('dp', 'ctx'), 'head'), parts along dimension 0
- grad_key: bfloat16 [32768, 1024], P(('dp', 'ctx'), 'head'), parts along dimension 0
- grad_value: bfloat16 [32768, 1024], P(('dp', 'ctx'), 'head'), parts along dimension 0
The draws below stay inside these ranges and needn't reach their ends.
There are 4 independent parts, one for each index of `dp`. The reference program is written for one: setup_inputs(seed, part) draws one part's arguments, and reference() takes and returns one part's arrays. A program takes and returns all parts, laid end to end along the dimension named above; each array names one. Nothing has to cross between parts.
Inputs may be any that keep to these rules, and one draw needn't show every extreme that they name: `vis_blocks`: slot 0 of row b is b itself; live slots 1 to vis_count[b] - 1 hold distinct blocks before b; slots at or past vis_count[b] hold b. Over the live slots of the 4 rows of one group of 4 consecutive query blocks, at most 2 distinct blocks of any other such group appear. `vis_len`: slot 0 and slots at or past vis_count hold 128.
All inputs are finite; a program needn't handle non-finite values.
Results may differ from the reference program's by a relative error of at most 0.012.
Values may be sent and summed in bfloat16 or wider, within the bound.
A program may use at most 128 MiB of HBM per device.

```python
import math
import jax
import jax.numpy as jnp
from jax import lax

HEAD_SIZE = 128
QUERY_HEADS = 64
KEY_VALUE_HEADS = 8
MASK_BLOCK_SIZE = 128
VIS = 6
CAP = 2
TOK_DEV = 512
BPD = 4
SEQUENCE_TOKENS = 8192
NB = 64


def tree_lists(key):
    group_count = NB // BPD
    key_pick = jax.random.fold_in(key, 11)
    key_order = jax.random.fold_in(key, 13)
    key_length = jax.random.fold_in(key, 14)
    key_last = jax.random.fold_in(key, 15)
    key_deal = jax.random.fold_in(key, 16)
    key_limit = jax.random.fold_in(key, 17)
    local_index = jnp.arange(BPD, dtype=jnp.int32)
    pick_score = jax.random.randint(key_pick, (group_count, group_count, BPD), 0, 1 << 20) * BPD + local_index
    unused_vals, picked = lax.top_k(pick_score, CAP)
    offered = jnp.any(picked[:, :, :, None] == local_index[None, None, None, :], axis=2)
    offered = offered.reshape(group_count, NB)
    block_index = jnp.arange(NB, dtype=jnp.int32)
    group_index = jnp.arange(group_count, dtype=jnp.int32)
    home_group = block_index // BPD
    remote_ok = offered & (home_group[None, :] < group_index[:, None])
    deal_width = BPD * (VIS - 1)
    order_score = jax.random.randint(key_order, (group_count, NB), 0, 1 << 20) * NB + block_index[None, :]
    order_score = jnp.where(remote_ok, order_score, -1)
    padded = jnp.concatenate([order_score, jnp.full((group_count, deal_width), -1, jnp.int32)], axis=1)
    top_vals, chosen = lax.top_k(padded, deal_width)
    valid = (top_vals >= 0).astype(jnp.int32)
    chosen = chosen.astype(jnp.int32)
    deal_index = jnp.arange(deal_width, dtype=jnp.int32)
    deal_score = jax.random.randint(key_deal, (group_count, deal_width), 0, 1 << 20) * deal_width + deal_index[None, :]
    deal_order = jnp.argsort(deal_score, axis=1, stable=True)
    chosen = jnp.take_along_axis(chosen, deal_order, axis=1)
    valid = jnp.take_along_axis(valid, deal_order, axis=1)
    chosen = jnp.transpose(chosen.reshape(group_count, VIS - 1, BPD), (0, 2, 1)).reshape(NB, VIS - 1)
    valid = jnp.transpose(valid.reshape(group_count, VIS - 1, BPD), (0, 2, 1)).reshape(NB, VIS - 1)
    prior_step = jnp.arange(1, BPD, dtype=jnp.int32)
    prior_blocks = block_index[:, None] - prior_step[None, :]
    prior_valid = (prior_step[None, :] <= (block_index % BPD)[:, None]).astype(jnp.int32)
    prior_blocks = jnp.where(prior_valid > 0, prior_blocks, block_index[:, None]).astype(jnp.int32)
    cand_blocks = jnp.concatenate([chosen, prior_blocks], axis=1)
    cand_valid = jnp.concatenate([valid, prior_valid], axis=1)
    packing = jnp.argsort(1 - cand_valid, axis=1, stable=True)
    chosen = jnp.take_along_axis(cand_blocks, packing, axis=1)[:, :VIS - 1]
    valid = jnp.take_along_axis(cand_valid, packing, axis=1)[:, :VIS - 1]
    limit = jax.random.randint(key_limit, (NB,), 1, VIS + 1).astype(jnp.int32)
    live_count = jnp.minimum(1 + jnp.sum(valid, axis=1), limit).astype(jnp.int32)
    slot_index = jnp.arange(VIS, dtype=jnp.int32)
    listed = jnp.concatenate([block_index[:, None], chosen], axis=1)
    blocks = jnp.where(slot_index[None, :] < live_count[:, None], listed, block_index[:, None])
    last_home = home_group == group_count - 1
    allowed_last = (block_index < NB - 1) & (last_home | offered[group_count - 1])
    last_score = jax.random.randint(key_last, (NB,), 0, 1 << 20) * NB + block_index
    last_score = jnp.where(allowed_last, last_score, -1)
    unused_last, last_pick = lax.top_k(last_score, VIS - 1)
    last_row = jnp.concatenate([jnp.array([NB - 1], jnp.int32), last_pick.astype(jnp.int32)])
    blocks = blocks.at[NB - 1].set(last_row)
    live_count = live_count.at[NB - 1].set(VIS)
    raw_lengths = jax.random.randint(key_length, (NB, VIS), 1, 2 * MASK_BLOCK_SIZE)
    lengths = jnp.minimum(raw_lengths, MASK_BLOCK_SIZE)
    live_other = (slot_index[None, :] >= 1) & (slot_index[None, :] < live_count[:, None])
    lengths = jnp.where(live_other, lengths, MASK_BLOCK_SIZE).astype(jnp.int32)
    return (blocks.astype(jnp.int32), live_count.astype(jnp.int32), lengths)


def draw_vis_blocks(key, part):
    return tree_lists(key)[0]


def draw_vis_count(key, part):
    return tree_lists(key)[1]


def draw_vis_len(key, part):
    return tree_lists(key)[2]


def rows_per_head(key, total_head_count, member):
    total_row_count = SEQUENCE_TOKENS
    own_key = jax.random.fold_in(key, 100 + member)
    values_drawn = jax.random.truncated_normal(own_key, -6.0, 6.0, (total_row_count, total_head_count, HEAD_SIZE), jnp.float32)
    return values_drawn.reshape(total_row_count, total_head_count * HEAD_SIZE)


def draw_query_states(key, part):
    return rows_per_head(key, QUERY_HEADS, 0).astype(jnp.bfloat16)


def draw_key_states(key, part):
    return rows_per_head(key, KEY_VALUE_HEADS, 1).astype(jnp.bfloat16)


def shard_levels(stream_key, shape, cuts, low, high):
    def one(dim, shards_of):
        heights = jax.random.uniform(jax.random.fold_in(jax.random.fold_in(stream_key, 6), dim), (shards_of,), jnp.float32, low / len(cuts), high / len(cuts))
        return jnp.repeat(jnp.exp(heights), shape[dim] // shards_of).reshape((-1,) + (1,) * (len(shape) - dim - 1))

    loudness = one(*cuts[0])
    for cut in cuts[1:]:
        loudness = loudness * one(*cut)
    return loudness


def noise(rng, shape, spread, most, cuts=(), kind=jnp.bfloat16):
    factor_of = shard_levels(rng, shape, cuts, -0.22, 0.18) if cuts else 1.0
    values = jax.random.normal(rng, shape, jnp.float32) * spread * factor_of
    return jnp.minimum(jnp.maximum(values, -most), most).astype(kind)


def setup_inputs(seed: int = 0, part: int = 0) -> dict:
    key_list = jax.random.split(jax.random.key(seed), 8)
    own_keys = jax.random.split(jax.random.fold_in(key_list[7], part), 8)
    return {
        "query_states": draw_query_states(jax.random.fold_in(jax.random.fold_in(key_list[7], part), 71), part),
        "key_states": draw_key_states(jax.random.fold_in(jax.random.fold_in(key_list[7], part), 71), part),
        "value_state_rows": noise(own_keys[2], (SEQUENCE_TOKENS, KEY_VALUE_HEADS * HEAD_SIZE), 1.0, 6.0, ((0, 16), (1, 4))),
        "grad_out": noise(own_keys[3], (SEQUENCE_TOKENS, QUERY_HEADS * HEAD_SIZE), 1.0, 6.0, ((0, 16), (1, 4))),
        "vis_blocks": draw_vis_blocks(jax.random.fold_in(jax.random.fold_in(key_list[7], part), 71), part),
        "vis_count": draw_vis_count(jax.random.fold_in(jax.random.fold_in(key_list[7], part), 71), part),
        "vis_len": draw_vis_len(jax.random.fold_in(jax.random.fold_in(key_list[7], part), 71), part),
    }


masked_score = -1e+30

def to_bf16(array):
    return lax.optimization_barrier(array.astype(jnp.bfloat16)).astype(jnp.float32)

def attend(query_block_rows, gradient_block_rows, key_value_slots, block_id, row_blocks, row_count, row_lens):
    inv_root = 1.0 / math.sqrt(HEAD_SIZE)
    key_value_width = KEY_VALUE_HEADS * HEAD_SIZE
    group_width_count = QUERY_HEADS // KEY_VALUE_HEADS
    total_slot_count = key_value_slots.shape[0]
    query_rows = query_block_rows.astype(jnp.float32).reshape(MASK_BLOCK_SIZE, KEY_VALUE_HEADS, group_width_count, HEAD_SIZE)
    output_gradients = gradient_block_rows.astype(jnp.float32).reshape(MASK_BLOCK_SIZE, KEY_VALUE_HEADS, group_width_count, HEAD_SIZE)
    key_portion = key_value_slots[:, :, :key_value_width].astype(jnp.float32).reshape(total_slot_count, MASK_BLOCK_SIZE, KEY_VALUE_HEADS, HEAD_SIZE)
    value_portion = key_value_slots[:, :, key_value_width:].astype(jnp.float32).reshape(total_slot_count, MASK_BLOCK_SIZE, KEY_VALUE_HEADS, HEAD_SIZE)
    query_pos = jnp.arange(MASK_BLOCK_SIZE, dtype=jnp.int32)[:, None, None]
    key_pos = jnp.arange(MASK_BLOCK_SIZE, dtype=jnp.int32)[None, None, :]
    slot_pos = jnp.arange(total_slot_count, dtype=jnp.int32)[None, :, None]
    visible = (slot_pos < row_count) & (key_pos < row_lens[None, :, None])
    visible = visible & ((row_blocks[None, :, None] != block_id) | (key_pos <= query_pos))
    scores = jnp.einsum('qgrd,vkgd->grqvk', query_rows, key_portion) * inv_root
    row_max = lax.optimization_barrier(jnp.max(jnp.where(visible, scores, masked_score), axis=(3, 4), keepdims=True))
    weights = jnp.exp(jnp.where(visible, scores - row_max, masked_score))
    soft_probs = weights / lax.optimization_barrier(jnp.sum(weights, axis=(3, 4), keepdims=True))
    probs_low = to_bf16(soft_probs)
    attention = jnp.einsum('grqvk,vkgd->qgrd', probs_low, value_portion).astype(jnp.bfloat16).reshape(MASK_BLOCK_SIZE, QUERY_HEADS * HEAD_SIZE)
    dprobs = jnp.einsum('qgrd,vkgd->grqvk', output_gradients, value_portion)
    row_delta = lax.optimization_barrier(jnp.sum(soft_probs * dprobs, axis=(3, 4), keepdims=True))
    dscores = to_bf16(soft_probs * (dprobs - row_delta) * inv_root)
    grad_query = jnp.einsum('grqvk,vkgd->qgrd', dscores, key_portion).astype(jnp.bfloat16).reshape(MASK_BLOCK_SIZE, QUERY_HEADS * HEAD_SIZE)
    grad_keys = jnp.einsum('grqvk,qgrd->vkgd', dscores, query_rows).reshape(total_slot_count, MASK_BLOCK_SIZE, key_value_width)
    grad_values = jnp.einsum('grqvk,qgrd->vkgd', probs_low, output_gradients).reshape(total_slot_count, MASK_BLOCK_SIZE, key_value_width)
    return (attention, grad_query, jnp.concatenate([grad_keys, grad_values], axis=2))

def reference(query_states, key_states, value_state_rows, grad_out, vis_blocks, vis_count, vis_len):
    key_value_width = KEY_VALUE_HEADS * HEAD_SIZE
    heads_each_group = TOK_DEV // MASK_BLOCK_SIZE
    group_total = NB // heads_each_group
    kv_blocks = jnp.concatenate([key_states, value_state_rows], axis=1).reshape(NB, MASK_BLOCK_SIZE, 2 * key_value_width)
    query_groups = query_states.reshape(group_total, heads_each_group, MASK_BLOCK_SIZE, QUERY_HEADS * HEAD_SIZE)
    grad_groups = grad_out.reshape(group_total, heads_each_group, MASK_BLOCK_SIZE, QUERY_HEADS * HEAD_SIZE)
    block_ids = jnp.arange(NB, dtype=jnp.int32).reshape(group_total, heads_each_group)
    block_lists = vis_blocks.reshape(group_total, heads_each_group, VIS)
    count_lists = vis_count.reshape(group_total, heads_each_group)
    length_lists = vis_len.reshape(group_total, heads_each_group, VIS)

    def group_step(carried, pieces):
        query_part, grad_part, ids_part, blocks_part, counts_part, lengths_part = pieces

        def block_step(inner):
            query_block_rows, gradient_block_rows, block_id, row_blocks, row_count, row_lens = inner
            return attend(query_block_rows, gradient_block_rows, kv_blocks[row_blocks], block_id, row_blocks, row_count, row_lens)
        attention, grad_query, slot_grads = lax.map(block_step, (query_part, grad_part, ids_part, blocks_part, counts_part, lengths_part))
        partial_sum = jnp.zeros((NB, MASK_BLOCK_SIZE, 2 * key_value_width), jnp.float32).at[blocks_part.reshape(-1)].add(slot_grads.reshape(heads_each_group * VIS, MASK_BLOCK_SIZE, 2 * key_value_width))
        return (carried + to_bf16(partial_sum), (attention, grad_query))
    summed, (attention, grad_query) = lax.scan(group_step, jnp.zeros((NB, MASK_BLOCK_SIZE, 2 * key_value_width), jnp.float32), (query_groups, grad_groups, block_ids, block_lists, count_lists, length_lists))
    summed = summed.reshape(SEQUENCE_TOKENS, 2 * key_value_width)
    return (attention.reshape(SEQUENCE_TOKENS, QUERY_HEADS * HEAD_SIZE), grad_query.reshape(SEQUENCE_TOKENS, QUERY_HEADS * HEAD_SIZE), summed[:, :key_value_width].astype(jnp.bfloat16), summed[:, key_value_width:].astype(jnp.bfloat16))
```

```python
import functools
import math

import jax
import jax.numpy as jnp
from jax import lax
from jax.experimental import pallas as pl
from jax.experimental.pallas import tpu as pltpu
from jax.sharding import PartitionSpec as P

D = 128
BLOCK = 128
PER = 4
CTX = 16
VIS = 6
CAP = 2
NEG = -1e30
INV_ROOT = 1.0 / math.sqrt(D)
EXP2_SCALE = INV_ROOT * math.log2(math.e)
MIB = 1 << 20


def barrier_all(me):
    barrier = pltpu.get_barrier_semaphore()
    for k in range(1, CTX):
        pl.semaphore_signal(
            barrier,
            inc=1,
            device_id={"ctx": lax.rem(me + k, CTX)},
            device_id_type=pl.DeviceIdType.MESH,
        )
    pl.semaphore_wait(barrier, CTX - 1)


def chosen(blocks_ref, count_ref, dst, src):
    low = jnp.int32(PER - 1)
    high = jnp.int32(0)
    for r in range(PER):
        row = dst * PER + r
        count = count_ref[row]
        for s in range(1, VIS):
            t = blocks_ref[row * VIS + s] - src * PER
            hit = (t >= 0) & (t < PER) & (s < count)
            low = jnp.minimum(low, jnp.where(hit, t, PER - 1))
            high = jnp.maximum(high, jnp.where(hit, t, 0))
    return low, high


def exchange_kernel(blocks_ref, count_ref, k_ref, v_ref, out_ref, packed, send_sem, recv_sem, own_sem):
    me = lax.axis_index("ctx")
    width = k_ref.shape[1]
    for t in range(PER):
        rows = pl.ds(t * BLOCK, BLOCK)
        packed[0, t, :, :width] = k_ref[rows, :]
        packed[0, t, :, width:] = v_ref[rows, :]
    own = pltpu.make_async_copy(packed.at[0], out_ref.at[pl.ds(0, PER)], own_sem)
    own.start()
    barrier_all(me)

    def copy_to(k):
        return pltpu.make_async_remote_copy(
            src_ref=packed.at[k, pl.ds(0, CAP)],
            dst_ref=out_ref.at[pl.ds(PER + CAP * me, CAP)],
            send_sem=send_sem.at[k],
            recv_sem=recv_sem.at[me],
            device_id={"ctx": me + k},
            device_id_type=pl.DeviceIdType.MESH,
        )

    def arrival(src):
        return pltpu.make_async_remote_copy(
            src_ref=packed.at[1, pl.ds(0, CAP)],
            dst_ref=out_ref.at[pl.ds(PER + CAP * src, CAP)],
            send_sem=send_sem.at[0],
            recv_sem=recv_sem.at[src],
            device_id={"ctx": me},
            device_id_type=pl.DeviceIdType.MESH,
        )

    @pl.loop(1, CTX - me)
    def _(k):
        for c, t in enumerate(chosen(blocks_ref, count_ref, me + k, me)):
            for ref, lanes in ((k_ref, pl.ds(0, width)), (v_ref, pl.ds(width, width))):
                block = ref[pl.ds(0, BLOCK), :]
                for other in range(1, PER):
                    block = jnp.where(t == other, ref[pl.ds(other * BLOCK, BLOCK), :], block)
                packed[k, c, :, lanes] = block
        copy_to(k).start()

    @pl.loop(0, me)
    def _(src):
        arrival(src).wait_recv()

    @pl.loop(1, CTX - me)
    def _(k):
        copy_to(k).wait_send()

    own.wait()


def attend_kernel(
    blocks_ref, count_ref, len_ref, q_ref, do_ref, kv_ref, attn_ref, dq_ref, part_ref,
    qs, dos, scores, dprobs, acc, place, low,
):
    i, g = pl.program_id(0), pl.program_id(1)
    me = lax.axis_index("ctx")
    heads = q_ref.shape[1] // D
    lanes = heads * BLOCK
    row = me * PER + i
    count = count_ref[row]

    @pl.when((i == 0) & (g == 0))
    def _():
        acc[...] = jnp.zeros_like(acc)
        for src in range(CTX):
            low[src] = PER
        for r in range(PER):
            for s in range(1, VIS):
                block = blocks_ref[(me * PER + r) * VIS + s]
                src = block // PER
                live = s < count_ref[me * PER + r]
                low[src] = jnp.where(live, jnp.minimum(low[src], block - src * PER), low[src])
        for r in range(PER):
            place[r * VIS] = r
            for s in range(1, VIS):
                block = blocks_ref[(me * PER + r) * VIS + s]
                src = block // PER
                t = block - src * PER
                far = PER + CAP * src + jnp.where(t == low[src], 0, 1)
                place[r * VIS + s] = jnp.where(src == me, t, far)

    for h in range(heads):
        qs[pl.ds(h * BLOCK, BLOCK), :] = q_ref[:, h * D : (h + 1) * D]
        dos[pl.ds(h * BLOCK, BLOCK), :] = do_ref[:, h * D : (h + 1) * D]

    k_at = pl.multiple_of(g * D, D)
    v_at = pl.multiple_of(kv_ref.shape[2] // 2 + g * D, D)
    nt = (((1,), (1,)), ((), ()))
    tn = (((0,), (0,)), ((), ()))
    f32 = jnp.float32
    key_pos = lax.broadcasted_iota(jnp.int32, (BLOCK, lanes), 0)

    def score(s, visible):
        at = place[i * VIS + s]
        raw = lax.dot_general(kv_ref[at, :, pl.ds(k_at, D)], qs[...], nt, preferred_element_type=f32)
        raw = jnp.where(visible, raw, NEG)
        scores[s] = raw
        return jnp.max(raw, axis=0, keepdims=True)

    query_pos = lax.rem(lax.broadcasted_iota(jnp.int32, (BLOCK, lanes), 1), BLOCK)
    top = score(0, key_pos <= query_pos)
    top = lax.fori_loop(
        1, count, lambda s, m: jnp.maximum(m, score(s, key_pos < len_ref[row * VIS + s])), top
    )
    shift = top * EXP2_SCALE

    def weigh(s, total):
        w = jnp.exp2(scores[s] * EXP2_SCALE - shift)
        scores[s] = w
        return total + jnp.sum(w, axis=0, keepdims=True)

    total = lax.fori_loop(0, count, weigh, jnp.zeros((1, lanes), f32))
    scale = 1.0 / total

    def mix(s, out):
        at = place[i * VIS + s]
        p = scores[s] * scale
        scores[s] = p
        low_p = p.astype(jnp.bfloat16)
        v = kv_ref[at, :, pl.ds(v_at, D)]
        acc[at, :, pl.ds(v_at, D)] += jnp.dot(low_p, dos[...], preferred_element_type=f32)
        dp = lax.dot_general(v, dos[...], nt, preferred_element_type=f32)
        dprobs[s] = dp
        attn, delta = out
        attn = attn + lax.dot_general(v, low_p, tn, preferred_element_type=f32)
        return attn, delta + jnp.sum(p * dp, axis=0, keepdims=True)

    attn, delta = lax.fori_loop(0, count, mix, (jnp.zeros((D, lanes), f32), jnp.zeros((1, lanes), f32)))
    for h in range(heads):
        attn_ref[:, h * D : (h + 1) * D] = attn[:, h * BLOCK : (h + 1) * BLOCK].T.astype(attn_ref.dtype)

    def back(s, dq):
        at = place[i * VIS + s]
        ds = (scores[s] * (dprobs[s] - delta) * INV_ROOT).astype(jnp.bfloat16)
        k = kv_ref[at, :, pl.ds(k_at, D)]
        acc[at, :, pl.ds(k_at, D)] += jnp.dot(ds, qs[...], preferred_element_type=f32)
        return dq + lax.dot_general(k, ds, tn, preferred_element_type=f32)

    dq = lax.fori_loop(0, count, back, jnp.zeros((D, lanes), f32))
    for h in range(heads):
        dq_ref[:, h * D : (h + 1) * D] = dq[:, h * BLOCK : (h + 1) * BLOCK].T.astype(dq_ref.dtype)

    @pl.when((i == pl.num_programs(0) - 1) & (g == pl.num_programs(1) - 1))
    def _():
        @pl.loop(0, acc.shape[0])
        def _(at):
            part_ref[at] = acc[at].astype(part_ref.dtype)


def return_kernel(blocks_ref, count_ref, part_ref, gk_ref, gv_ref, own, landed, total, send_sem, recv_sem, own_sem):
    me = lax.axis_index("ctx")
    width = gk_ref.shape[1]
    mine = pltpu.make_async_copy(part_ref.at[pl.ds(0, PER)], own, own_sem)
    mine.start()
    barrier_all(me)

    def copy_to(src):
        return pltpu.make_async_remote_copy(
            src_ref=part_ref.at[pl.ds(PER + CAP * src, CAP)],
            dst_ref=landed.at[me],
            send_sem=send_sem.at[src],
            recv_sem=recv_sem.at[me],
            device_id={"ctx": src},
            device_id_type=pl.DeviceIdType.MESH,
        )

    def arrival(dst):
        return pltpu.make_async_remote_copy(
            src_ref=part_ref.at[pl.ds(PER, CAP)],
            dst_ref=landed.at[dst],
            send_sem=send_sem.at[0],
            recv_sem=recv_sem.at[dst],
            device_id={"ctx": me},
            device_id_type=pl.DeviceIdType.MESH,
        )

    @pl.loop(0, me)
    def _(k):
        copy_to(me - 1 - k).start()

    mine.wait()
    total[...] = own[...].astype(jnp.float32)

    @pl.loop(me + 1, CTX)
    def _(dst):
        picks = chosen(blocks_ref, count_ref, dst, me)
        arrival(dst).wait_recv()
        for c in range(CAP):
            for t in range(PER):
                got = landed[dst, c].astype(jnp.float32)
                total[t] += jnp.where(picks[c] == t, got, 0.0)

    @pl.loop(0, me)
    def _(src):
        copy_to(src).wait_send()

    for t in range(PER):
        rows = pl.ds(t * BLOCK, BLOCK)
        gk_ref[rows, :] = total[t, :, :width].astype(gk_ref.dtype)
        gv_ref[rows, :] = total[t, :, width:].astype(gv_ref.dtype)


def body(query_states, key_states, value_state_rows, grad_out, vis_blocks, vis_count, vis_len):
    tokens, q_width = query_states.shape
    width = key_states.shape[1]
    kv_heads = width // D
    bf16, f32 = jnp.bfloat16, jnp.float32
    blocks = vis_blocks.reshape(-1)
    lens = vis_len.reshape(-1)
    held = PER + CAP * CTX
    smem = pl.BlockSpec(memory_space=pltpu.SMEM)
    vmem = pl.BlockSpec(memory_space=pltpu.VMEM)
    hbm = pl.BlockSpec(memory_space=pl.ANY)

    kv_all = pl.pallas_call(
        exchange_kernel,
        out_shape=jax.ShapeDtypeStruct((held, BLOCK, 2 * width), bf16),
        in_specs=[smem, smem, vmem, vmem],
        out_specs=hbm,
        scratch_shapes=[
            pltpu.VMEM((CTX, PER, BLOCK, 2 * width), bf16),
            pltpu.SemaphoreType.DMA((CTX,)),
            pltpu.SemaphoreType.DMA((CTX,)),
            pltpu.SemaphoreType.DMA,
        ],
        compiler_params=pltpu.CompilerParams(
            collective_id=0, has_side_effects=True, vmem_limit_bytes=24 * MIB
        ),
    )(blocks, vis_count, key_states, value_state_rows)

    heads_block = q_width // kv_heads
    lanes = heads_block // D * BLOCK
    tile = pl.BlockSpec((BLOCK, heads_block), lambda i, g: (i, g))
    attention, grad_query, part = pl.pallas_call(
        attend_kernel,
        grid=(PER, kv_heads),
        out_shape=(
            jax.ShapeDtypeStruct((tokens, q_width), bf16),
            jax.ShapeDtypeStruct((tokens, q_width), bf16),
            jax.ShapeDtypeStruct((held, BLOCK, 2 * width), bf16),
        ),
        in_specs=[smem, smem, smem, tile, tile, vmem],
        out_specs=(tile, tile, vmem),
        scratch_shapes=[
            pltpu.VMEM((lanes, D), bf16),
            pltpu.VMEM((lanes, D), bf16),
            pltpu.VMEM((VIS, BLOCK, lanes), f32),
            pltpu.VMEM((VIS, BLOCK, lanes), f32),
            pltpu.VMEM((held, BLOCK, 2 * width), f32),
            pltpu.SMEM((PER * VIS,), jnp.int32),
            pltpu.SMEM((CTX,), jnp.int32),
        ],
        compiler_params=pltpu.CompilerParams(vmem_limit_bytes=56 * MIB),
    )(blocks, vis_count, lens, query_states, grad_out, kv_all)

    grad_key, grad_value = pl.pallas_call(
        return_kernel,
        out_shape=(
            jax.ShapeDtypeStruct((tokens, width), bf16),
            jax.ShapeDtypeStruct((tokens, width), bf16),
        ),
        in_specs=[smem, smem, hbm],
        out_specs=(vmem, vmem),
        scratch_shapes=[
            pltpu.VMEM((PER, BLOCK, 2 * width), bf16),
            pltpu.VMEM((CTX, CAP, BLOCK, 2 * width), bf16),
            pltpu.VMEM((PER, BLOCK, 2 * width), f32),
            pltpu.SemaphoreType.DMA((CTX,)),
            pltpu.SemaphoreType.DMA((CTX,)),
            pltpu.SemaphoreType.DMA,
        ],
        compiler_params=pltpu.CompilerParams(
            collective_id=1, has_side_effects=True, vmem_limit_bytes=24 * MIB
        ),
    )(blocks, vis_count, part)
    return attention, grad_query, grad_key, grad_value


def solution(mesh):
    rows = P(("dp", "ctx"), "head")
    return jax.shard_map(
        body,
        mesh=mesh,
        in_specs=(rows, rows, rows, rows, P("dp", None), P("dp"), P("dp", None)),
        out_specs=(rows, rows, rows, rows),
        check_vma=False,
    )
```

```python
import functools
import math

import jax
import jax.numpy as jnp
from jax import lax
from jax.experimental import pallas as pl
from jax.experimental.pallas import tpu as pltpu
from jax.sharding import PartitionSpec as P

D = 128
BLOCK = 128
PER = 4
SIDE = 4
CTX = SIDE * SIDE
VIS = 6
CAP = 2
ROW = SIDE * PER
NEG = -1e30
INV_ROOT = 1.0 / math.sqrt(D)
EXP2_SCALE = INV_ROOT * math.log2(math.e)
MIB = 1 << 20
MESH = pl.DeviceIdType.MESH


def coords():
    me = lax.axis_index("ctx")
    return me, me // SIDE, lax.rem(me, SIDE)


def at(y, z):
    return {"ctx": lax.rem(y + SIDE, SIDE) * SIDE + z}


def barrier_neighbours(y, z):
    barrier = pltpu.get_barrier_semaphore()

    def greet(where):
        pl.semaphore_signal(barrier, inc=1, device_id=where, device_id_type=MESH)

    greet(at(y + 1, z))
    greet(at(y - 1, z))
    pl.when(z > 0)(lambda: greet(at(y, z - 1)))
    pl.when(z < SIDE - 1)(lambda: greet(at(y, z + 1)))
    pl.semaphore_wait(barrier, 2 + jnp.where(z > 0, 1, 0) + jnp.where(z < SIDE - 1, 1, 0))


def chosen(blocks_ref, count_ref, dst, src):
    low = jnp.int32(PER - 1)
    high = jnp.int32(0)
    for r in range(PER):
        row = dst * PER + r
        count = count_ref[row]
        for s in range(1, VIS):
            t = blocks_ref[row * VIS + s] - src * PER
            hit = (t >= 0) & (t < PER) & (s < count)
            low = jnp.minimum(low, jnp.where(hit, t, PER - 1))
            high = jnp.maximum(high, jnp.where(hit, t, 0))
    return low, high


def far_at(y, z):
    return pl.ds(ROW + (y * SIDE + z) * CAP, CAP)


STEPS = 2 * SIDE - 1


def nth(n, z):
    d = (n + 1) // 2
    return z + jnp.where(lax.rem(n, 2) == 1, -d, d), d


def exchange_kernel(
    blocks_ref, count_ref, k_ref, v_ref, out_ref,
    row, packed, relay,
    z_recv, up_send, down_send, far_recv, y_send, relay_recv, relay_send, keep_sem,
):
    me, y, z = coords()
    width = k_ref.shape[1]
    for t in range(PER):
        rows = pl.ds(t * BLOCK, BLOCK)
        row[z, t, :, :width] = k_ref[rows, :]
        row[z, t, :, width:] = v_ref[rows, :]
    barrier_neighbours(y, z)

    def z_copy(zs, to, sems):
        return pltpu.make_async_remote_copy(
            src_ref=row.at[zs],
            dst_ref=row.at[zs],
            send_sem=sems.at[zs],
            recv_sem=z_recv.at[zs],
            device_id=at(y, to),
            device_id_type=MESH,
        )

    def y_near(yd, zs):
        return pltpu.make_async_remote_copy(
            src_ref=packed.at[yd, zs],
            dst_ref=out_ref.at[far_at(y, zs)],
            send_sem=y_send.at[yd * SIDE + zs],
            recv_sem=far_recv.at[y * SIDE + zs],
            device_id=at(yd, z),
            device_id_type=MESH,
        )

    def y_far(yd, zs):
        return pltpu.make_async_remote_copy(
            src_ref=packed.at[yd, zs],
            dst_ref=relay.at[zs],
            send_sem=y_send.at[yd * SIDE + zs],
            recv_sem=relay_recv.at[zs],
            device_id=at(jnp.where(y == 0, SIDE - 1, 2), z),
            device_id_type=MESH,
        )

    def relay_copy(zs):
        return pltpu.make_async_remote_copy(
            src_ref=relay.at[zs],
            dst_ref=out_ref.at[far_at(3 - y, zs)],
            send_sem=relay_send.at[zs],
            recv_sem=far_recv.at[(3 - y) * SIDE + zs],
            device_id=at(5 - y, z),
            device_id_type=MESH,
        )

    def keep(zs):
        return pltpu.make_async_copy(row.at[zs], out_ref.at[pl.ds(zs * PER, PER)], keep_sem.at[zs])

    def wanted(zs):
        inside = (zs >= 0) & (zs < SIDE)
        return inside, inside & ((zs <= z) | (y < SIDE - 1))

    def pack(yd, zs):
        picks = chosen(blocks_ref, count_ref, yd * SIDE + z, y * SIDE + zs)
        for c in range(CAP):
            block = row[zs, 0]
            for t in range(1, PER):
                block = jnp.where(picks[c] == t, row[zs, t], block)
            packed[yd, zs, c] = block

    def step(n):
        zs, d = nth(n, z)
        inside, mine = wanted(zs)

        @pl.when(mine)
        def _():
            pl.when(d > 0)(lambda: z_copy(zs, z, up_send).wait_recv())
            pl.when((zs <= z) & (z < SIDE - 1))(lambda: z_copy(zs, z + 1, up_send).start())
            pl.when((zs >= z) & (z > 0) & (y < SIDE - 1))(
                lambda: z_copy(zs, z - 1, down_send).start()
            )
            keep(zs).start()

        @pl.when(inside)
        def _():
            @pl.loop(0, SIDE - 1 - y)
            def _(h):
                hop = jnp.where(y == 2, 1, jnp.where(h == 0, 2, jnp.where(h == 1, 1, 3)))
                yd = y + hop
                pack(yd, zs)
                pl.when(hop == 2)(lambda: y_far(yd, zs).start())
                pl.when(hop != 2)(lambda: y_near(yd, zs).start())

    def relay_step(n):
        zs, _ = nth(n, z)

        @pl.when((zs >= 0) & (zs < SIDE) & (y >= 2))
        def _():
            pltpu.make_async_remote_copy(
                src_ref=relay.at[zs],
                dst_ref=relay.at[zs],
                send_sem=relay_send.at[zs],
                recv_sem=relay_recv.at[zs],
                device_id=at(y, z),
                device_id_type=MESH,
            ).wait_recv()
            relay_copy(zs).start()

    @pl.loop(0, STEPS + 1)
    def _(n):
        pl.when(n < STEPS)(lambda: step(n))
        pl.when(n > 0)(lambda: relay_step(n - 1))

    @pl.loop(0, y * SIDE)
    def _(n):
        pltpu.make_async_remote_copy(
            src_ref=packed.at[0, 0],
            dst_ref=out_ref.at[pl.ds(ROW + n * CAP, CAP)],
            send_sem=relay_send.at[0],
            recv_sem=far_recv.at[n],
            device_id=at(y, z),
            device_id_type=MESH,
        ).wait_recv()

    @pl.loop(0, SIDE)
    def _(zs):
        _, mine = wanted(zs)

        @pl.when(mine)
        def _():
            pl.when((zs <= z) & (z < SIDE - 1))(lambda: z_copy(zs, z + 1, up_send).wait_send())
            pl.when((zs >= z) & (z > 0) & (y < SIDE - 1))(
                lambda: z_copy(zs, z - 1, down_send).wait_send()
            )
            keep(zs).wait()

        @pl.loop(y + 1, SIDE)
        def _(yd):
            y_near(yd, zs).wait_send()

        pl.when(y >= 2)(lambda: relay_copy(zs).wait_send())


def attend_kernel(
    blocks_ref, count_ref, len_ref, q_ref, do_ref, kv_ref, attn_ref, dq_ref, part_ref,
    qs, dos, scores, dprobs, acc, place, low,
):
    i, g = pl.program_id(0), pl.program_id(1)
    me = lax.axis_index("ctx")
    heads = q_ref.shape[1] // D
    lanes = heads * BLOCK
    row = me * PER + i
    count = count_ref[row]

    @pl.when((i == 0) & (g == 0))
    def _():
        acc[...] = jnp.zeros_like(acc)
        for src in range(CTX):
            low[src] = PER
        for r in range(PER):
            for s in range(1, VIS):
                block = blocks_ref[(me * PER + r) * VIS + s]
                src = block // PER
                live = s < count_ref[me * PER + r]
                low[src] = jnp.where(live, jnp.minimum(low[src], block - src * PER), low[src])
        for r in range(PER):
            place[r * VIS] = lax.rem(me, SIDE) * PER + r
            for s in range(1, VIS):
                block = blocks_ref[(me * PER + r) * VIS + s]
                src = block // PER
                t = block - src * PER
                far = ROW + CAP * src + jnp.where(t == low[src], 0, 1)
                near = lax.rem(src, SIDE) * PER + t
                place[r * VIS + s] = jnp.where(src // SIDE == me // SIDE, near, far)

    for h in range(heads):
        qs[pl.ds(h * BLOCK, BLOCK), :] = q_ref[:, h * D : (h + 1) * D]
        dos[pl.ds(h * BLOCK, BLOCK), :] = do_ref[:, h * D : (h + 1) * D]

    k_at = pl.multiple_of(g * D, D)
    v_at = pl.multiple_of(kv_ref.shape[2] // 2 + g * D, D)
    nt = (((1,), (1,)), ((), ()))
    tn = (((0,), (0,)), ((), ()))
    f32 = jnp.float32
    key_pos = lax.broadcasted_iota(jnp.int32, (BLOCK, lanes), 0)

    def score(s, visible):
        at = place[i * VIS + s]
        raw = lax.dot_general(kv_ref[at, :, pl.ds(k_at, D)], qs[...], nt, preferred_element_type=f32)
        raw = jnp.where(visible, raw, NEG)
        scores[s] = raw
        return jnp.max(raw, axis=0, keepdims=True)

    query_pos = lax.rem(lax.broadcasted_iota(jnp.int32, (BLOCK, lanes), 1), BLOCK)
    top = score(0, key_pos <= query_pos)
    top = lax.fori_loop(
        1, count, lambda s, m: jnp.maximum(m, score(s, key_pos < len_ref[row * VIS + s])), top
    )
    shift = top * EXP2_SCALE

    def weigh(s, total):
        w = jnp.exp2(scores[s] * EXP2_SCALE - shift)
        scores[s] = w
        return total + jnp.sum(w, axis=0, keepdims=True)

    total = lax.fori_loop(0, count, weigh, jnp.zeros((1, lanes), f32))
    scale = 1.0 / total

    def mix(s, out):
        at = place[i * VIS + s]
        p = scores[s] * scale
        scores[s] = p
        low_p = p.astype(jnp.bfloat16)
        v = kv_ref[at, :, pl.ds(v_at, D)]
        acc[at, :, pl.ds(v_at, D)] += jnp.dot(low_p, dos[...], preferred_element_type=f32)
        dp = lax.dot_general(v, dos[...], nt, preferred_element_type=f32)
        dprobs[s] = dp
        attn, delta = out
        attn = attn + lax.dot_general(v, low_p, tn, preferred_element_type=f32)
        return attn, delta + jnp.sum(p * dp, axis=0, keepdims=True)

    attn, delta = lax.fori_loop(0, count, mix, (jnp.zeros((D, lanes), f32), jnp.zeros((1, lanes), f32)))
    for h in range(heads):
        attn_ref[:, h * D : (h + 1) * D] = attn[:, h * BLOCK : (h + 1) * BLOCK].T.astype(attn_ref.dtype)

    def back(s, dq):
        at = place[i * VIS + s]
        ds = (scores[s] * (dprobs[s] - delta) * INV_ROOT).astype(jnp.bfloat16)
        k = kv_ref[at, :, pl.ds(k_at, D)]
        acc[at, :, pl.ds(k_at, D)] += jnp.dot(ds, qs[...], preferred_element_type=f32)
        return dq + lax.dot_general(k, ds, tn, preferred_element_type=f32)

    dq = lax.fori_loop(0, count, back, jnp.zeros((D, lanes), f32))
    for h in range(heads):
        dq_ref[:, h * D : (h + 1) * D] = dq[:, h * BLOCK : (h + 1) * BLOCK].T.astype(dq_ref.dtype)

    @pl.when((i == pl.num_programs(0) - 1) & (g == pl.num_programs(1) - 1))
    def _():
        @pl.loop(0, acc.shape[0])
        def _(at):
            part_ref[at] = acc[at].astype(part_ref.dtype)


def return_kernel(
    blocks_ref, count_ref, part_ref, gk_ref, gv_ref,
    own, landed, relay, running, from_left, from_right, total,
    y_send, y_recv, relay_send, relay_recv, z_send, left_recv, right_recv, own_sem,
):
    me, y, z = coords()
    width = gk_ref.shape[1]

    def own_copy(zs):
        return pltpu.make_async_copy(part_ref.at[pl.ds(zs * PER, PER)], own.at[zs], own_sem.at[zs])

    for zs in range(SIDE):
        pl.when(zs <= z)(lambda: own_copy(zs).start())
    barrier_neighbours(y, z)

    def y_near(ys, zs):
        return pltpu.make_async_remote_copy(
            src_ref=part_ref.at[far_at(ys, zs)],
            dst_ref=landed.at[y, zs],
            send_sem=y_send.at[ys * SIDE + zs],
            recv_sem=y_recv.at[y * SIDE + zs],
            device_id=at(ys, z),
            device_id_type=MESH,
        )

    def y_far(ys, zs):
        return pltpu.make_async_remote_copy(
            src_ref=part_ref.at[far_at(ys, zs)],
            dst_ref=relay.at[zs],
            send_sem=y_send.at[ys * SIDE + zs],
            recv_sem=relay_recv.at[zs],
            device_id=at(5 - y, z),
            device_id_type=MESH,
        )

    def relay_copy(zs):
        return pltpu.make_async_remote_copy(
            src_ref=relay.at[zs],
            dst_ref=landed.at[5 - y, zs],
            send_sem=relay_send.at[zs],
            recv_sem=y_recv.at[(5 - y) * SIDE + zs],
            device_id=at(3 - y, z),
            device_id_type=MESH,
        )

    def z_copy(zs, to, landing, sems):
        return pltpu.make_async_remote_copy(
            src_ref=running.at[zs],
            dst_ref=landing.at[zs],
            send_sem=z_send.at[zs],
            recv_sem=sems.at[zs],
            device_id=at(y, to),
            device_id_type=MESH,
        )

    def inside(zs):
        return (zs >= 0) & (zs < SIDE)

    @pl.loop(0, STEPS)
    def _(n):
        zs, _ = nth(STEPS - 1 - n, z)

        @pl.when(inside(zs))
        def _():
            pl.when(y >= 2)(lambda: y_far(y - 2, zs).start())
            pl.when(y >= 1)(lambda: y_near(y - 1, zs).start())
            pl.when(y >= 3)(lambda: y_near(y - 3, zs).start())

    def relay_step(n):
        zs, _ = nth(n, z)

        @pl.when(inside(zs) & (y >= 2))
        def _():
            pltpu.make_async_remote_copy(
                src_ref=relay.at[zs],
                dst_ref=relay.at[zs],
                send_sem=relay_send.at[zs],
                recv_sem=relay_recv.at[zs],
                device_id=at(y, z),
                device_id_type=MESH,
            ).wait_recv()
            relay_copy(zs).start()

    def step(n):
        zs, d = nth(n, z)

        @pl.when(inside(zs) & ((zs <= z) | (y < SIDE - 1)))
        def _():
            @pl.when(zs <= z)
            def _():
                own_copy(zs).wait()
                total[...] = own[zs].astype(jnp.float32)

            @pl.when(zs > z)
            def _():
                total[...] = jnp.zeros_like(total)

            @pl.loop(y + 1, SIDE)
            def _(yd):
                picks = chosen(blocks_ref, count_ref, yd * SIDE + z, y * SIDE + zs)
                pltpu.make_async_remote_copy(
                    src_ref=landed.at[yd, zs],
                    dst_ref=landed.at[yd, zs],
                    send_sem=relay_send.at[0],
                    recv_sem=y_recv.at[yd * SIDE + zs],
                    device_id=at(y, z),
                    device_id_type=MESH,
                ).wait_recv()
                for c in range(CAP):
                    for t in range(PER):
                        got = landed[yd, zs, c].astype(jnp.float32)
                        total[t] += jnp.where(picks[c] == t, got, 0.0)

            @pl.when((zs <= z) & (z < SIDE - 1))
            def _():
                z_copy(zs, z, from_right, right_recv).wait_recv()
                total[...] += from_right[zs].astype(jnp.float32)

            @pl.when((zs >= z) & (z > 0) & (y < SIDE - 1))
            def _():
                z_copy(zs, z, from_left, left_recv).wait_recv()
                total[...] += from_left[zs].astype(jnp.float32)

            @pl.when(d > 0)
            def _():
                running[zs] = total[...].astype(running.dtype)
                pl.when(zs < z)(lambda: z_copy(zs, z - 1, from_right, right_recv).start())
                pl.when(zs > z)(lambda: z_copy(zs, z + 1, from_left, left_recv).start())

    @pl.loop(0, STEPS)
    def _(n):
        relay_step(STEPS - 1 - n)
        step(STEPS - 1 - n)

    for t in range(PER):
        rows = pl.ds(t * BLOCK, BLOCK)
        gk_ref[rows, :] = total[t, :, :width].astype(gk_ref.dtype)
        gv_ref[rows, :] = total[t, :, width:].astype(gv_ref.dtype)

    @pl.loop(0, SIDE)
    def _(zs):
        pl.when((zs < z) | ((zs > z) & (y < SIDE - 1)))(
            lambda: z_copy(zs, z, from_right, right_recv).wait_send()
        )

        @pl.loop(0, y)
        def _(ys):
            y_near(ys, zs).wait_send()

        pl.when(y >= 2)(lambda: relay_copy(zs).wait_send())


def body(query_states, key_states, value_state_rows, grad_out, vis_blocks, vis_count, vis_len):
    tokens, q_width = query_states.shape
    width = key_states.shape[1]
    kv_heads = width // D
    bf16, f32 = jnp.bfloat16, jnp.float32
    blocks = vis_blocks.reshape(-1)
    lens = vis_len.reshape(-1)
    held = ROW + CAP * SIDE * (SIDE - 1)
    sems = lambda n: pltpu.SemaphoreType.DMA((n,))
    smem = pl.BlockSpec(memory_space=pltpu.SMEM)
    vmem = pl.BlockSpec(memory_space=pltpu.VMEM)
    hbm = pl.BlockSpec(memory_space=pl.ANY)

    kv_all = pl.pallas_call(
        exchange_kernel,
        out_shape=jax.ShapeDtypeStruct((held, BLOCK, 2 * width), bf16),
        in_specs=[smem, smem, vmem, vmem],
        out_specs=hbm,
        scratch_shapes=[
            pltpu.VMEM((SIDE, PER, BLOCK, 2 * width), bf16),
            pltpu.VMEM((SIDE, SIDE, CAP, BLOCK, 2 * width), bf16),
            pltpu.VMEM((SIDE, CAP, BLOCK, 2 * width), bf16),
            sems(SIDE),
            sems(SIDE),
            sems(SIDE),
            sems(CTX),
            sems(CTX),
            sems(SIDE),
            sems(SIDE),
            sems(SIDE),
        ],
        compiler_params=pltpu.CompilerParams(
            collective_id=0, has_side_effects=True, vmem_limit_bytes=24 * MIB
        ),
    )(blocks, vis_count, key_states, value_state_rows)

    heads_block = q_width // kv_heads
    lanes = heads_block // D * BLOCK
    tile = pl.BlockSpec((BLOCK, heads_block), lambda i, g: (i, g))
    attention, grad_query, part = pl.pallas_call(
        attend_kernel,
        grid=(PER, kv_heads),
        out_shape=(
            jax.ShapeDtypeStruct((tokens, q_width), bf16),
            jax.ShapeDtypeStruct((tokens, q_width), bf16),
            jax.ShapeDtypeStruct((held, BLOCK, 2 * width), bf16),
        ),
        in_specs=[smem, smem, smem, tile, tile, vmem],
        out_specs=(tile, tile, vmem),
        scratch_shapes=[
            pltpu.VMEM((lanes, D), bf16),
            pltpu.VMEM((lanes, D), bf16),
            pltpu.VMEM((VIS, BLOCK, lanes), f32),
            pltpu.VMEM((VIS, BLOCK, lanes), f32),
            pltpu.VMEM((held, BLOCK, 2 * width), f32),
            pltpu.SMEM((PER * VIS,), jnp.int32),
            pltpu.SMEM((CTX,), jnp.int32),
        ],
        compiler_params=pltpu.CompilerParams(vmem_limit_bytes=56 * MIB),
    )(blocks, vis_count, lens, query_states, grad_out, kv_all)

    grad_key, grad_value = pl.pallas_call(
        return_kernel,
        out_shape=(
            jax.ShapeDtypeStruct((tokens, width), bf16),
            jax.ShapeDtypeStruct((tokens, width), bf16),
        ),
        in_specs=[smem, smem, hbm],
        out_specs=(vmem, vmem),
        scratch_shapes=[
            pltpu.VMEM((SIDE, PER, BLOCK, 2 * width), bf16),
            pltpu.VMEM((SIDE, SIDE, CAP, BLOCK, 2 * width), bf16),
            pltpu.VMEM((SIDE, CAP, BLOCK, 2 * width), bf16),
            pltpu.VMEM((SIDE, PER, BLOCK, 2 * width), bf16),
            pltpu.VMEM((SIDE, PER, BLOCK, 2 * width), bf16),
            pltpu.VMEM((SIDE, PER, BLOCK, 2 * width), bf16),
            pltpu.VMEM((PER, BLOCK, 2 * width), f32),
            sems(CTX),
            sems(CTX),
            sems(SIDE),
            sems(SIDE),
            sems(SIDE),
            sems(SIDE),
            sems(SIDE),
            sems(SIDE),
        ],
        compiler_params=pltpu.CompilerParams(
            collective_id=1, has_side_effects=True, vmem_limit_bytes=24 * MIB
        ),
    )(blocks, vis_count, part)
    return attention, grad_query, grad_key, grad_value


def solution(mesh):
    rows = P(("dp", "ctx"), "head")
    return jax.shard_map(
        body,
        mesh=mesh,
        in_specs=(rows, rows, rows, rows, P("dp", None), P("dp"), P("dp", None)),
        out_specs=(rows, rows, rows, rows),
        check_vma=False,
    )
```

```python
import functools
import math

import jax
import jax.numpy as jnp
from jax import lax
from jax.experimental import pallas as pl
from jax.experimental.pallas import tpu as pltpu
from jax.sharding import PartitionSpec as P

D = 128
BLOCK = 128
PER = 4
SIDE = 4
CTX = SIDE * SIDE
VIS = 6
CAP = 2
ROW = SIDE * PER
NEG = -1e30
INV_ROOT = 1.0 / math.sqrt(D)
EXP2_SCALE = INV_ROOT * math.log2(math.e)
MIB = 1 << 20
CHUNK = 1024
MESH = pl.DeviceIdType.MESH


def coords():
    me = lax.axis_index("ctx")
    return me, me // SIDE, lax.rem(me, SIDE)


def at(y, z):
    return {"ctx": lax.rem(y + SIDE, SIDE) * SIDE + z}


def barrier_neighbours(y, z):
    barrier = pltpu.get_barrier_semaphore()

    def greet(where):
        pl.semaphore_signal(barrier, inc=1, device_id=where, device_id_type=MESH)

    greet(at(y + 1, z))
    greet(at(y - 1, z))
    pl.when(z > 0)(lambda: greet(at(y, z - 1)))
    pl.when(z < SIDE - 1)(lambda: greet(at(y, z + 1)))
    pl.semaphore_wait(barrier, 2 + jnp.where(z > 0, 1, 0) + jnp.where(z < SIDE - 1, 1, 0))


def chosen(blocks_ref, count_ref, dst, src):
    low = jnp.int32(PER - 1)
    high = jnp.int32(0)
    for r in range(PER):
        row = dst * PER + r
        count = count_ref[row]
        for s in range(1, VIS):
            t = blocks_ref[row * VIS + s] - src * PER
            hit = (t >= 0) & (t < PER) & (s < count)
            low = jnp.minimum(low, jnp.where(hit, t, PER - 1))
            high = jnp.maximum(high, jnp.where(hit, t, 0))
    return low, high


def far_at(y, z):
    return pl.ds(ROW + (y * SIDE + z) * CAP, CAP)


STEPS = 2 * SIDE - 1


def nth(n, z):
    d = (n + 1) // 2
    return z + jnp.where(lax.rem(n, 2) == 1, -d, d), d


def exchange_kernel(
    blocks_ref, count_ref, k_ref, v_ref, out_ref,
    row, packed, relay,
    z_recv, up_send, down_send, far_recv, y_send, relay_recv, relay_send, keep_sem,
):
    me, y, z = coords()
    width = k_ref.shape[1]
    for t in range(PER):
        rows = pl.ds(t * BLOCK, BLOCK)
        row[z, t, :, :width] = k_ref[rows, :]
        row[z, t, :, width:] = v_ref[rows, :]
    barrier_neighbours(y, z)

    def z_copy(zs, to, sems):
        return pltpu.make_async_remote_copy(
            src_ref=row.at[zs],
            dst_ref=row.at[zs],
            send_sem=sems.at[zs],
            recv_sem=z_recv.at[zs],
            device_id=at(y, to),
            device_id_type=MESH,
        )

    def y_near(yd, zs):
        return pltpu.make_async_remote_copy(
            src_ref=packed.at[yd, zs],
            dst_ref=out_ref.at[far_at(y, zs)],
            send_sem=y_send.at[yd * SIDE + zs],
            recv_sem=far_recv.at[y * SIDE + zs],
            device_id=at(yd, z),
            device_id_type=MESH,
        )

    def y_far(yd, zs):
        return pltpu.make_async_remote_copy(
            src_ref=packed.at[yd, zs],
            dst_ref=relay.at[zs],
            send_sem=y_send.at[yd * SIDE + zs],
            recv_sem=relay_recv.at[zs],
            device_id=at(jnp.where(y == 0, SIDE - 1, 2), z),
            device_id_type=MESH,
        )

    def relay_copy(zs):
        return pltpu.make_async_remote_copy(
            src_ref=relay.at[zs],
            dst_ref=out_ref.at[far_at(3 - y, zs)],
            send_sem=relay_send.at[zs],
            recv_sem=far_recv.at[(3 - y) * SIDE + zs],
            device_id=at(5 - y, z),
            device_id_type=MESH,
        )

    def keep(zs):
        return pltpu.make_async_copy(row.at[zs], out_ref.at[pl.ds(zs * PER, PER)], keep_sem.at[zs])

    def wanted(zs):
        inside = (zs >= 0) & (zs < SIDE)
        return inside, inside & ((zs <= z) | (y < SIDE - 1))

    def pack(yd, zs):
        picks = chosen(blocks_ref, count_ref, yd * SIDE + z, y * SIDE + zs)
        for c in range(CAP):
            block = row[zs, 0]
            for t in range(1, PER):
                block = jnp.where(picks[c] == t, row[zs, t], block)
            packed[yd, zs, c] = block

    def step(n):
        zs, d = nth(n, z)
        inside, mine = wanted(zs)

        @pl.when(mine)
        def _():
            pl.when(d > 0)(lambda: z_copy(zs, z, up_send).wait_recv())
            pl.when((zs <= z) & (z < SIDE - 1))(lambda: z_copy(zs, z + 1, up_send).start())
            pl.when((zs >= z) & (z > 0) & (y < SIDE - 1))(
                lambda: z_copy(zs, z - 1, down_send).start()
            )
            keep(zs).start()

        @pl.when(inside)
        def _():
            @pl.loop(0, SIDE - 1 - y)
            def _(h):
                hop = jnp.where(y == 2, 1, jnp.where(h == 0, 2, jnp.where(h == 1, 1, 3)))
                yd = y + hop
                pack(yd, zs)
                pl.when(hop == 2)(lambda: y_far(yd, zs).start())
                pl.when(hop != 2)(lambda: y_near(yd, zs).start())

    def relay_step(n):
        zs, _ = nth(n, z)

        @pl.when((zs >= 0) & (zs < SIDE) & (y >= 2))
        def _():
            pltpu.make_async_remote_copy(
                src_ref=relay.at[zs],
                dst_ref=relay.at[zs],
                send_sem=relay_send.at[zs],
                recv_sem=relay_recv.at[zs],
                device_id=at(y, z),
                device_id_type=MESH,
            ).wait_recv()
            relay_copy(zs).start()

    @pl.loop(0, STEPS + 1)
    def _(n):
        pl.when(n < STEPS)(lambda: step(n))
        pl.when(n > 0)(lambda: relay_step(n - 1))

    @pl.loop(0, y * SIDE)
    def _(n):
        pltpu.make_async_remote_copy(
            src_ref=packed.at[0, 0],
            dst_ref=out_ref.at[pl.ds(ROW + n * CAP, CAP)],
            send_sem=relay_send.at[0],
            recv_sem=far_recv.at[n],
            device_id=at(y, z),
            device_id_type=MESH,
        ).wait_recv()

    @pl.loop(0, SIDE)
    def _(zs):
        _, mine = wanted(zs)

        @pl.when(mine)
        def _():
            pl.when((zs <= z) & (z < SIDE - 1))(lambda: z_copy(zs, z + 1, up_send).wait_send())
            pl.when((zs >= z) & (z > 0) & (y < SIDE - 1))(
                lambda: z_copy(zs, z - 1, down_send).wait_send()
            )
            keep(zs).wait()

        @pl.loop(y + 1, SIDE)
        def _(yd):
            y_near(yd, zs).wait_send()

        pl.when(y >= 2)(lambda: relay_copy(zs).wait_send())


def attend_kernel(
    blocks_ref, count_ref, len_ref, q_ref, do_ref, kv_ref, attn_ref, dq_ref, part_ref,
    qs, dos, qt, dot, keys, values, scores, attn_t, dq_t, acc, place, seen, low,
):
    i, g = pl.program_id(0), pl.program_id(1)
    me = lax.axis_index("ctx")
    heads = q_ref.shape[1] // D
    lanes = heads * BLOCK
    width = kv_ref.shape[2] // 2
    row = me * PER + i
    pairs = (count_ref[row] + 1) // 2
    f32, bf16 = jnp.float32, jnp.bfloat16

    @pl.when((i == 0) & (g == 0))
    def _():
        acc[...] = jnp.zeros_like(acc)
        for src in range(CTX):
            low[src] = PER
        for r in range(PER):
            for s in range(1, VIS):
                block = blocks_ref[(me * PER + r) * VIS + s]
                src = block // PER
                live = s < count_ref[me * PER + r]
                low[src] = jnp.where(live, jnp.minimum(low[src], block - src * PER), low[src])
        for r in range(PER):
            own = lax.rem(me, SIDE) * PER + r
            place[r * VIS] = own
            seen[r * VIS] = BLOCK
            for s in range(1, VIS):
                block = blocks_ref[(me * PER + r) * VIS + s]
                live = s < count_ref[me * PER + r]
                src = block // PER
                t = block - src * PER
                far = ROW + CAP * src + jnp.where(t == low[src], 0, 1)
                near = lax.rem(src, SIDE) * PER + t
                there = jnp.where(src // SIDE == me // SIDE, near, far)
                place[r * VIS + s] = jnp.where(live, there, own)
                seen[r * VIS + s] = jnp.where(live, len_ref[(me * PER + r) * VIS + s], 0)

    for h in range(heads):
        q = q_ref[:, h * D : (h + 1) * D]
        do = do_ref[:, h * D : (h + 1) * D]
        qs[pl.ds(h * BLOCK, BLOCK), :] = q
        dos[pl.ds(h * BLOCK, BLOCK), :] = do
        qt[:, h * BLOCK : (h + 1) * BLOCK] = q.T
        dot[:, h * BLOCK : (h + 1) * BLOCK] = do.T

    k_at = pl.multiple_of(g * D, D)
    v_at = pl.multiple_of(width + g * D, D)
    for s in range(VIS):
        rows = pl.ds(s * BLOCK, BLOCK)
        keys[rows, :] = kv_ref[place[i * VIS + s], :, pl.ds(k_at, D)]
        values[rows, :] = kv_ref[place[i * VIS + s], :, pl.ds(v_at, D)]

    tn = (((0,), (0,)), ((), ()))
    key_pos = lax.broadcasted_iota(jnp.int32, (BLOCK, CHUNK), 0)
    query_pos = lax.rem(lax.broadcasted_iota(jnp.int32, (BLOCK, CHUNK), 1), BLOCK)

    def pair_rows(p):
        return pl.ds(pl.multiple_of(p * 2 * BLOCK, 2 * BLOCK), 2 * BLOCK)

    def add_to(p, at_lane, product):
        for half in range(2):
            acc[place[i * VIS + 2 * p + half], :, pl.ds(at_lane, D)] += product[
                half * BLOCK : (half + 1) * BLOCK
            ]

    @pl.loop(0, lanes // CHUNK)
    def _(c):
        at_c = pl.ds(pl.multiple_of(c * CHUNK, CHUNK), CHUNK)

        def score(p, top):
            raw = jnp.dot(keys[pair_rows(p), :], qt[:, at_c], preferred_element_type=f32)
            first = key_pos < seen[i * VIS + 2 * p]
            first = first & ((key_pos <= query_pos) | (p > 0))
            second = key_pos < seen[i * VIS + 2 * p + 1]
            raw = jnp.where(jnp.concatenate([first, second], axis=0), raw, NEG)
            scores[pair_rows(p), :] = raw
            return jnp.maximum(top, jnp.max(raw, axis=0, keepdims=True))

        top = lax.fori_loop(0, pairs, score, jnp.full((1, CHUNK), NEG, f32))
        shift = top * EXP2_SCALE

        def weigh(p, total):
            w = jnp.exp2(scores[pair_rows(p), :] * EXP2_SCALE - shift)
            scores[pair_rows(p), :] = w
            return total + jnp.sum(w, axis=0, keepdims=True)

        scale = 1.0 / lax.fori_loop(0, pairs, weigh, jnp.zeros((1, CHUNK), f32))
        attn_t[...] = jnp.zeros_like(attn_t)
        dq_t[...] = jnp.zeros_like(dq_t)

        @pl.loop(0, pairs)
        def _(p):
            probs = scores[pair_rows(p), :] * scale
            scores[pair_rows(p), :] = probs
            probs = probs.astype(bf16)
            add_to(p, v_at, jnp.dot(probs, dos[at_c, :], preferred_element_type=f32))
            attn_t[...] += lax.dot_general(values[pair_rows(p), :], probs, tn, preferred_element_type=f32)

        delta = jnp.sum(attn_t[...] * dot[:, at_c].astype(f32), axis=0, keepdims=True)

        @pl.loop(0, pairs)
        def _(p):
            dprobs = jnp.dot(values[pair_rows(p), :], dot[:, at_c], preferred_element_type=f32)
            ds = (scores[pair_rows(p), :] * (dprobs - delta)).astype(bf16)
            add_to(p, k_at, jnp.dot(ds, qs[at_c, :], preferred_element_type=f32))
            dq_t[...] += lax.dot_general(keys[pair_rows(p), :], ds, tn, preferred_element_type=f32)

        for h in range(CHUNK // BLOCK):
            to = pl.ds(pl.multiple_of((c * (CHUNK // BLOCK) + h) * D, D), D)
            part = slice(h * BLOCK, (h + 1) * BLOCK)
            attn_ref[:, to] = attn_t[:, part].astype(bf16).T
            dq_ref[:, to] = (dq_t[:, part] * INV_ROOT).astype(bf16).T

    @pl.when((i == pl.num_programs(0) - 1) & (g == pl.num_programs(1) - 1))
    def _():
        @pl.loop(0, acc.shape[0])
        def _(at):
            part_ref[at, :, :width] = (acc[at, :, :width] * INV_ROOT).astype(bf16)
            part_ref[at, :, width:] = acc[at, :, width:].astype(bf16)


def return_kernel(
    blocks_ref, count_ref, part_ref, gk_ref, gv_ref,
    own, landed, relay, running, from_left, from_right, total,
    y_send, y_recv, relay_send, relay_recv, z_send, left_recv, right_recv, own_sem,
):
    me, y, z = coords()
    width = gk_ref.shape[1]

    def own_copy(zs):
        return pltpu.make_async_copy(part_ref.at[pl.ds(zs * PER, PER)], own.at[zs], own_sem.at[zs])

    for zs in range(SIDE):
        pl.when(zs <= z)(lambda: own_copy(zs).start())
    barrier_neighbours(y, z)

    def y_near(ys, zs):
        return pltpu.make_async_remote_copy(
            src_ref=part_ref.at[far_at(ys, zs)],
            dst_ref=landed.at[y, zs],
            send_sem=y_send.at[ys * SIDE + zs],
            recv_sem=y_recv.at[y * SIDE + zs],
            device_id=at(ys, z),
            device_id_type=MESH,
        )

    def y_far(ys, zs):
        return pltpu.make_async_remote_copy(
            src_ref=part_ref.at[far_at(ys, zs)],
            dst_ref=relay.at[zs],
            send_sem=y_send.at[ys * SIDE + zs],
            recv_sem=relay_recv.at[zs],
            device_id=at(5 - y, z),
            device_id_type=MESH,
        )

    def relay_copy(zs):
        return pltpu.make_async_remote_copy(
            src_ref=relay.at[zs],
            dst_ref=landed.at[5 - y, zs],
            send_sem=relay_send.at[zs],
            recv_sem=y_recv.at[(5 - y) * SIDE + zs],
            device_id=at(3 - y, z),
            device_id_type=MESH,
        )

    def z_copy(zs, to, landing, sems):
        return pltpu.make_async_remote_copy(
            src_ref=running.at[zs],
            dst_ref=landing.at[zs],
            send_sem=z_send.at[zs],
            recv_sem=sems.at[zs],
            device_id=at(y, to),
            device_id_type=MESH,
        )

    def inside(zs):
        return (zs >= 0) & (zs < SIDE)

    @pl.loop(0, STEPS)
    def _(n):
        zs, _ = nth(STEPS - 1 - n, z)

        @pl.when(inside(zs))
        def _():
            pl.when(y >= 2)(lambda: y_far(y - 2, zs).start())
            pl.when(y >= 1)(lambda: y_near(y - 1, zs).start())
            pl.when(y >= 3)(lambda: y_near(y - 3, zs).start())

    def relay_step(n):
        zs, _ = nth(n, z)

        @pl.when(inside(zs) & (y >= 2))
        def _():
            pltpu.make_async_remote_copy(
                src_ref=relay.at[zs],
                dst_ref=relay.at[zs],
                send_sem=relay_send.at[zs],
                recv_sem=relay_recv.at[zs],
                device_id=at(y, z),
                device_id_type=MESH,
            ).wait_recv()
            relay_copy(zs).start()

    def step(n):
        zs, d = nth(n, z)

        @pl.when(inside(zs) & ((zs <= z) | (y < SIDE - 1)))
        def _():
            @pl.when(zs <= z)
            def _():
                own_copy(zs).wait()
                total[...] = own[zs].astype(jnp.float32)

            @pl.when(zs > z)
            def _():
                total[...] = jnp.zeros_like(total)

            @pl.loop(y + 1, SIDE)
            def _(yd):
                picks = chosen(blocks_ref, count_ref, yd * SIDE + z, y * SIDE + zs)
                pltpu.make_async_remote_copy(
                    src_ref=landed.at[yd, zs],
                    dst_ref=landed.at[yd, zs],
                    send_sem=relay_send.at[0],
                    recv_sem=y_recv.at[yd * SIDE + zs],
                    device_id=at(y, z),
                    device_id_type=MESH,
                ).wait_recv()
                for t in range(PER):
                    got = jnp.where(picks[1] == t, landed[yd, zs, 1], jnp.zeros_like(landed[yd, zs, 1]))
                    got = jnp.where(picks[0] == t, landed[yd, zs, 0], got)
                    total[t] += got.astype(jnp.float32)

            @pl.when((zs <= z) & (z < SIDE - 1))
            def _():
                z_copy(zs, z, from_right, right_recv).wait_recv()
                total[...] += from_right[zs].astype(jnp.float32)

            @pl.when((zs >= z) & (z > 0) & (y < SIDE - 1))
            def _():
                z_copy(zs, z, from_left, left_recv).wait_recv()
                total[...] += from_left[zs].astype(jnp.float32)

            @pl.when(d > 0)
            def _():
                running[zs] = total[...].astype(running.dtype)
                pl.when(zs < z)(lambda: z_copy(zs, z - 1, from_right, right_recv).start())
                pl.when(zs > z)(lambda: z_copy(zs, z + 1, from_left, left_recv).start())

    @pl.loop(0, STEPS)
    def _(n):
        relay_step(STEPS - 1 - n)
        step(STEPS - 1 - n)

    for t in range(PER):
        rows = pl.ds(t * BLOCK, BLOCK)
        gk_ref[rows, :] = total[t, :, :width].astype(gk_ref.dtype)
        gv_ref[rows, :] = total[t, :, width:].astype(gv_ref.dtype)

    @pl.loop(0, SIDE)
    def _(zs):
        pl.when((zs < z) | ((zs > z) & (y < SIDE - 1)))(
            lambda: z_copy(zs, z, from_right, right_recv).wait_send()
        )

        @pl.loop(0, y)
        def _(ys):
            y_near(ys, zs).wait_send()

        pl.when(y >= 2)(lambda: relay_copy(zs).wait_send())


def attend(blocks, counts, lens, query_states, grad_out, kv_all):
    tokens, q_width = query_states.shape
    held, _, width = kv_all.shape
    width //= 2
    kv_heads = width // D
    bf16, f32 = jnp.bfloat16, jnp.float32
    smem = pl.BlockSpec(memory_space=pltpu.SMEM)
    vmem = pl.BlockSpec(memory_space=pltpu.VMEM)
    heads_block = q_width // kv_heads
    lanes = heads_block // D * BLOCK
    tile = pl.BlockSpec((BLOCK, heads_block), lambda i, g: (i, g))
    return pl.pallas_call(
        attend_kernel,
        grid=(PER, kv_heads),
        out_shape=(
            jax.ShapeDtypeStruct((tokens, q_width), bf16),
            jax.ShapeDtypeStruct((tokens, q_width), bf16),
            jax.ShapeDtypeStruct((held, BLOCK, 2 * width), bf16),
        ),
        in_specs=[smem, smem, smem, tile, tile, vmem],
        out_specs=(tile, tile, vmem),
        scratch_shapes=[
            pltpu.VMEM((lanes, D), bf16),
            pltpu.VMEM((lanes, D), bf16),
            pltpu.VMEM((D, lanes), bf16),
            pltpu.VMEM((D, lanes), bf16),
            pltpu.VMEM((VIS * BLOCK, D), bf16),
            pltpu.VMEM((VIS * BLOCK, D), bf16),
            pltpu.VMEM((VIS * BLOCK, CHUNK), f32),
            pltpu.VMEM((D, CHUNK), f32),
            pltpu.VMEM((D, CHUNK), f32),
            pltpu.VMEM((held, BLOCK, 2 * width), f32),
            pltpu.SMEM((PER * VIS,), jnp.int32),
            pltpu.SMEM((PER * VIS,), jnp.int32),
            pltpu.SMEM((CTX,), jnp.int32),
        ],
        compiler_params=pltpu.CompilerParams(vmem_limit_bytes=56 * MIB),
    )(blocks, counts, lens, query_states, grad_out, kv_all)


def body(query_states, key_states, value_state_rows, grad_out, vis_blocks, vis_count, vis_len):
    tokens, q_width = query_states.shape
    width = key_states.shape[1]
    kv_heads = width // D
    bf16, f32 = jnp.bfloat16, jnp.float32
    blocks = vis_blocks.reshape(-1)
    lens = vis_len.reshape(-1)
    held = ROW + CAP * SIDE * (SIDE - 1)
    sems = lambda n: pltpu.SemaphoreType.DMA((n,))
    smem = pl.BlockSpec(memory_space=pltpu.SMEM)
    vmem = pl.BlockSpec(memory_space=pltpu.VMEM)
    hbm = pl.BlockSpec(memory_space=pl.ANY)

    kv_all = pl.pallas_call(
        exchange_kernel,
        out_shape=jax.ShapeDtypeStruct((held, BLOCK, 2 * width), bf16),
        in_specs=[smem, smem, vmem, vmem],
        out_specs=hbm,
        scratch_shapes=[
            pltpu.VMEM((SIDE, PER, BLOCK, 2 * width), bf16),
            pltpu.VMEM((SIDE, SIDE, CAP, BLOCK, 2 * width), bf16),
            pltpu.VMEM((SIDE, CAP, BLOCK, 2 * width), bf16),
            sems(SIDE),
            sems(SIDE),
            sems(SIDE),
            sems(CTX),
            sems(CTX),
            sems(SIDE),
            sems(SIDE),
            sems(SIDE),
        ],
        compiler_params=pltpu.CompilerParams(
            collective_id=0, has_side_effects=True, vmem_limit_bytes=24 * MIB
        ),
    )(blocks, vis_count, key_states, value_state_rows)

    attention, grad_query, part = attend(
        blocks, vis_count, lens, query_states, grad_out, kv_all
    )
    grad_key, grad_value = pl.pallas_call(
        return_kernel,
        out_shape=(
            jax.ShapeDtypeStruct((tokens, width), bf16),
            jax.ShapeDtypeStruct((tokens, width), bf16),
        ),
        in_specs=[smem, smem, hbm],
        out_specs=(vmem, vmem),
        scratch_shapes=[
            pltpu.VMEM((SIDE, PER, BLOCK, 2 * width), bf16),
            pltpu.VMEM((SIDE, SIDE, CAP, BLOCK, 2 * width), bf16),
            pltpu.VMEM((SIDE, CAP, BLOCK, 2 * width), bf16),
            pltpu.VMEM((SIDE, PER, BLOCK, 2 * width), bf16),
            pltpu.VMEM((SIDE, PER, BLOCK, 2 * width), bf16),
            pltpu.VMEM((SIDE, PER, BLOCK, 2 * width), bf16),
            pltpu.VMEM((PER, BLOCK, 2 * width), f32),
            sems(CTX),
            sems(CTX),
            sems(SIDE),
            sems(SIDE),
            sems(SIDE),
            sems(SIDE),
            sems(SIDE),
            sems(SIDE),
        ],
        compiler_params=pltpu.CompilerParams(
            collective_id=1, has_side_effects=True, vmem_limit_bytes=24 * MIB
        ),
    )(blocks, vis_count, part)
    return attention, grad_query, grad_key, grad_value


def solution(mesh):
    rows = P(("dp", "ctx"), "head")
    return jax.shard_map(
        body,
        mesh=mesh,
        in_specs=(rows, rows, rows, rows, P("dp", None), P("dp"), P("dp", None)),
        out_specs=(rows, rows, rows, rows),
        check_vma=False,
    )
```

```python
import functools
import math

import jax
import jax.numpy as jnp
from jax import lax
from jax.experimental import pallas as pl
from jax.experimental.pallas import tpu as pltpu
from jax.sharding import PartitionSpec as P

D = 128
BLOCK = 128
PER = 4
SIDE = 4
CTX = SIDE * SIDE
VIS = 6
CAP = 2
ROW = SIDE * PER
HELD = ROW + CAP * SIDE * (SIDE - 1)
STEPS = 2 * SIDE - 1
NEG = -1e30
INV_ROOT = 1.0 / math.sqrt(D)
EXP2_SCALE = INV_ROOT * math.log2(math.e)
MIB = 1 << 20
MESH = pl.DeviceIdType.MESH


def coords():
    me = lax.axis_index("ctx")
    return me, me // SIDE, lax.rem(me, SIDE)


def at(y, z):
    return {"ctx": lax.rem(y + SIDE, SIDE) * SIDE + z}


def barrier_neighbours(y, z):
    barrier = pltpu.get_barrier_semaphore()

    def greet(where):
        pl.semaphore_signal(barrier, inc=1, device_id=where, device_id_type=MESH)

    greet(at(y + 1, z))
    greet(at(y - 1, z))
    pl.when(z > 0)(lambda: greet(at(y, z - 1)))
    pl.when(z < SIDE - 1)(lambda: greet(at(y, z + 1)))
    pl.semaphore_wait(barrier, 2 + jnp.where(z > 0, 1, 0) + jnp.where(z < SIDE - 1, 1, 0))


def far_at(y, z):
    return pl.ds(ROW + (y * SIDE + z) * CAP, CAP)


def nth(n, z):
    d = (n + 1) // 2
    return z + jnp.where(lax.rem(n, 2) == 1, -d, d), d


def prep_kernel(blocks_ref, count_ref, len_ref, picks, place, seen, slot_of, low):
    me, y, z = coords()

    @pl.loop(0, SIDE * SIDE)
    def _(k):
        dst = (k // SIDE) * SIDE + z
        src = y * SIDE + lax.rem(k, SIDE)
        first, last = jnp.int32(PER - 1), jnp.int32(0)
        for r in range(PER):
            row = dst * PER + r
            count = count_ref[row]
            for s in range(1, VIS):
                t = blocks_ref[row, s] - src * PER
                hit = (t >= 0) & (t < PER) & (s < count)
                first = jnp.minimum(first, jnp.where(hit, t, PER - 1))
                last = jnp.maximum(last, jnp.where(hit, t, 0))
        picks[2 * k] = first
        picks[2 * k + 1] = last

    @pl.loop(0, PER * HELD)
    def _(n):
        slot_of[n] = -1

    for src in range(CTX):
        low[src] = PER
    for r in range(PER):
        for s in range(1, VIS):
            block = blocks_ref[me * PER + r, s]
            src = block // PER
            live = s < count_ref[me * PER + r]
            low[src] = jnp.where(live, jnp.minimum(low[src], block - src * PER), low[src])
    for r in range(PER):
        own = z * PER + r
        place[r * VIS] = own
        seen[r * VIS] = BLOCK
        slot_of[own * PER + r] = r * VIS
        for s in range(1, VIS):
            block = blocks_ref[me * PER + r, s]
            live = s < count_ref[me * PER + r]
            src = block // PER
            t = block - src * PER
            far = ROW + CAP * src + jnp.where(t == low[src], 0, 1)
            near = lax.rem(src, SIDE) * PER + t
            there = jnp.where(src // SIDE == y, near, far)
            place[r * VIS + s] = jnp.where(live, there, own)
            seen[r * VIS + s] = jnp.where(live, len_ref[me * PER + r, s], 0)

            @pl.when(live)
            def _():
                slot_of[there * PER + r] = r * VIS + s


class Attention:
    def __init__(self, head, place, seen, q_ref, do_ref, held_ref, attn_ref, dq_ref, slots_ref, scratch):
        self.place, self.seen = place, seen
        self.attn_ref, self.dq_ref, self.slots_ref = attn_ref, dq_ref, slots_ref
        (self.q, self.do, self.held, self.qs, self.dos, self.qt, self.dot, self.keys, self.values,
         self.scores, sem) = scratch
        lanes = self.q.shape[1]
        columns = pl.ds(head * lanes, lanes)
        self.loads = (
            pltpu.make_async_copy(q_ref.at[:, columns], self.q, sem.at[0]),
            pltpu.make_async_copy(do_ref.at[:, columns], self.do, sem.at[1]),
            pltpu.make_async_copy(held_ref, self.held, sem.at[2]),
        )

    @staticmethod
    def scratch(tokens, lanes):
        f32, bf16 = jnp.float32, jnp.bfloat16
        return [
            pltpu.VMEM((tokens, lanes), bf16),
            pltpu.VMEM((tokens, lanes), bf16),
            pltpu.VMEM((HELD, BLOCK, 2 * D), bf16),
            pltpu.VMEM((lanes, D), bf16),
            pltpu.VMEM((lanes, D), bf16),
            pltpu.VMEM((D, lanes), bf16),
            pltpu.VMEM((D, lanes), bf16),
            pltpu.VMEM((VIS * BLOCK, D), bf16),
            pltpu.VMEM((VIS * BLOCK, D), bf16),
            pltpu.VMEM((VIS * BLOCK, lanes), f32),
            pltpu.SemaphoreType.DMA((3,)),
        ]

    def start(self):
        for load in self.loads:
            load.start()

    def wait(self):
        for load in self.loads:
            load.wait()

    def unit(self, i):
        f32, bf16 = jnp.float32, jnp.bfloat16
        lanes = self.q.shape[1]
        tokens = pl.ds(pl.multiple_of(i * BLOCK, BLOCK), BLOCK)
        for h in range(lanes // D):
            part = slice(h * D, (h + 1) * D)
            q, do = self.q[tokens, part], self.do[tokens, part]
            self.qs[part, :] = q
            self.dos[part, :] = do
            self.qt[:, part] = q.T
            self.dot[:, part] = do.T
        for s in range(VIS):
            block = self.held[self.place[i * VIS + s]]
            rows = slice(s * BLOCK, (s + 1) * BLOCK)
            self.keys[rows, :] = block[:, :D]
            self.values[rows, :] = block[:, D:]

        tn = (((0,), (0,)), ((), ()))
        key_pos = lax.broadcasted_iota(jnp.int32, (BLOCK, lanes), 0)
        query_pos = lax.broadcasted_iota(jnp.int32, (BLOCK, lanes), 1) & (BLOCK - 1)
        pairs = [slice(p * 2 * BLOCK, (p + 1) * 2 * BLOCK) for p in range(VIS // 2)]
        top = jnp.full((1, lanes), NEG, f32)
        for p, rows in enumerate(pairs):
            raw = jnp.dot(self.keys[rows, :], self.qt[...], preferred_element_type=f32)
            first = key_pos <= query_pos if p == 0 else key_pos < self.seen[i * VIS + 2 * p]
            second = key_pos < self.seen[i * VIS + 2 * p + 1]
            raw = jnp.where(jnp.concatenate([first, second], axis=0), raw, NEG)
            self.scores[rows, :] = raw
            top = jnp.maximum(top, jnp.max(raw, axis=0, keepdims=True))
        shift = top * EXP2_SCALE
        total = jnp.zeros((1, lanes), f32)
        for rows in pairs:
            w = jnp.exp2(self.scores[rows, :] * EXP2_SCALE - shift)
            self.scores[rows, :] = w
            total = total + jnp.sum(w, axis=0, keepdims=True)
        scale = 1.0 / total
        attn = jnp.zeros((D, lanes), f32)
        for p, rows in enumerate(pairs):
            probs = self.scores[rows, :] * scale
            self.scores[rows, :] = probs
            probs = probs.astype(bf16)
            product = jnp.dot(probs, self.dos[...], preferred_element_type=f32).astype(bf16)
            self.slots_ref[i * VIS + 2 * p, :, D:] = product[:BLOCK]
            self.slots_ref[i * VIS + 2 * p + 1, :, D:] = product[BLOCK:]
            attn = attn + lax.dot_general(self.values[rows, :], probs, tn, preferred_element_type=f32)
        delta = jnp.sum(attn * self.dot[...].astype(f32), axis=0, keepdims=True)
        dq = jnp.zeros((D, lanes), f32)
        for p, rows in enumerate(pairs):
            dprobs = jnp.dot(self.values[rows, :], self.dot[...], preferred_element_type=f32)
            ds = (self.scores[rows, :] * (dprobs - delta)).astype(bf16)
            product = (jnp.dot(ds, self.qs[...], preferred_element_type=f32) * INV_ROOT).astype(bf16)
            self.slots_ref[i * VIS + 2 * p, :, :D] = product[:BLOCK]
            self.slots_ref[i * VIS + 2 * p + 1, :, :D] = product[BLOCK:]
            dq = dq + lax.dot_general(self.keys[rows, :], ds, tn, preferred_element_type=f32)
        for h in range(lanes // D):
            part = slice(h * D, (h + 1) * D)
            self.attn_ref[tokens, part] = attn[:, part].astype(bf16).T
            self.dq_ref[tokens, part] = (dq[:, part] * INV_ROOT).astype(bf16).T


def exchange_scratch(sems):
    bf16 = jnp.bfloat16
    return [
        pltpu.VMEM((SIDE, PER, BLOCK, 2 * D), bf16),
        pltpu.VMEM((SIDE, SIDE, CAP, BLOCK, 2 * D), bf16),
        pltpu.VMEM((SIDE, CAP, BLOCK, 2 * D), bf16),
        sems(SIDE),
        sems(SIDE),
        sems(SIDE),
        sems(CTX),
        sems(CTX),
        sems(SIDE),
        sems(SIDE),
        sems(SIDE),
        sems(2),
    ]


def exchange(head, picks_ref, k_ref, v_ref, out_ref, scratch, attention):
    row, packed, relay, z_recv, up_send, down_send, far_recv, y_send, relay_recv, relay_send, keep_sem, in_sem = scratch
    me, y, z = coords()
    columns = pl.ds(head * D, D)
    mine_in = (
        pltpu.make_async_copy(k_ref.at[:, :, columns], row.at[z, :, :, pl.ds(0, D)], in_sem.at[0]),
        pltpu.make_async_copy(v_ref.at[:, :, columns], row.at[z, :, :, pl.ds(D, D)], in_sem.at[1]),
    )
    for copy in mine_in:
        copy.start()
    if attention:
        attention.start()
    barrier_neighbours(y, z)
    for copy in mine_in:
        copy.wait()

    def z_copy(zs, to, sems):
        return pltpu.make_async_remote_copy(
            src_ref=row.at[zs],
            dst_ref=row.at[zs],
            send_sem=sems.at[zs],
            recv_sem=z_recv.at[zs],
            device_id=at(y, to),
            device_id_type=MESH,
        )

    def y_near(yd, zs):
        return pltpu.make_async_remote_copy(
            src_ref=packed.at[yd, zs],
            dst_ref=out_ref.at[far_at(y, zs)],
            send_sem=y_send.at[yd * SIDE + zs],
            recv_sem=far_recv.at[y * SIDE + zs],
            device_id=at(yd, z),
            device_id_type=MESH,
        )

    def y_far(yd, zs):
        return pltpu.make_async_remote_copy(
            src_ref=packed.at[yd, zs],
            dst_ref=relay.at[zs],
            send_sem=y_send.at[yd * SIDE + zs],
            recv_sem=relay_recv.at[zs],
            device_id=at(jnp.where(y == 0, SIDE - 1, 2), z),
            device_id_type=MESH,
        )

    def relay_copy(zs):
        return pltpu.make_async_remote_copy(
            src_ref=relay.at[zs],
            dst_ref=out_ref.at[far_at(3 - y, zs)],
            send_sem=relay_send.at[zs],
            recv_sem=far_recv.at[(3 - y) * SIDE + zs],
            device_id=at(5 - y, z),
            device_id_type=MESH,
        )

    def keep(zs):
        return pltpu.make_async_copy(row.at[zs], out_ref.at[pl.ds(zs * PER, PER)], keep_sem.at[zs])

    def wanted(zs):
        inside = (zs >= 0) & (zs < SIDE)
        return inside, inside & ((zs <= z) | (y < SIDE - 1))

    def pack(yd, zs):
        for c in range(CAP):
            pick = picks_ref[(yd * SIDE + zs) * CAP + c]
            block = row[zs, 0]
            for t in range(1, PER):
                block = jnp.where(pick == t, row[zs, t], block)
            packed[yd, zs, c] = block

    def step(n):
        zs, d = nth(n, z)
        inside, mine = wanted(zs)

        @pl.when(mine)
        def _():
            pl.when(d > 0)(lambda: z_copy(zs, z, up_send).wait_recv())
            pl.when((zs <= z) & (z < SIDE - 1))(lambda: z_copy(zs, z + 1, up_send).start())
            pl.when((zs >= z) & (z > 0) & (y < SIDE - 1))(
                lambda: z_copy(zs, z - 1, down_send).start()
            )
            keep(zs).start()

        @pl.when(inside)
        def _():
            @pl.loop(0, SIDE - 1 - y)
            def _(h):
                hop = jnp.where(y == 2, 1, jnp.where(h == 0, 2, jnp.where(h == 1, 1, 3)))
                yd = y + hop
                pack(yd, zs)
                pl.when(hop == 2)(lambda: y_far(yd, zs).start())
                pl.when(hop != 2)(lambda: y_near(yd, zs).start())

    def relay_step(n):
        zs, _ = nth(n, z)

        @pl.when((zs >= 0) & (zs < SIDE) & (y >= 2))
        def _():
            pltpu.make_async_remote_copy(
                src_ref=relay.at[zs],
                dst_ref=relay.at[zs],
                send_sem=relay_send.at[zs],
                recv_sem=relay_recv.at[zs],
                device_id=at(y, z),
                device_id_type=MESH,
            ).wait_recv()
            relay_copy(zs).start()

    def both(n):
        pl.when(n < STEPS)(lambda: step(n))
        pl.when((n > 0) & (n <= STEPS))(lambda: relay_step(n - 1))

    if attention:
        both(jnp.int32(0))
        attention.wait()

        @pl.loop(0, PER)
        def _(u):
            attention.unit(u)

            @pl.loop(2 * u + 1, 2 * u + 3)
            def _(n):
                both(n)
    else:
        pl.loop(0, STEPS + 1)(both)

    @pl.loop(0, y * SIDE)
    def _(n):
        pltpu.make_async_remote_copy(
            src_ref=packed.at[0, 0],
            dst_ref=out_ref.at[pl.ds(ROW + n * CAP, CAP)],
            send_sem=relay_send.at[0],
            recv_sem=far_recv.at[n],
            device_id=at(y, z),
            device_id_type=MESH,
        ).wait_recv()

    @pl.loop(0, SIDE)
    def _(zs):
        _, mine = wanted(zs)

        @pl.when(mine)
        def _():
            pl.when((zs <= z) & (z < SIDE - 1))(lambda: z_copy(zs, z + 1, up_send).wait_send())
            pl.when((zs >= z) & (z > 0) & (y < SIDE - 1))(
                lambda: z_copy(zs, z - 1, down_send).wait_send()
            )
            keep(zs).wait()

        @pl.loop(y + 1, SIDE)
        def _(yd):
            y_near(yd, zs).wait_send()

        pl.when(y >= 2)(lambda: relay_copy(zs).wait_send())


def return_scratch(sems):
    bf16 = jnp.bfloat16
    return [
        pltpu.VMEM((SIDE * (SIDE - 1), CAP, BLOCK, 2 * D), bf16),
        pltpu.VMEM((SIDE, SIDE, CAP, BLOCK, 2 * D), bf16),
        pltpu.VMEM((SIDE, CAP, BLOCK, 2 * D), bf16),
        pltpu.VMEM((SIDE, PER, BLOCK, 2 * D), bf16),
        pltpu.VMEM((SIDE, PER, BLOCK, 2 * D), bf16),
        pltpu.VMEM((SIDE, PER, BLOCK, 2 * D), bf16),
        pltpu.VMEM((PER, BLOCK, 2 * D), jnp.float32),
        sems(CTX),
        sems(CTX),
        sems(SIDE),
        sems(SIDE),
        sems(SIDE),
        sems(SIDE),
        sems(SIDE),
    ]


def give_back(picks_ref, slot_of, slots_ref, write, scratch, attention):
    (far, landed, relay, running, from_left, from_right, total,
     y_send, y_recv, relay_send, relay_recv, z_send, left_recv, right_recv) = scratch
    me, y, z = coords()
    if attention:
        attention.start()
    barrier_neighbours(y, z)

    def gathered(e):
        out = jnp.zeros((BLOCK, 2 * D), jnp.float32)
        for r in range(PER):
            slot = slot_of[e * PER + r]
            got = slots_ref[jnp.maximum(slot, 0)]
            out = out + jnp.where(slot >= 0, got, jnp.zeros_like(got)).astype(jnp.float32)
        return out

    def y_near(ys, zs):
        return pltpu.make_async_remote_copy(
            src_ref=far.at[ys * SIDE + zs],
            dst_ref=landed.at[y, zs],
            send_sem=y_send.at[ys * SIDE + zs],
            recv_sem=y_recv.at[y * SIDE + zs],
            device_id=at(ys, z),
            device_id_type=MESH,
        )

    def y_far(ys, zs):
        return pltpu.make_async_remote_copy(
            src_ref=far.at[ys * SIDE + zs],
            dst_ref=relay.at[zs],
            send_sem=y_send.at[ys * SIDE + zs],
            recv_sem=relay_recv.at[zs],
            device_id=at(5 - y, z),
            device_id_type=MESH,
        )

    def relay_copy(zs):
        return pltpu.make_async_remote_copy(
            src_ref=relay.at[zs],
            dst_ref=landed.at[5 - y, zs],
            send_sem=relay_send.at[zs],
            recv_sem=y_recv.at[(5 - y) * SIDE + zs],
            device_id=at(3 - y, z),
            device_id_type=MESH,
        )

    def z_copy(zs, to, landing, sems):
        return pltpu.make_async_remote_copy(
            src_ref=running.at[zs],
            dst_ref=landing.at[zs],
            send_sem=z_send.at[zs],
            recv_sem=sems.at[zs],
            device_id=at(y, to),
            device_id_type=MESH,
        )

    def inside(zs):
        return (zs >= 0) & (zs < SIDE)

    @pl.loop(0, STEPS)
    def _(n):
        zs, _ = nth(STEPS - 1 - n, z)

        @pl.when(inside(zs))
        def _():
            @pl.loop(0, y)
            def _(h):
                hop = jnp.where(y == 1, 1, jnp.where(h == 0, 2, jnp.where(h == 1, 1, 3)))
                ys = y - hop
                for c in range(CAP):
                    far[ys * SIDE + zs, c] = gathered(ROW + (ys * SIDE + zs) * CAP + c).astype(far.dtype)
                pl.when(hop == 2)(lambda: y_far(ys, zs).start())
                pl.when(hop != 2)(lambda: y_near(ys, zs).start())

    def relay_step(n):
        zs, _ = nth(n, z)

        @pl.when(inside(zs) & (y >= 2))
        def _():
            pltpu.make_async_remote_copy(
                src_ref=relay.at[zs],
                dst_ref=relay.at[zs],
                send_sem=relay_send.at[zs],
                recv_sem=relay_recv.at[zs],
                device_id=at(y, z),
                device_id_type=MESH,
            ).wait_recv()
            relay_copy(zs).start()

    def step(n):
        zs, d = nth(n, z)

        @pl.when(inside(zs) & ((zs <= z) | (y < SIDE - 1)))
        def _():
            for t in range(PER):
                total[t] = gathered(zs * PER + t)

            @pl.loop(y + 1, SIDE)
            def _(yd):
                pltpu.make_async_remote_copy(
                    src_ref=landed.at[yd, zs],
                    dst_ref=landed.at[yd, zs],
                    send_sem=relay_send.at[0],
                    recv_sem=y_recv.at[yd * SIDE + zs],
                    device_id=at(y, z),
                    device_id_type=MESH,
                ).wait_recv()
                for t in range(PER):
                    low, high = landed[yd, zs, 0], landed[yd, zs, 1]
                    got = jnp.where(picks_ref[(yd * SIDE + zs) * CAP + 1] == t, high, jnp.zeros_like(high))
                    got = jnp.where(picks_ref[(yd * SIDE + zs) * CAP] == t, low, got)
                    total[t] += got.astype(jnp.float32)

            @pl.when((zs <= z) & (z < SIDE - 1))
            def _():
                z_copy(zs, z, from_right, right_recv).wait_recv()
                total[...] += from_right[zs].astype(jnp.float32)

            @pl.when((zs >= z) & (z > 0) & (y < SIDE - 1))
            def _():
                z_copy(zs, z, from_left, left_recv).wait_recv()
                total[...] += from_left[zs].astype(jnp.float32)

            @pl.when(d > 0)
            def _():
                running[zs] = total[...].astype(running.dtype)
                pl.when(zs < z)(lambda: z_copy(zs, z - 1, from_right, right_recv).start())
                pl.when(zs > z)(lambda: z_copy(zs, z + 1, from_left, left_recv).start())

    def relay_nth(n):
        pl.when((n >= 0) & (n < STEPS))(lambda: relay_step(STEPS - 1 - n))

    def step_nth(n):
        pl.when((n >= 0) & (n < STEPS))(lambda: step(STEPS - 1 - n))

    if attention:
        attention.wait()

        @pl.loop(0, PER)
        def _(u):
            attention.unit(u)

            @pl.loop(2 * u, 2 * u + 2)
            def _(n):
                step_nth(n - 2)
                relay_nth(n)

        step_nth(jnp.int32(STEPS - 1))
    else:

        @pl.loop(0, STEPS)
        def _(n):
            relay_nth(n)
            step_nth(n)

    write(total)

    @pl.loop(0, SIDE)
    def _(zs):
        pl.when((zs < z) | ((zs > z) & (y < SIDE - 1)))(
            lambda: z_copy(zs, z, from_right, right_recv).wait_send()
        )

        @pl.loop(0, y)
        def _(ys):
            y_near(ys, zs).wait_send()

        pl.when(y >= 2)(lambda: relay_copy(zs).wait_send())


def first_exchange(picks, k_ref, v_ref, held_ref, *scratch):
    exchange(0, picks, k_ref, v_ref, held_ref, scratch, None)


def exchange_and_attend(
    picks, place, seen, k_ref, v_ref, q_ref, do_ref, held_ref, next_ref, attn_ref, dq_ref, slots_ref, *scratch
):
    attention = Attention(0, place, seen, q_ref, do_ref, held_ref, attn_ref, dq_ref, slots_ref, scratch[:11])
    exchange(1, picks, k_ref, v_ref, next_ref, scratch[11:], attention)


def return_and_attend(
    picks, slot_of, place, seen, q_ref, do_ref, held_ref, done_ref, grads_ref, attn_ref, dq_ref, slots_ref, *scratch
):
    attention = Attention(1, place, seen, q_ref, do_ref, held_ref, attn_ref, dq_ref, slots_ref, scratch[:11])

    def write(total):
        for t in range(PER):
            grads_ref[pl.ds(t * BLOCK, BLOCK), :] = total[t].astype(grads_ref.dtype)

    give_back(picks, slot_of, done_ref, write, scratch[11:], attention)


def last_return(picks, slot_of, done_ref, grads_ref, gk_ref, gv_ref, *scratch):
    def write(total):
        gk_ref[:, :D] = grads_ref[:, :D]
        gv_ref[:, :D] = grads_ref[:, D:]
        for t in range(PER):
            rows = pl.ds(t * BLOCK, BLOCK)
            gk_ref[rows, D:] = total[t, :, :D].astype(gk_ref.dtype)
            gv_ref[rows, D:] = total[t, :, D:].astype(gv_ref.dtype)

    give_back(picks, slot_of, done_ref, write, scratch, None)


def body(query_states, key_states, value_state_rows, grad_out, vis_blocks, vis_count, vis_len):
    tokens, q_width = query_states.shape
    width = key_states.shape[1]
    lanes = q_width * D // width
    bf16, i32 = jnp.bfloat16, jnp.int32
    sems = lambda n: pltpu.SemaphoreType.DMA((n,))
    smem = pl.BlockSpec(memory_space=pltpu.SMEM)
    vmem = pl.BlockSpec(memory_space=pltpu.VMEM)
    hbm = pl.BlockSpec(memory_space=pl.ANY)
    shape = jax.ShapeDtypeStruct
    held = shape((HELD, BLOCK, 2 * D), bf16)
    half = shape((tokens, lanes), bf16)
    slots = shape((PER * VIS, BLOCK, 2 * D), bf16)
    grads = shape((tokens, 2 * D), bf16)
    whole = shape((tokens, width), bf16)

    def remote(n):
        return pltpu.CompilerParams(collective_id=n, has_side_effects=True, vmem_limit_bytes=48 * MIB)

    picks, place, seen, slot_of = pl.pallas_call(
        prep_kernel,
        out_shape=tuple(shape((n,), i32) for n in (CTX * CAP, PER * VIS, PER * VIS, PER * HELD)),
        in_specs=[smem] * 3,
        out_specs=(smem,) * 4,
        scratch_shapes=[pltpu.SMEM((CTX,), i32)],
    )(vis_blocks, vis_count, vis_len)
    keys = key_states.reshape(PER, BLOCK, width)
    values = value_state_rows.reshape(PER, BLOCK, width)

    held_0 = pl.pallas_call(
        first_exchange,
        out_shape=held,
        in_specs=[smem, hbm, hbm],
        out_specs=hbm,
        scratch_shapes=exchange_scratch(sems),
        compiler_params=remote(0),
    )(picks, keys, values)
    held_1, attn_0, dq_0, slots_0 = pl.pallas_call(
        exchange_and_attend,
        out_shape=(held, half, half, slots),
        in_specs=[smem] * 3 + [hbm] * 5,
        out_specs=(hbm, vmem, vmem, vmem),
        scratch_shapes=Attention.scratch(tokens, lanes) + exchange_scratch(sems),
        compiler_params=remote(1),
    )(picks, place, seen, keys, values, query_states, grad_out, held_0)
    grads_0, attn_1, dq_1, slots_1 = pl.pallas_call(
        return_and_attend,
        out_shape=(grads, half, half, slots),
        in_specs=[smem] * 4 + [hbm] * 3 + [vmem],
        out_specs=(vmem, vmem, vmem, vmem),
        scratch_shapes=Attention.scratch(tokens, lanes) + return_scratch(sems),
        compiler_params=remote(2),
    )(picks, slot_of, place, seen, query_states, grad_out, held_1, slots_0)
    grad_key, grad_value = pl.pallas_call(
        last_return,
        out_shape=(whole, whole),
        in_specs=[smem] * 2 + [vmem] * 2,
        out_specs=(vmem, vmem),
        scratch_shapes=return_scratch(sems),
        compiler_params=remote(3),
    )(picks, slot_of, slots_1, grads_0)
    attention = jnp.concatenate([attn_0, attn_1], axis=1)
    grad_query = jnp.concatenate([dq_0, dq_1], axis=1)
    return attention, grad_query, grad_key, grad_value


def solution(mesh):
    rows = P(("dp", "ctx"), "head")
    return jax.shard_map(
        body,
        mesh=mesh,
        in_specs=(rows, rows, rows, rows, P("dp", None), P("dp"), P("dp", None)),
        out_specs=(rows, rows, rows, rows),
        check_vma=False,
    )
```

```python
import functools
import math

import jax
import jax.numpy as jnp
from jax import lax
from jax.experimental import pallas as pl
from jax.experimental.pallas import tpu as pltpu
from jax.sharding import PartitionSpec as P

D = 128
BLOCK = 128
PER = 4
SIDE = 4
CTX = SIDE * SIDE
VIS = 6
CAP = 2
ROW = SIDE * PER
HELD = ROW + CAP * SIDE * (SIDE - 1)
STEPS = 2 * SIDE - 1
PAIRS = [slice(p * 2 * BLOCK, (p + 1) * 2 * BLOCK) for p in range(VIS // 2)]
TN = (((0,), (0,)), ((), ()))
NEG = -1e30
INV_ROOT = 1.0 / math.sqrt(D)
EXP2_SCALE = INV_ROOT * math.log2(math.e)
MIB = 1 << 20
MESH = pl.DeviceIdType.MESH


def coords():
    me = lax.axis_index("ctx")
    return me, me // SIDE, lax.rem(me, SIDE)


def at(y, z):
    return {"ctx": lax.rem(y + SIDE, SIDE) * SIDE + z}


def barrier_neighbours(y, z):
    barrier = pltpu.get_barrier_semaphore()

    def greet(where):
        pl.semaphore_signal(barrier, inc=1, device_id=where, device_id_type=MESH)

    greet(at(y + 1, z))
    greet(at(y - 1, z))
    pl.when(z > 0)(lambda: greet(at(y, z - 1)))
    pl.when(z < SIDE - 1)(lambda: greet(at(y, z + 1)))
    pl.semaphore_wait(barrier, 2 + jnp.where(z > 0, 1, 0) + jnp.where(z < SIDE - 1, 1, 0))


def far_at(y, z):
    return pl.ds(ROW + (y * SIDE + z) * CAP, CAP)


def nth(n, z):
    d = (n + 1) // 2
    return z + jnp.where(lax.rem(n, 2) == 1, -d, d), d


def chosen(blocks_ref, count_ref, dst, src):
    low, high = jnp.int32(PER - 1), jnp.int32(0)
    for r in range(PER):
        row = dst * PER + r
        count = count_ref[row]
        for s in range(1, VIS):
            t = blocks_ref[s, row] - src * PER
            hit = (t >= 0) & (t < PER) & (s < count)
            low = jnp.minimum(low, jnp.where(hit, t, PER - 1))
            high = jnp.maximum(high, jnp.where(hit, t, 0))
    return low, high


def tables(blocks_ref, count_ref, len_ref, place, seen, slot_of):
    me, y, z = coords()

    @pl.loop(0, PER)
    def _(r):
        row = me * PER + r
        own = z * PER + r
        place[r * VIS] = own
        seen[r * VIS] = BLOCK

        @pl.loop(1, VIS)
        def _(s):
            block = blocks_ref[s, row]
            live = s < count_ref[row]
            src = block // PER
            t = block - src * PER
            low, _ = chosen(blocks_ref, count_ref, me, src)
            far = ROW + CAP * src + jnp.where(t == low, 0, 1)
            near = lax.rem(src, SIDE) * PER + t
            there = jnp.where(src // SIDE == y, near, far)
            place[r * VIS + s] = jnp.where(live, there, own)
            seen[r * VIS + s] = jnp.where(live, len_ref[s, row], 0)

    @pl.loop(0, HELD)
    def _(e):
        for r in range(PER):
            slot = jnp.int32(-1)
            for s in range(VIS):
                hit = (place[r * VIS + s] == e) & (seen[r * VIS + s] > 0)
                slot = jnp.where(hit, r * VIS + s, slot)
            slot_of[e * PER + r] = slot


class Attention:
    def __init__(self, head, place, seen, q_ref, do_ref, held_ref, attn_ref, dq_ref, slots_ref, scratch):
        self.place, self.seen = place, seen
        self.attn_ref, self.dq_ref, self.slots_ref = attn_ref, dq_ref, slots_ref
        (self.q, self.do, self.held, self.qs, self.dos, self.qt, self.dot, self.keys, self.values,
         self.scores, self.scale, self.delta, sem) = scratch
        lanes = self.q.shape[1]
        columns = pl.ds(head * lanes, lanes)
        self.loads = (
            pltpu.make_async_copy(q_ref.at[:, columns], self.q, sem.at[0]),
            pltpu.make_async_copy(do_ref.at[:, columns], self.do, sem.at[1]),
            pltpu.make_async_copy(held_ref, self.held, sem.at[2]),
        )

    @staticmethod
    def scratch(tokens, lanes):
        f32, bf16 = jnp.float32, jnp.bfloat16
        return [
            pltpu.VMEM((tokens, lanes), bf16),
            pltpu.VMEM((tokens, lanes), bf16),
            pltpu.VMEM((HELD, BLOCK, 2 * D), bf16),
            pltpu.VMEM((lanes, D), bf16),
            pltpu.VMEM((lanes, D), bf16),
            pltpu.VMEM((D, lanes), bf16),
            pltpu.VMEM((D, lanes), bf16),
            pltpu.VMEM((VIS * BLOCK, D), bf16),
            pltpu.VMEM((VIS * BLOCK, D), bf16),
            pltpu.VMEM((VIS * BLOCK, lanes), f32),
            pltpu.VMEM((1, lanes), f32),
            pltpu.VMEM((1, lanes), f32),
            pltpu.SemaphoreType.DMA((3,)),
        ]

    def start(self):
        for load in self.loads:
            load.start()

    def wait(self):
        for load in self.loads:
            load.wait()

    def weigh(self, i):
        f32, bf16 = jnp.float32, jnp.bfloat16
        lanes = self.q.shape[1]
        tokens = pl.ds(pl.multiple_of(i * BLOCK, BLOCK), BLOCK)
        for h in range(lanes // D):
            part = slice(h * D, (h + 1) * D)
            q, do = self.q[tokens, part], self.do[tokens, part]
            self.qs[part, :] = q
            self.dos[part, :] = do
            self.qt[:, part] = q.T
            self.dot[:, part] = do.T
        for s in range(VIS):
            block = self.held[self.place[i * VIS + s]]
            rows = slice(s * BLOCK, (s + 1) * BLOCK)
            self.keys[rows, :] = block[:, :D]
            self.values[rows, :] = block[:, D:]

        key_pos = lax.broadcasted_iota(jnp.int32, (BLOCK, lanes), 0)
        query_pos = lax.broadcasted_iota(jnp.int32, (BLOCK, lanes), 1) & (BLOCK - 1)
        top = jnp.full((1, lanes), NEG, f32)
        for p, rows in enumerate(PAIRS):
            raw = jnp.dot(self.keys[rows, :], self.qt[...], preferred_element_type=f32)
            first = key_pos <= query_pos if p == 0 else key_pos < self.seen[i * VIS + 2 * p]
            second = key_pos < self.seen[i * VIS + 2 * p + 1]
            raw = jnp.where(jnp.concatenate([first, second], axis=0), raw, NEG)
            self.scores[rows, :] = raw
            top = jnp.maximum(top, jnp.max(raw, axis=0, keepdims=True))
        shift = top * EXP2_SCALE
        total = jnp.zeros((1, lanes), f32)
        for rows in PAIRS:
            w = jnp.exp2(self.scores[rows, :] * EXP2_SCALE - shift)
            self.scores[rows, :] = w
            total = total + jnp.sum(w, axis=0, keepdims=True)
        self.scale[...] = 1.0 / total

    def mix(self, i):
        f32, bf16 = jnp.float32, jnp.bfloat16
        lanes = self.q.shape[1]
        scale = self.scale[...]
        attn = jnp.zeros((D, lanes), f32)
        for p, rows in enumerate(PAIRS):
            probs = self.scores[rows, :] * scale
            self.scores[rows, :] = probs
            probs = probs.astype(bf16)
            product = jnp.dot(probs, self.dos[...], preferred_element_type=f32).astype(bf16)
            self.slots_ref[i * VIS + 2 * p, :, D:] = product[:BLOCK]
            self.slots_ref[i * VIS + 2 * p + 1, :, D:] = product[BLOCK:]
            attn = attn + lax.dot_general(self.values[rows, :], probs, TN, preferred_element_type=f32)
        self.delta[...] = jnp.sum(attn * self.dot[...].astype(f32), axis=0, keepdims=True)
        self.put(self.attn_ref, i, attn)

    def back(self, i):
        f32, bf16 = jnp.float32, jnp.bfloat16
        lanes = self.q.shape[1]
        delta = self.delta[...]
        dq = jnp.zeros((D, lanes), f32)
        for p, rows in enumerate(PAIRS):
            dprobs = jnp.dot(self.values[rows, :], self.dot[...], preferred_element_type=f32)
            ds = (self.scores[rows, :] * (dprobs - delta)).astype(bf16)
            product = (jnp.dot(ds, self.qs[...], preferred_element_type=f32) * INV_ROOT).astype(bf16)
            self.slots_ref[i * VIS + 2 * p, :, :D] = product[:BLOCK]
            self.slots_ref[i * VIS + 2 * p + 1, :, :D] = product[BLOCK:]
            dq = dq + lax.dot_general(self.keys[rows, :], ds, TN, preferred_element_type=f32)
        self.put(self.dq_ref, i, dq * INV_ROOT)

    def put(self, ref, i, transposed):
        tokens = pl.ds(pl.multiple_of(i * BLOCK, BLOCK), BLOCK)
        for h in range(transposed.shape[1] // D):
            part = slice(h * D, (h + 1) * D)
            ref[tokens, part] = transposed[:, part].astype(ref.dtype).T

    def run(self, between):
        @pl.loop(0, 3 * PER)
        def _(k):
            i = k // 3
            phase = k - 3 * i
            pl.when(phase == 0)(lambda: self.weigh(i))
            pl.when(phase == 1)(lambda: self.mix(i))
            pl.when(phase == 2)(lambda: self.back(i))
            between(k)


def listed(k, table):
    low = high = jnp.int32(0)
    for key, (first, last) in table.items():
        low, high = jnp.where(k == key, first, low), jnp.where(k == key, last, high)
    return low, high


def exchange_scratch(sems):
    bf16 = jnp.bfloat16
    return [
        pltpu.VMEM((SIDE, PER, BLOCK, 2 * D), bf16),
        pltpu.VMEM((SIDE, SIDE, CAP, BLOCK, 2 * D), bf16),
        pltpu.VMEM((SIDE, CAP, BLOCK, 2 * D), bf16),
        sems(SIDE),
        sems(SIDE),
        sems(SIDE),
        sems(CTX),
        sems(CTX),
        sems(SIDE),
        sems(SIDE),
        sems(SIDE),
        sems(2),
    ]


def exchange(head, picks_ref, k_ref, v_ref, out_ref, scratch, attention, lists=None):
    row, packed, relay, z_recv, up_send, down_send, far_recv, y_send, relay_recv, relay_send, keep_sem, in_sem = scratch
    me, y, z = coords()
    columns = pl.ds(head * D, D)
    mine_in = (
        pltpu.make_async_copy(k_ref.at[:, :, columns], row.at[z, :, :, pl.ds(0, D)], in_sem.at[0]),
        pltpu.make_async_copy(v_ref.at[:, :, columns], row.at[z, :, :, pl.ds(D, D)], in_sem.at[1]),
    )
    for copy in mine_in:
        copy.start()
    if attention:
        attention.start()
    barrier_neighbours(y, z)
    for copy in mine_in:
        copy.wait()

    def z_copy(zs, to, sems):
        return pltpu.make_async_remote_copy(
            src_ref=row.at[zs],
            dst_ref=row.at[zs],
            send_sem=sems.at[zs],
            recv_sem=z_recv.at[zs],
            device_id=at(y, to),
            device_id_type=MESH,
        )

    def y_near(yd, zs):
        return pltpu.make_async_remote_copy(
            src_ref=packed.at[yd, zs],
            dst_ref=out_ref.at[far_at(y, zs)],
            send_sem=y_send.at[yd * SIDE + zs],
            recv_sem=far_recv.at[y * SIDE + zs],
            device_id=at(yd, z),
            device_id_type=MESH,
        )

    def y_far(yd, zs):
        return pltpu.make_async_remote_copy(
            src_ref=packed.at[yd, zs],
            dst_ref=relay.at[zs],
            send_sem=y_send.at[yd * SIDE + zs],
            recv_sem=relay_recv.at[zs],
            device_id=at(jnp.where(y == 0, SIDE - 1, 2), z),
            device_id_type=MESH,
        )

    def relay_copy(zs):
        return pltpu.make_async_remote_copy(
            src_ref=relay.at[zs],
            dst_ref=out_ref.at[far_at(3 - y, zs)],
            send_sem=relay_send.at[zs],
            recv_sem=far_recv.at[(3 - y) * SIDE + zs],
            device_id=at(5 - y, z),
            device_id_type=MESH,
        )

    def keep(zs):
        return pltpu.make_async_copy(row.at[zs], out_ref.at[pl.ds(zs * PER, PER)], keep_sem.at[zs])

    def wanted(zs):
        inside = (zs >= 0) & (zs < SIDE)
        return inside, inside & ((zs <= z) | (y < SIDE - 1))

    def pack(yd, zs):
        first = (yd * SIDE + zs) * CAP
        if lists:
            blocks_ref, count_ref = lists[:2]
            picks_ref[first], picks_ref[first + 1] = chosen(
                blocks_ref, count_ref, yd * SIDE + z, y * SIDE + zs
            )
        for c in range(CAP):
            pick = picks_ref[first + c]
            block = row[zs, 0]
            for t in range(1, PER):
                block = jnp.where(pick == t, row[zs, t], block)
            packed[yd, zs, c] = block

    def step(n):
        zs, d = nth(n, z)
        inside, mine = wanted(zs)

        @pl.when(mine)
        def _():
            pl.when(d > 0)(lambda: z_copy(zs, z, up_send).wait_recv())
            pl.when((zs <= z) & (z < SIDE - 1))(lambda: z_copy(zs, z + 1, up_send).start())
            pl.when((zs >= z) & (z > 0) & (y < SIDE - 1))(
                lambda: z_copy(zs, z - 1, down_send).start()
            )
            keep(zs).start()

        @pl.when(inside)
        def _():
            @pl.loop(0, SIDE - 1 - y)
            def _(h):
                hop = jnp.where(y == 2, 1, jnp.where(h == 0, 2, jnp.where(h == 1, 1, 3)))
                yd = y + hop
                pack(yd, zs)
                pl.when(hop == 2)(lambda: y_far(yd, zs).start())
                pl.when(hop != 2)(lambda: y_near(yd, zs).start())

    def relay_step(n):
        zs, _ = nth(n, z)

        @pl.when((zs >= 0) & (zs < SIDE) & (y >= 2))
        def _():
            pltpu.make_async_remote_copy(
                src_ref=relay.at[zs],
                dst_ref=relay.at[zs],
                send_sem=relay_send.at[zs],
                recv_sem=relay_recv.at[zs],
                device_id=at(y, z),
                device_id_type=MESH,
            ).wait_recv()
            relay_copy(zs).start()

    step(jnp.int32(0))
    if attention:
        attention.wait()

        def between(k):
            pl.loop(*listed(k, {1: (1, 3), 4: (3, 5), 7: (5, 7)}))(step)
            pl.loop(*listed(k, {1: (0, 1), 4: (1, 3), 7: (3, 5), 9: (5, 7)}))(relay_step)

        attention.run(between)
    else:
        tables(*lists)

        @pl.loop(1, STEPS + 1)
        def _(n):
            pl.when(n < STEPS)(lambda: step(n))
            relay_step(n - 1)

    @pl.loop(0, y * SIDE)
    def _(n):
        pltpu.make_async_remote_copy(
            src_ref=packed.at[0, 0],
            dst_ref=out_ref.at[pl.ds(ROW + n * CAP, CAP)],
            send_sem=relay_send.at[0],
            recv_sem=far_recv.at[n],
            device_id=at(y, z),
            device_id_type=MESH,
        ).wait_recv()

    @pl.loop(0, SIDE)
    def _(zs):
        _, mine = wanted(zs)

        @pl.when(mine)
        def _():
            pl.when((zs <= z) & (z < SIDE - 1))(lambda: z_copy(zs, z + 1, up_send).wait_send())
            pl.when((zs >= z) & (z > 0) & (y < SIDE - 1))(
                lambda: z_copy(zs, z - 1, down_send).wait_send()
            )
            keep(zs).wait()

        @pl.loop(y + 1, SIDE)
        def _(yd):
            y_near(yd, zs).wait_send()

        pl.when(y >= 2)(lambda: relay_copy(zs).wait_send())


def return_scratch(sems):
    bf16 = jnp.bfloat16
    return [
        pltpu.VMEM((SIDE * (SIDE - 1), CAP, BLOCK, 2 * D), bf16),
        pltpu.VMEM((SIDE, SIDE, CAP, BLOCK, 2 * D), bf16),
        pltpu.VMEM((SIDE, CAP, BLOCK, 2 * D), bf16),
        pltpu.VMEM((SIDE, PER, BLOCK, 2 * D), bf16),
        pltpu.VMEM((SIDE, PER, BLOCK, 2 * D), bf16),
        pltpu.VMEM((SIDE, PER, BLOCK, 2 * D), bf16),
        pltpu.VMEM((PER, BLOCK, 2 * D), jnp.float32),
        sems(CTX),
        sems(CTX),
        sems(SIDE),
        sems(SIDE),
        sems(2 * SIDE),
        sems(2 * SIDE),
        sems(2 * SIDE),
    ]


def give_back(picks_ref, slot_of, slots_ref, write, scratch, attention):
    (far, landed, relay, running, from_left, from_right, total,
     y_send, y_recv, relay_send, relay_recv, z_send, left_recv, right_recv) = scratch
    me, y, z = coords()
    if attention:
        attention.start()
    barrier_neighbours(y, z)

    def gathered(e):
        out = jnp.zeros((BLOCK, 2 * D), jnp.float32)
        for r in range(PER):
            slot = slot_of[e * PER + r]
            got = slots_ref[jnp.maximum(slot, 0)]
            out = out + jnp.where(slot >= 0, got, jnp.zeros_like(got)).astype(jnp.float32)
        return out

    def y_near(ys, zs):
        return pltpu.make_async_remote_copy(
            src_ref=far.at[ys * SIDE + zs],
            dst_ref=landed.at[y, zs],
            send_sem=y_send.at[ys * SIDE + zs],
            recv_sem=y_recv.at[y * SIDE + zs],
            device_id=at(ys, z),
            device_id_type=MESH,
        )

    def y_far(ys, zs):
        return pltpu.make_async_remote_copy(
            src_ref=far.at[ys * SIDE + zs],
            dst_ref=relay.at[zs],
            send_sem=y_send.at[ys * SIDE + zs],
            recv_sem=relay_recv.at[zs],
            device_id=at(5 - y, z),
            device_id_type=MESH,
        )

    def relay_copy(zs):
        return pltpu.make_async_remote_copy(
            src_ref=relay.at[zs],
            dst_ref=landed.at[5 - y, zs],
            send_sem=relay_send.at[zs],
            recv_sem=y_recv.at[(5 - y) * SIDE + zs],
            device_id=at(3 - y, z),
            device_id_type=MESH,
        )

    def z_copy(zs, half, to, landing, sems):
        blocks = pl.ds(2 * half, 2)
        return pltpu.make_async_remote_copy(
            src_ref=running.at[zs, blocks],
            dst_ref=landing.at[zs, blocks],
            send_sem=z_send.at[2 * zs + half],
            recv_sem=sems.at[2 * zs + half],
            device_id=at(y, to),
            device_id_type=MESH,
        )

    def inside(zs):
        return (zs >= 0) & (zs < SIDE)

    @pl.loop(0, STEPS)
    def _(n):
        zs, _ = nth(STEPS - 1 - n, z)

        @pl.when(inside(zs))
        def _():
            @pl.loop(0, y)
            def _(h):
                hop = jnp.where(y == 1, 1, jnp.where(h == 0, 2, jnp.where(h == 1, 1, 3)))
                ys = y - hop
                for c in range(CAP):
                    far[ys * SIDE + zs, c] = gathered(ROW + (ys * SIDE + zs) * CAP + c).astype(far.dtype)
                pl.when(hop == 2)(lambda: y_far(ys, zs).start())
                pl.when(hop != 2)(lambda: y_near(ys, zs).start())

    def relay_step(n):
        zs, _ = nth(n, z)

        @pl.when(inside(zs) & (y >= 2))
        def _():
            pltpu.make_async_remote_copy(
                src_ref=relay.at[zs],
                dst_ref=relay.at[zs],
                send_sem=relay_send.at[zs],
                recv_sem=relay_recv.at[zs],
                device_id=at(y, z),
                device_id_type=MESH,
            ).wait_recv()
            relay_copy(zs).start()

    def step(n):
        zs, d = nth(n, z)

        @pl.when(inside(zs) & ((zs <= z) | (y < SIDE - 1)))
        def _():
            for t in range(PER):
                total[t] = gathered(zs * PER + t)

            @pl.loop(y + 1, SIDE)
            def _(yd):
                pltpu.make_async_remote_copy(
                    src_ref=landed.at[yd, zs],
                    dst_ref=landed.at[yd, zs],
                    send_sem=relay_send.at[0],
                    recv_sem=y_recv.at[yd * SIDE + zs],
                    device_id=at(y, z),
                    device_id_type=MESH,
                ).wait_recv()
                for t in range(PER):
                    low, high = landed[yd, zs, 0], landed[yd, zs, 1]
                    got = jnp.where(picks_ref[(yd * SIDE + zs) * CAP + 1] == t, high, jnp.zeros_like(high))
                    got = jnp.where(picks_ref[(yd * SIDE + zs) * CAP] == t, low, got)
                    total[t] += got.astype(jnp.float32)

            @pl.loop(0, 2)
            def _(half):
                blocks = pl.ds(2 * half, 2)

                @pl.when((zs <= z) & (z < SIDE - 1))
                def _():
                    z_copy(zs, half, z, from_right, right_recv).wait_recv()
                    total[blocks] += from_right[zs, blocks].astype(jnp.float32)

                @pl.when((zs >= z) & (z > 0) & (y < SIDE - 1))
                def _():
                    z_copy(zs, half, z, from_left, left_recv).wait_recv()
                    total[blocks] += from_left[zs, blocks].astype(jnp.float32)

                @pl.when(d > 0)
                def _():
                    running[zs, blocks] = total[blocks].astype(running.dtype)
                    pl.when(zs < z)(lambda: z_copy(zs, half, z - 1, from_right, right_recv).start())
                    pl.when(zs > z)(lambda: z_copy(zs, half, z + 1, from_left, left_recv).start())

    def relay_nth(n):
        relay_step(STEPS - 1 - n)

    def step_nth(n):
        step(STEPS - 1 - n)

    if attention:
        attention.wait()

        def between(k):
            pl.loop(*listed(k, {2: (0, 2), 4: (2, 4), 6: (4, 6), 8: (6, 7)}))(step_nth)
            pl.loop(*listed(k, {1: (0, 2), 2: (2, 4), 4: (4, 6), 6: (6, 7)}))(relay_nth)

        attention.run(between)
    else:

        @pl.loop(0, STEPS)
        def _(n):
            relay_nth(n)
            step_nth(n)

    write(total)

    @pl.loop(0, SIDE)
    def _(zs):
        @pl.when((zs < z) | ((zs > z) & (y < SIDE - 1)))
        def _():
            for half in range(2):
                z_copy(zs, half, z, from_right, right_recv).wait_send()

        @pl.loop(0, y)
        def _(ys):
            y_near(ys, zs).wait_send()

        pl.when(y >= 2)(lambda: relay_copy(zs).wait_send())


def first_exchange(
    blocks_ref, count_ref, len_ref, k_ref, v_ref, held_ref, picks, place, seen, slot_of, *scratch
):
    lists = (blocks_ref, count_ref, len_ref, place, seen, slot_of)
    exchange(0, picks, k_ref, v_ref, held_ref, scratch, None, lists)


def exchange_and_attend(
    picks, place, seen, k_ref, v_ref, q_ref, do_ref, held_ref, next_ref, attn_ref, dq_ref, slots_ref, *scratch
):
    attention = Attention(0, place, seen, q_ref, do_ref, held_ref, attn_ref, dq_ref, slots_ref, scratch[:13])
    exchange(1, picks, k_ref, v_ref, next_ref, scratch[13:], attention)


def return_and_attend(
    picks, slot_of, place, seen, q_ref, do_ref, held_ref, done_ref, grads_ref, attn_ref, dq_ref, slots_ref, *scratch
):
    attention = Attention(1, place, seen, q_ref, do_ref, held_ref, attn_ref, dq_ref, slots_ref, scratch[:13])

    def write(total):
        for t in range(PER):
            grads_ref[pl.ds(t * BLOCK, BLOCK), :] = total[t].astype(grads_ref.dtype)

    give_back(picks, slot_of, done_ref, write, scratch[13:], attention)


def last_return(picks, slot_of, done_ref, grads_ref, gk_ref, gv_ref, *scratch):
    def write(total):
        gk_ref[:, :D] = grads_ref[:, :D]
        gv_ref[:, :D] = grads_ref[:, D:]
        for t in range(PER):
            rows = pl.ds(t * BLOCK, BLOCK)
            gk_ref[rows, D:] = total[t, :, :D].astype(gk_ref.dtype)
            gv_ref[rows, D:] = total[t, :, D:].astype(gv_ref.dtype)

    give_back(picks, slot_of, done_ref, write, scratch, None)


def body(query_states, key_states, value_state_rows, grad_out, vis_blocks, vis_count, vis_len):
    tokens, q_width = query_states.shape
    width = key_states.shape[1]
    lanes = q_width * D // width
    bf16 = jnp.bfloat16
    sems = lambda n: pltpu.SemaphoreType.DMA((n,))
    smem = pl.BlockSpec(memory_space=pltpu.SMEM)
    vmem = pl.BlockSpec(memory_space=pltpu.VMEM)
    hbm = pl.BlockSpec(memory_space=pltpu.HBM)
    shape = jax.ShapeDtypeStruct
    held = shape((HELD, BLOCK, 2 * D), bf16)
    half = shape((tokens, lanes), bf16)
    slots = shape((PER * VIS, BLOCK, 2 * D), bf16)
    grads = shape((tokens, 2 * D), bf16)
    whole = shape((tokens, width), bf16)

    def remote(n):
        return pltpu.CompilerParams(collective_id=n, has_side_effects=True, vmem_limit_bytes=56 * MIB)

    keys = key_states.reshape(PER, BLOCK, width)
    values = value_state_rows.reshape(PER, BLOCK, width)

    sizes = (CTX * CAP, PER * VIS, PER * VIS, PER * HELD)
    held_0, picks, place, seen, slot_of = pl.pallas_call(
        first_exchange,
        out_shape=(held,) + tuple(shape((n,), jnp.int32) for n in sizes),
        in_specs=[smem] * 3 + [hbm] * 2,
        out_specs=(hbm,) + (smem,) * 4,
        scratch_shapes=exchange_scratch(sems),
        compiler_params=remote(0),
    )(vis_blocks.T, vis_count, vis_len.T, keys, values)
    held_1, attn_0, dq_0, slots_0 = pl.pallas_call(
        exchange_and_attend,
        out_shape=(held, half, half, slots),
        in_specs=[smem] * 3 + [hbm] * 5,
        out_specs=(hbm, vmem, vmem, vmem),
        scratch_shapes=Attention.scratch(tokens, lanes) + exchange_scratch(sems),
        compiler_params=remote(1),
    )(picks, place, seen, keys, values, query_states, grad_out, held_0)
    grads_0, attn_1, dq_1, slots_1 = pl.pallas_call(
        return_and_attend,
        out_shape=(grads, half, half, slots),
        in_specs=[smem] * 4 + [hbm] * 3 + [vmem],
        out_specs=(vmem, vmem, vmem, vmem),
        scratch_shapes=Attention.scratch(tokens, lanes) + return_scratch(sems),
        compiler_params=remote(2),
    )(picks, slot_of, place, seen, query_states, grad_out, held_1, slots_0)
    grad_key, grad_value = pl.pallas_call(
        last_return,
        out_shape=(whole, whole),
        in_specs=[smem] * 2 + [vmem] * 2,
        out_specs=(vmem, vmem),
        scratch_shapes=return_scratch(sems),
        compiler_params=remote(3),
    )(picks, slot_of, slots_1, grads_0)
    attention = jnp.concatenate([attn_0, attn_1], axis=1)
    grad_query = jnp.concatenate([dq_0, dq_1], axis=1)
    return attention, grad_query, grad_key, grad_value


def solution(mesh):
    rows = P(("dp", "ctx"), "head")
    return jax.shard_map(
        body,
        mesh=mesh,
        in_specs=(rows, rows, rows, rows, P("dp", None), P("dp"), P("dp", None)),
        out_specs=(rows, rows, rows, rows),
        check_vma=False,
    )
```

```python
import functools
import math

import jax
import jax.numpy as jnp
from jax import lax
from jax.experimental import pallas as pl
from jax.experimental.pallas import tpu as pltpu
from jax.sharding import PartitionSpec as P

D = 128
BLOCK = 128
PER = 4
SIDE = 4
CTX = SIDE * SIDE
VIS = 6
CAP = 2
ROW = SIDE * PER
HELD = ROW + CAP * SIDE * (SIDE - 1)
STEPS = 2 * SIDE - 1
PAIRS = [slice(p * 2 * BLOCK, (p + 1) * 2 * BLOCK) for p in range(VIS // 2)]
TN = (((0,), (0,)), ((), ()))
NEG = -1e30
INV_ROOT = 1.0 / math.sqrt(D)
EXP2_SCALE = INV_ROOT * math.log2(math.e)
MIB = 1 << 20
MESH = pl.DeviceIdType.MESH


def coords():
    me = lax.axis_index("ctx")
    return me, me // SIDE, lax.rem(me, SIDE)


def at(y, z):
    return {"ctx": lax.rem(y + SIDE, SIDE) * SIDE + z}


def barrier_neighbours(y, z):
    barrier = pltpu.get_barrier_semaphore()

    def greet(where):
        pl.semaphore_signal(barrier, inc=1, device_id=where, device_id_type=MESH)

    greet(at(y + 1, z))
    greet(at(y - 1, z))
    pl.when(z > 0)(lambda: greet(at(y, z - 1)))
    pl.when(z < SIDE - 1)(lambda: greet(at(y, z + 1)))
    pl.semaphore_wait(barrier, 2 + jnp.where(z > 0, 1, 0) + jnp.where(z < SIDE - 1, 1, 0))


def far_at(y, z):
    return pl.ds(ROW + (y * SIDE + z) * CAP, CAP)


def nth(n, z):
    d = (n + 1) // 2
    return z + jnp.where(lax.rem(n, 2) == 1, -d, d), d


def target(j, z):
    inner = jnp.where(j == 0, 3, jnp.where(j == 1, 0, jnp.where(j == 2, 2, 1)))
    return jnp.where(z == 0, 3 - j, jnp.where(z == 3, j, jnp.where(z == 1, inner, 3 - inner)))


def chosen(blocks_ref, count_ref, dst, src):
    low, high = jnp.int32(PER - 1), jnp.int32(0)
    for r in range(PER):
        row = dst * PER + r
        count = count_ref[row]
        for s in range(1, VIS):
            t = blocks_ref[s, row] - src * PER
            hit = (t >= 0) & (t < PER) & (s < count)
            low = jnp.minimum(low, jnp.where(hit, t, PER - 1))
            high = jnp.maximum(high, jnp.where(hit, t, 0))
    return low, high


def tables(blocks_ref, count_ref, len_ref, place, seen, slot_of):
    me, y, z = coords()

    @pl.loop(0, PER)
    def _(r):
        row = me * PER + r
        own = z * PER + r
        place[r * VIS] = own
        seen[r * VIS] = BLOCK

        @pl.loop(1, VIS)
        def _(s):
            block = blocks_ref[s, row]
            live = s < count_ref[row]
            src = block // PER
            t = block - src * PER
            low, _ = chosen(blocks_ref, count_ref, me, src)
            far = ROW + CAP * src + jnp.where(t == low, 0, 1)
            near = lax.rem(src, SIDE) * PER + t
            there = jnp.where(src // SIDE == y, near, far)
            place[r * VIS + s] = jnp.where(live, there, own)
            seen[r * VIS + s] = jnp.where(live, len_ref[s, row], 0)

    @pl.loop(0, HELD)
    def _(e):
        for r in range(PER):
            slot = jnp.int32(-1)
            for s in range(VIS):
                hit = (place[r * VIS + s] == e) & (seen[r * VIS + s] > 0)
                slot = jnp.where(hit, r * VIS + s, slot)
            slot_of[e * PER + r] = slot


class Attention:
    def __init__(self, head, place, seen, q_ref, do_ref, held_ref, attn_ref, dq_ref, slots_ref, scratch):
        self.place, self.seen = place, seen
        self.attn_ref, self.dq_ref, self.slots_ref = attn_ref, dq_ref, slots_ref
        (self.q, self.do, self.held, self.qs, self.dos, self.qt, self.dot, self.keys, self.values,
         self.scores, self.scale, self.delta, sem) = scratch
        lanes = self.q.shape[1]
        columns = pl.ds(head * lanes, lanes)
        self.loads = (
            pltpu.make_async_copy(q_ref.at[:, columns], self.q, sem.at[0]),
            pltpu.make_async_copy(do_ref.at[:, columns], self.do, sem.at[1]),
            pltpu.make_async_copy(held_ref, self.held, sem.at[2]),
        )

    @staticmethod
    def scratch(tokens, lanes):
        f32, bf16 = jnp.float32, jnp.bfloat16
        return [
            pltpu.VMEM((tokens, lanes), bf16),
            pltpu.VMEM((tokens, lanes), bf16),
            pltpu.VMEM((HELD, BLOCK, 2 * D), bf16),
            pltpu.VMEM((lanes, D), bf16),
            pltpu.VMEM((lanes, D), bf16),
            pltpu.VMEM((D, lanes), bf16),
            pltpu.VMEM((D, lanes), bf16),
            pltpu.VMEM((VIS * BLOCK, D), bf16),
            pltpu.VMEM((VIS * BLOCK, D), bf16),
            pltpu.VMEM((VIS * BLOCK, lanes), f32),
            pltpu.VMEM((1, lanes), f32),
            pltpu.VMEM((1, lanes), f32),
            pltpu.SemaphoreType.DMA((3,)),
        ]

    def start(self):
        for load in self.loads:
            load.start()

    def wait(self):
        for load in self.loads:
            load.wait()

    def weigh(self, i):
        f32, bf16 = jnp.float32, jnp.bfloat16
        lanes = self.q.shape[1]
        tokens = pl.ds(pl.multiple_of(i * BLOCK, BLOCK), BLOCK)
        for h in range(lanes // D):
            part = slice(h * D, (h + 1) * D)
            q, do = self.q[tokens, part], self.do[tokens, part]
            self.qs[part, :] = q
            self.dos[part, :] = do
            self.qt[:, part] = q.T
            self.dot[:, part] = do.T
        for s in range(VIS):
            block = self.held[self.place[i * VIS + s]]
            rows = slice(s * BLOCK, (s + 1) * BLOCK)
            self.keys[rows, :] = block[:, :D]
            self.values[rows, :] = block[:, D:]

        key_pos = lax.broadcasted_iota(jnp.int32, (BLOCK, lanes), 0)
        query_pos = lax.broadcasted_iota(jnp.int32, (BLOCK, lanes), 1) & (BLOCK - 1)
        top = jnp.full((1, lanes), NEG, f32)
        for p, rows in enumerate(PAIRS):
            raw = jnp.dot(self.keys[rows, :], self.qt[...], preferred_element_type=f32)
            first = key_pos <= query_pos if p == 0 else key_pos < self.seen[i * VIS + 2 * p]
            second = key_pos < self.seen[i * VIS + 2 * p + 1]
            raw = jnp.where(jnp.concatenate([first, second], axis=0), raw, NEG)
            self.scores[rows, :] = raw
            top = jnp.maximum(top, jnp.max(raw, axis=0, keepdims=True))
        shift = top * EXP2_SCALE
        total = jnp.zeros((1, lanes), f32)
        for rows in PAIRS:
            w = jnp.exp2(self.scores[rows, :] * EXP2_SCALE - shift)
            self.scores[rows, :] = w
            total = total + jnp.sum(w, axis=0, keepdims=True)
        self.scale[...] = 1.0 / total

    def mix(self, i):
        f32, bf16 = jnp.float32, jnp.bfloat16
        lanes = self.q.shape[1]
        scale = self.scale[...]
        attn = jnp.zeros((D, lanes), f32)
        for p, rows in enumerate(PAIRS):
            probs = self.scores[rows, :] * scale
            self.scores[rows, :] = probs
            probs = probs.astype(bf16)
            product = jnp.dot(probs, self.dos[...], preferred_element_type=f32).astype(bf16)
            self.slots_ref[i * VIS + 2 * p, :, D:] = product[:BLOCK]
            self.slots_ref[i * VIS + 2 * p + 1, :, D:] = product[BLOCK:]
            attn = attn + lax.dot_general(self.values[rows, :], probs, TN, preferred_element_type=f32)
        self.delta[...] = jnp.sum(attn * self.dot[...].astype(f32), axis=0, keepdims=True)
        self.put(self.attn_ref, i, attn)

    def back(self, i):
        f32, bf16 = jnp.float32, jnp.bfloat16
        lanes = self.q.shape[1]
        delta = self.delta[...]
        dq = jnp.zeros((D, lanes), f32)
        for p, rows in enumerate(PAIRS):
            dprobs = jnp.dot(self.values[rows, :], self.dot[...], preferred_element_type=f32)
            ds = (self.scores[rows, :] * (dprobs - delta)).astype(bf16)
            product = (jnp.dot(ds, self.qs[...], preferred_element_type=f32) * INV_ROOT).astype(bf16)
            self.slots_ref[i * VIS + 2 * p, :, :D] = product[:BLOCK]
            self.slots_ref[i * VIS + 2 * p + 1, :, :D] = product[BLOCK:]
            dq = dq + lax.dot_general(self.keys[rows, :], ds, TN, preferred_element_type=f32)
        self.put(self.dq_ref, i, dq * INV_ROOT)

    def put(self, ref, i, transposed):
        tokens = pl.ds(pl.multiple_of(i * BLOCK, BLOCK), BLOCK)
        for h in range(transposed.shape[1] // D):
            part = slice(h * D, (h + 1) * D)
            ref[tokens, part] = transposed[:, part].astype(ref.dtype).T

    def run(self, between):
        @pl.loop(0, 3 * PER)
        def _(k):
            i = k // 3
            phase = k - 3 * i
            pl.when(phase == 0)(lambda: self.weigh(i))
            pl.when(phase == 1)(lambda: self.mix(i))
            pl.when(phase == 2)(lambda: self.back(i))
            between(k)


def listed(k, table):
    low = high = jnp.int32(0)
    for key, (first, last) in table.items():
        low, high = jnp.where(k == key, first, low), jnp.where(k == key, last, high)
    return low, high


def exchange_scratch(sems):
    bf16 = jnp.bfloat16
    return [
        pltpu.VMEM((SIDE, PER, BLOCK, 2 * D), bf16),
        pltpu.VMEM((SIDE, SIDE, CAP, BLOCK, 2 * D), bf16),
        pltpu.VMEM((SIDE, CAP, BLOCK, 2 * D), bf16),
        sems(SIDE),
        sems(SIDE),
        sems(SIDE),
        sems(CTX),
        sems(CTX),
        sems(SIDE),
        sems(SIDE),
        sems(SIDE),
        sems(2),
    ]


def exchange(head, picks_ref, k_ref, v_ref, out_ref, scratch, attention, lists=None):
    row, packed, relay, z_recv, up_send, down_send, far_recv, y_send, relay_recv, relay_send, keep_sem, in_sem = scratch
    me, y, z = coords()
    columns = pl.ds(head * D, D)
    mine_in = (
        pltpu.make_async_copy(k_ref.at[:, :, columns], row.at[z, :, :, pl.ds(0, D)], in_sem.at[0]),
        pltpu.make_async_copy(v_ref.at[:, :, columns], row.at[z, :, :, pl.ds(D, D)], in_sem.at[1]),
    )
    for copy in mine_in:
        copy.start()
    if attention:
        attention.start()
    barrier_neighbours(y, z)
    for copy in mine_in:
        copy.wait()

    def z_copy(zs, to, sems):
        return pltpu.make_async_remote_copy(
            src_ref=row.at[zs],
            dst_ref=row.at[zs],
            send_sem=sems.at[zs],
            recv_sem=z_recv.at[zs],
            device_id=at(y, to),
            device_id_type=MESH,
        )

    def y_near(yd, zs):
        return pltpu.make_async_remote_copy(
            src_ref=packed.at[yd, zs],
            dst_ref=out_ref.at[far_at(y, zs)],
            send_sem=y_send.at[yd * SIDE + zs],
            recv_sem=far_recv.at[y * SIDE + zs],
            device_id=at(yd, z),
            device_id_type=MESH,
        )

    def y_far(yd, zs):
        return pltpu.make_async_remote_copy(
            src_ref=packed.at[yd, zs],
            dst_ref=relay.at[zs],
            send_sem=y_send.at[yd * SIDE + zs],
            recv_sem=relay_recv.at[zs],
            device_id=at(jnp.where(y == 0, SIDE - 1, 2), z),
            device_id_type=MESH,
        )

    def relay_copy(zs):
        return pltpu.make_async_remote_copy(
            src_ref=relay.at[zs],
            dst_ref=out_ref.at[far_at(3 - y, zs)],
            send_sem=relay_send.at[zs],
            recv_sem=far_recv.at[(3 - y) * SIDE + zs],
            device_id=at(5 - y, z),
            device_id_type=MESH,
        )

    def keep(zs):
        return pltpu.make_async_copy(row.at[zs], out_ref.at[pl.ds(zs * PER, PER)], keep_sem.at[zs])

    def wanted(zs):
        inside = (zs >= 0) & (zs < SIDE)
        return inside, inside & ((zs <= z) | (y < SIDE - 1))

    def pack(yd, zs):
        first = (yd * SIDE + zs) * CAP
        if lists:
            blocks_ref, count_ref = lists[:2]
            picks_ref[first], picks_ref[first + 1] = chosen(
                blocks_ref, count_ref, yd * SIDE + z, y * SIDE + zs
            )
        for c in range(CAP):
            pick = picks_ref[first + c]
            block = row[zs, 0]
            for t in range(1, PER):
                block = jnp.where(pick == t, row[zs, t], block)
            packed[yd, zs, c] = block

    def step(n):
        zs, d = nth(n, z)
        inside, mine = wanted(zs)

        @pl.when(mine)
        def _():
            pl.when(d > 0)(lambda: z_copy(zs, z, up_send).wait_recv())
            pl.when((zs <= z) & (z < SIDE - 1))(lambda: z_copy(zs, z + 1, up_send).start())
            pl.when((zs >= z) & (z > 0) & (y < SIDE - 1))(
                lambda: z_copy(zs, z - 1, down_send).start()
            )
            keep(zs).start()

        @pl.when(inside)
        def _():
            @pl.loop(0, SIDE - 1 - y)
            def _(h):
                hop = jnp.where(y == 2, 1, jnp.where(h == 0, 2, jnp.where(h == 1, 1, 3)))
                yd = y + hop
                pack(yd, zs)
                pl.when(hop == 2)(lambda: y_far(yd, zs).start())
                pl.when(hop != 2)(lambda: y_near(yd, zs).start())

    def relay_step(n):
        zs, _ = nth(n, z)

        @pl.when((zs >= 0) & (zs < SIDE) & (y >= 2))
        def _():
            pltpu.make_async_remote_copy(
                src_ref=relay.at[zs],
                dst_ref=relay.at[zs],
                send_sem=relay_send.at[zs],
                recv_sem=relay_recv.at[zs],
                device_id=at(y, z),
                device_id_type=MESH,
            ).wait_recv()
            relay_copy(zs).start()

    step(jnp.int32(0))
    if attention:
        attention.wait()

        def between(k):
            pl.loop(*listed(k, {1: (1, 3), 4: (3, 5), 7: (5, 7)}))(step)
            pl.loop(*listed(k, {1: (0, 1), 4: (1, 3), 7: (3, 5), 9: (5, 7)}))(relay_step)

        attention.run(between)
    else:
        tables(*lists)

        @pl.loop(1, STEPS + 1)
        def _(n):
            pl.when(n < STEPS)(lambda: step(n))
            relay_step(n - 1)

    @pl.loop(0, y * SIDE)
    def _(n):
        pltpu.make_async_remote_copy(
            src_ref=packed.at[0, 0],
            dst_ref=out_ref.at[pl.ds(ROW + n * CAP, CAP)],
            send_sem=relay_send.at[0],
            recv_sem=far_recv.at[n],
            device_id=at(y, z),
            device_id_type=MESH,
        ).wait_recv()

    @pl.loop(0, SIDE)
    def _(zs):
        _, mine = wanted(zs)

        @pl.when(mine)
        def _():
            pl.when((zs <= z) & (z < SIDE - 1))(lambda: z_copy(zs, z + 1, up_send).wait_send())
            pl.when((zs >= z) & (z > 0) & (y < SIDE - 1))(
                lambda: z_copy(zs, z - 1, down_send).wait_send()
            )
            keep(zs).wait()

        @pl.loop(y + 1, SIDE)
        def _(yd):
            y_near(yd, zs).wait_send()

        pl.when(y >= 2)(lambda: relay_copy(zs).wait_send())


def return_scratch(sems):
    bf16 = jnp.bfloat16
    return [
        pltpu.VMEM((SIDE * (SIDE - 1), CAP, BLOCK, 2 * D), bf16),
        pltpu.VMEM((SIDE, SIDE, CAP, BLOCK, 2 * D), bf16),
        pltpu.VMEM((SIDE, CAP, BLOCK, 2 * D), bf16),
        pltpu.VMEM((SIDE, PER, BLOCK, 2 * D), bf16),
        pltpu.VMEM((SIDE, PER, BLOCK, 2 * D), bf16),
        pltpu.VMEM((SIDE, PER, BLOCK, 2 * D), bf16),
        pltpu.VMEM((PER, BLOCK, 2 * D), jnp.float32),
        sems(CTX),
        sems(CTX),
        sems(SIDE),
        sems(SIDE),
        sems(2 * SIDE),
        sems(2 * SIDE),
        sems(2 * SIDE),
    ]


def give_back(picks_ref, slot_of, slots_ref, write, scratch, attention):
    (far, landed, relay, running, from_left, from_right, total,
     y_send, y_recv, relay_send, relay_recv, z_send, left_recv, right_recv) = scratch
    me, y, z = coords()
    if attention:
        attention.start()
    barrier_neighbours(y, z)

    def gathered(e):
        out = jnp.zeros((BLOCK, 2 * D), jnp.float32)
        for r in range(PER):
            slot = slot_of[e * PER + r]
            got = slots_ref[jnp.maximum(slot, 0)]
            out = out + jnp.where(slot >= 0, got, jnp.zeros_like(got)).astype(jnp.float32)
        return out

    def y_near(ys, zs):
        return pltpu.make_async_remote_copy(
            src_ref=far.at[ys * SIDE + zs],
            dst_ref=landed.at[y, zs],
            send_sem=y_send.at[ys * SIDE + zs],
            recv_sem=y_recv.at[y * SIDE + zs],
            device_id=at(ys, z),
            device_id_type=MESH,
        )

    def y_far(ys, zs):
        return pltpu.make_async_remote_copy(
            src_ref=far.at[ys * SIDE + zs],
            dst_ref=relay.at[zs],
            send_sem=y_send.at[ys * SIDE + zs],
            recv_sem=relay_recv.at[zs],
            device_id=at(5 - y, z),
            device_id_type=MESH,
        )

    def relay_copy(zs):
        return pltpu.make_async_remote_copy(
            src_ref=relay.at[zs],
            dst_ref=landed.at[5 - y, zs],
            send_sem=relay_send.at[zs],
            recv_sem=y_recv.at[(5 - y) * SIDE + zs],
            device_id=at(3 - y, z),
            device_id_type=MESH,
        )

    def z_copy(zs, half, to, landing, sems):
        blocks = pl.ds(2 * half, 2)
        return pltpu.make_async_remote_copy(
            src_ref=running.at[zs, blocks],
            dst_ref=landing.at[zs, blocks],
            send_sem=z_send.at[2 * zs + half],
            recv_sem=sems.at[2 * zs + half],
            device_id=at(y, to),
            device_id_type=MESH,
        )

    def send(j):
        zs = target(j, z)

        @pl.loop(0, y)
        def _(h):
            hop = jnp.where(y == 1, 1, jnp.where(h == 0, 2, jnp.where(h == 1, 1, 3)))
            ys = y - hop
            for c in range(CAP):
                far[ys * SIDE + zs, c] = gathered(ROW + (ys * SIDE + zs) * CAP + c).astype(far.dtype)
            pl.when(hop == 2)(lambda: y_far(ys, zs).start())
            pl.when(hop != 2)(lambda: y_near(ys, zs).start())

    def pass_on(j):
        zs = target(j, z)

        @pl.when(y >= 2)
        def _():
            pltpu.make_async_remote_copy(
                src_ref=relay.at[zs],
                dst_ref=relay.at[zs],
                send_sem=relay_send.at[zs],
                recv_sem=relay_recv.at[zs],
                device_id=at(y, z),
                device_id_type=MESH,
            ).wait_recv()
            relay_copy(zs).start()

    def add_up(j):
        zs = target(j, z)

        @pl.when((zs <= z) | (y < SIDE - 1))
        def _():
            for t in range(PER):
                total[t] = gathered(zs * PER + t)

            @pl.loop(y + 1, SIDE)
            def _(yd):
                pltpu.make_async_remote_copy(
                    src_ref=landed.at[yd, zs],
                    dst_ref=landed.at[yd, zs],
                    send_sem=relay_send.at[0],
                    recv_sem=y_recv.at[yd * SIDE + zs],
                    device_id=at(y, z),
                    device_id_type=MESH,
                ).wait_recv()
                for t in range(PER):
                    low, high = landed[yd, zs, 0], landed[yd, zs, 1]
                    got = jnp.where(picks_ref[(yd * SIDE + zs) * CAP + 1] == t, high, jnp.zeros_like(high))
                    got = jnp.where(picks_ref[(yd * SIDE + zs) * CAP] == t, low, got)
                    total[t] += got.astype(jnp.float32)

            @pl.loop(0, 2)
            def _(half):
                blocks = pl.ds(2 * half, 2)

                @pl.when((zs <= z) & (z < SIDE - 1))
                def _():
                    z_copy(zs, half, z, from_right, right_recv).wait_recv()
                    total[blocks] += from_right[zs, blocks].astype(jnp.float32)

                @pl.when((zs >= z) & (z > 0) & (y < SIDE - 1))
                def _():
                    z_copy(zs, half, z, from_left, left_recv).wait_recv()
                    total[blocks] += from_left[zs, blocks].astype(jnp.float32)

                @pl.when(zs != z)
                def _():
                    running[zs, blocks] = total[blocks].astype(running.dtype)
                    pl.when(zs < z)(lambda: z_copy(zs, half, z - 1, from_right, right_recv).start())
                    pl.when(zs > z)(lambda: z_copy(zs, half, z + 1, from_left, left_recv).start())

    send(jnp.int32(0))
    if attention:
        attention.wait()

        def between(k):
            pl.loop(*listed(k, {1: (0, 1), 4: (1, 2), 6: (2, 3), 8: (3, 4)}))(pass_on)
            pl.loop(*listed(k, {1: (1, 2), 3: (2, 3), 5: (3, 4)}))(send)
            pl.loop(*listed(k, {3: (0, 1), 6: (1, 2), 8: (2, 3), 10: (3, 4)}))(add_up)

        attention.run(between)
    else:

        @pl.loop(0, SIDE)
        def _(j):
            pass_on(j)
            pl.when(j < SIDE - 1)(lambda: send(j + 1))
            add_up(j)

    write(total)

    @pl.loop(0, SIDE)
    def _(zs):
        @pl.when((zs < z) | ((zs > z) & (y < SIDE - 1)))
        def _():
            for half in range(2):
                z_copy(zs, half, z, from_right, right_recv).wait_send()

        @pl.loop(0, y)
        def _(ys):
            y_near(ys, zs).wait_send()

        pl.when(y >= 2)(lambda: relay_copy(zs).wait_send())


def first_exchange(
    blocks_ref, count_ref, len_ref, k_ref, v_ref, held_ref, picks, place, seen, slot_of, *scratch
):
    lists = (blocks_ref, count_ref, len_ref, place, seen, slot_of)
    exchange(0, picks, k_ref, v_ref, held_ref, scratch, None, lists)


def exchange_and_attend(
    picks, place, seen, k_ref, v_ref, q_ref, do_ref, held_ref, next_ref, attn_ref, dq_ref, slots_ref, *scratch
):
    attention = Attention(0, place, seen, q_ref, do_ref, held_ref, attn_ref, dq_ref, slots_ref, scratch[:13])
    exchange(1, picks, k_ref, v_ref, next_ref, scratch[13:], attention)


def return_and_attend(
    picks, slot_of, place, seen, q_ref, do_ref, held_ref, done_ref, grads_ref, attn_ref, dq_ref, slots_ref, *scratch
):
    attention = Attention(1, place, seen, q_ref, do_ref, held_ref, attn_ref, dq_ref, slots_ref, scratch[:13])

    def write(total):
        for t in range(PER):
            grads_ref[pl.ds(t * BLOCK, BLOCK), :] = total[t].astype(grads_ref.dtype)

    give_back(picks, slot_of, done_ref, write, scratch[13:], attention)


def last_return(picks, slot_of, done_ref, grads_ref, gk_ref, gv_ref, *scratch):
    def write(total):
        gk_ref[:, :D] = grads_ref[:, :D]
        gv_ref[:, :D] = grads_ref[:, D:]
        for t in range(PER):
            rows = pl.ds(t * BLOCK, BLOCK)
            gk_ref[rows, D:] = total[t, :, :D].astype(gk_ref.dtype)
            gv_ref[rows, D:] = total[t, :, D:].astype(gv_ref.dtype)

    give_back(picks, slot_of, done_ref, write, scratch, None)


def body(query_states, key_states, value_state_rows, grad_out, vis_blocks, vis_count, vis_len):
    tokens, q_width = query_states.shape
    width = key_states.shape[1]
    lanes = q_width * D // width
    bf16 = jnp.bfloat16
    sems = lambda n: pltpu.SemaphoreType.DMA((n,))
    smem = pl.BlockSpec(memory_space=pltpu.SMEM)
    vmem = pl.BlockSpec(memory_space=pltpu.VMEM)
    hbm = pl.BlockSpec(memory_space=pltpu.HBM)
    shape = jax.ShapeDtypeStruct
    held = shape((HELD, BLOCK, 2 * D), bf16)
    half = shape((tokens, lanes), bf16)
    slots = shape((PER * VIS, BLOCK, 2 * D), bf16)
    grads = shape((tokens, 2 * D), bf16)
    whole = shape((tokens, width), bf16)

    def remote(n, mib):
        return pltpu.CompilerParams(collective_id=n, has_side_effects=True, vmem_limit_bytes=mib * MIB)

    keys = key_states.reshape(PER, BLOCK, width)
    values = value_state_rows.reshape(PER, BLOCK, width)

    sizes = (CTX * CAP, PER * VIS, PER * VIS, PER * HELD)
    held_0, picks, place, seen, slot_of = pl.pallas_call(
        first_exchange,
        out_shape=(held,) + tuple(shape((n,), jnp.int32) for n in sizes),
        in_specs=[smem] * 3 + [hbm] * 2,
        out_specs=(hbm,) + (smem,) * 4,
        scratch_shapes=exchange_scratch(sems),
        compiler_params=remote(0, 58),
    )(vis_blocks.T, vis_count, vis_len.T, keys, values)
    held_1, attn_0, dq_0, slots_0 = pl.pallas_call(
        exchange_and_attend,
        out_shape=(held, half, half, slots),
        in_specs=[smem] * 3 + [hbm] * 5,
        out_specs=(hbm, vmem, vmem, vmem),
        scratch_shapes=Attention.scratch(tokens, lanes) + exchange_scratch(sems),
        compiler_params=remote(1, 58),
    )(picks, place, seen, keys, values, query_states, grad_out, held_0)
    grads_0, attn_1, dq_1, slots_1 = pl.pallas_call(
        return_and_attend,
        out_shape=(grads, half, half, slots),
        in_specs=[smem] * 4 + [hbm] * 3 + [vmem],
        out_specs=(vmem, vmem, vmem, vmem),
        scratch_shapes=Attention.scratch(tokens, lanes) + return_scratch(sems),
        compiler_params=remote(2, 48),
    )(picks, slot_of, place, seen, query_states, grad_out, held_1, slots_0)
    grad_key, grad_value = pl.pallas_call(
        last_return,
        out_shape=(whole, whole),
        in_specs=[smem] * 2 + [vmem] * 2,
        out_specs=(vmem, vmem),
        scratch_shapes=return_scratch(sems),
        compiler_params=remote(3, 24),
    )(picks, slot_of, slots_1, grads_0)
    attention = jnp.concatenate([attn_0, attn_1], axis=1)
    grad_query = jnp.concatenate([dq_0, dq_1], axis=1)
    return attention, grad_query, grad_key, grad_value


def solution(mesh):
    rows = P(("dp", "ctx"), "head")
    return jax.shard_map(
        body,
        mesh=mesh,
        in_specs=(rows, rows, rows, rows, P("dp", None), P("dp"), P("dp", None)),
        out_specs=(rows, rows, rows, rows),
        check_vma=False,
    )
```

```python
import functools
import math

import jax
import jax.numpy as jnp
from jax import lax
from jax.experimental import pallas as pl
from jax.experimental.pallas import tpu as pltpu
from jax.sharding import PartitionSpec as P

D = 128
BLOCK = 128
PER = 4
SIDE = 4
CTX = SIDE * SIDE
VIS = 6
CAP = 2
ROW = SIDE * PER
HELD = ROW + CAP * SIDE * (SIDE - 1)
STEPS = 2 * SIDE - 1
PAIRS = [slice(p * 2 * BLOCK, (p + 1) * 2 * BLOCK) for p in range(VIS // 2)]
TN = (((0,), (0,)), ((), ()))
NEG = -1e30
INV_ROOT = 1.0 / math.sqrt(D)
EXP2_SCALE = INV_ROOT * math.log2(math.e)
MIB = 1 << 20
MESH = pl.DeviceIdType.MESH


def coords():
    me = lax.axis_index("ctx")
    return me, me // SIDE, lax.rem(me, SIDE)


def at(y, z):
    return {"ctx": lax.rem(y + SIDE, SIDE) * SIDE + z}


def barrier_neighbours(y, z):
    barrier = pltpu.get_barrier_semaphore()

    def greet(where):
        pl.semaphore_signal(barrier, inc=1, device_id=where, device_id_type=MESH)

    greet(at(y + 1, z))
    greet(at(y - 1, z))
    pl.when(z > 0)(lambda: greet(at(y, z - 1)))
    pl.when(z < SIDE - 1)(lambda: greet(at(y, z + 1)))
    pl.semaphore_wait(barrier, 2 + jnp.where(z > 0, 1, 0) + jnp.where(z < SIDE - 1, 1, 0))


def far_at(y, z):
    return pl.ds(ROW + (y * SIDE + z) * CAP, CAP)


def nth(n, z):
    d = (n + 1) // 2
    return z + jnp.where(lax.rem(n, 2) == 1, -d, d), d


def target(j, z):
    inner = jnp.where(j == 0, 3, jnp.where(j == 1, 0, jnp.where(j == 2, 2, 1)))
    return jnp.where(z == 0, 3 - j, jnp.where(z == 3, j, jnp.where(z == 1, inner, 3 - inner)))


def chosen(blocks_ref, count_ref, dst, src):
    low, high = jnp.int32(PER - 1), jnp.int32(0)
    for r in range(PER):
        row = dst * PER + r
        count = count_ref[row]
        for s in range(1, VIS):
            t = blocks_ref[s, row] - src * PER
            hit = (t >= 0) & (t < PER) & (s < count)
            low = jnp.minimum(low, jnp.where(hit, t, PER - 1))
            high = jnp.maximum(high, jnp.where(hit, t, 0))
    return low, high


def tables(blocks_ref, count_ref, len_ref, place, seen, slot_of):
    me, y, z = coords()

    @pl.loop(0, PER)
    def _(r):
        row = me * PER + r
        own = z * PER + r
        place[r * VIS] = own
        seen[r * VIS] = BLOCK

        @pl.loop(1, VIS)
        def _(s):
            block = blocks_ref[s, row]
            live = s < count_ref[row]
            src = block // PER
            t = block - src * PER
            low, _ = chosen(blocks_ref, count_ref, me, src)
            far = ROW + CAP * src + jnp.where(t == low, 0, 1)
            near = lax.rem(src, SIDE) * PER + t
            there = jnp.where(src // SIDE == y, near, far)
            place[r * VIS + s] = jnp.where(live, there, own)
            seen[r * VIS + s] = jnp.where(live, len_ref[s, row], 0)

    @pl.loop(0, HELD)
    def _(e):
        for r in range(PER):
            slot = jnp.int32(-1)
            for s in range(VIS):
                hit = (place[r * VIS + s] == e) & (seen[r * VIS + s] > 0)
                slot = jnp.where(hit, r * VIS + s, slot)
            slot_of[e * PER + r] = slot


class Attention:
    def __init__(self, head, place, seen, q_ref, do_ref, held_ref, attn_ref, dq_ref, slots_ref, scratch):
        self.place, self.seen = place, seen
        self.attn_ref, self.dq_ref, self.slots_ref = attn_ref, dq_ref, slots_ref
        (self.q, self.do, self.held, self.qs, self.dos, self.qt, self.dot, self.keys, self.values,
         self.scores, self.scale, self.delta, sem) = scratch
        lanes = self.q.shape[1]
        columns = pl.ds(head * lanes, lanes)
        self.loads = (
            pltpu.make_async_copy(q_ref.at[:, columns], self.q, sem.at[0]),
            pltpu.make_async_copy(do_ref.at[:, columns], self.do, sem.at[1]),
            pltpu.make_async_copy(held_ref, self.held, sem.at[2]),
        )

    @staticmethod
    def scratch(tokens, lanes):
        f32, bf16 = jnp.float32, jnp.bfloat16
        return [
            pltpu.VMEM((tokens, lanes), bf16),
            pltpu.VMEM((tokens, lanes), bf16),
            pltpu.VMEM((HELD, BLOCK, 2 * D), bf16),
            pltpu.VMEM((lanes, D), bf16),
            pltpu.VMEM((lanes, D), bf16),
            pltpu.VMEM((D, lanes), bf16),
            pltpu.VMEM((D, lanes), bf16),
            pltpu.VMEM((VIS * BLOCK, D), bf16),
            pltpu.VMEM((VIS * BLOCK, D), bf16),
            pltpu.VMEM((VIS * BLOCK, lanes), f32),
            pltpu.VMEM((1, lanes), f32),
            pltpu.VMEM((1, lanes), f32),
            pltpu.SemaphoreType.DMA((3,)),
        ]

    def start(self):
        for load in self.loads[:2]:
            load.start()

    def load_held(self):
        self.loads[2].start()

    def wait_all(self):
        for load in self.loads:
            load.wait()

    def wait(self):
        self.load_held()
        self.wait_all()

    def weigh(self, i):
        f32, bf16 = jnp.float32, jnp.bfloat16
        lanes = self.q.shape[1]
        tokens = pl.ds(pl.multiple_of(i * BLOCK, BLOCK), BLOCK)
        for h in range(lanes // D):
            part = slice(h * D, (h + 1) * D)
            q, do = self.q[tokens, part], self.do[tokens, part]
            self.qs[part, :] = q
            self.dos[part, :] = do
            self.qt[:, part] = q.T
            self.dot[:, part] = do.T
        for s in range(VIS):
            block = self.held[self.place[i * VIS + s]]
            rows = slice(s * BLOCK, (s + 1) * BLOCK)
            self.keys[rows, :] = block[:, :D]
            self.values[rows, :] = block[:, D:]

        key_pos = lax.broadcasted_iota(jnp.int32, (BLOCK, lanes), 0)
        query_pos = lax.broadcasted_iota(jnp.int32, (BLOCK, lanes), 1) & (BLOCK - 1)
        top = jnp.full((1, lanes), NEG, f32)
        for p, rows in enumerate(PAIRS):
            raw = jnp.dot(self.keys[rows, :], self.qt[...], preferred_element_type=f32)
            first = key_pos <= query_pos if p == 0 else key_pos < self.seen[i * VIS + 2 * p]
            second = key_pos < self.seen[i * VIS + 2 * p + 1]
            raw = jnp.where(jnp.concatenate([first, second], axis=0), raw, NEG)
            self.scores[rows, :] = raw
            top = jnp.maximum(top, jnp.max(raw, axis=0, keepdims=True))
        shift = top * EXP2_SCALE
        total = jnp.zeros((1, lanes), f32)
        for rows in PAIRS:
            w = jnp.exp2(self.scores[rows, :] * EXP2_SCALE - shift)
            self.scores[rows, :] = w
            total = total + jnp.sum(w, axis=0, keepdims=True)
        self.scale[...] = 1.0 / total

    def mix(self, i):
        f32, bf16 = jnp.float32, jnp.bfloat16
        lanes = self.q.shape[1]
        scale = self.scale[...]
        attn = jnp.zeros((D, lanes), f32)
        for p, rows in enumerate(PAIRS):
            probs = self.scores[rows, :] * scale
            self.scores[rows, :] = probs
            probs = probs.astype(bf16)
            product = jnp.dot(probs, self.dos[...], preferred_element_type=f32).astype(bf16)
            self.slots_ref[i * VIS + 2 * p, :, D:] = product[:BLOCK]
            self.slots_ref[i * VIS + 2 * p + 1, :, D:] = product[BLOCK:]
            attn = attn + lax.dot_general(self.values[rows, :], probs, TN, preferred_element_type=f32)
        self.delta[...] = jnp.sum(attn * self.dot[...].astype(f32), axis=0, keepdims=True)
        self.put(self.attn_ref, i, attn)

    def back(self, i):
        f32, bf16 = jnp.float32, jnp.bfloat16
        lanes = self.q.shape[1]
        delta = self.delta[...]
        dq = jnp.zeros((D, lanes), f32)
        for p, rows in enumerate(PAIRS):
            dprobs = jnp.dot(self.values[rows, :], self.dot[...], preferred_element_type=f32)
            ds = (self.scores[rows, :] * (dprobs - delta)).astype(bf16)
            product = (jnp.dot(ds, self.qs[...], preferred_element_type=f32) * INV_ROOT).astype(bf16)
            self.slots_ref[i * VIS + 2 * p, :, :D] = product[:BLOCK]
            self.slots_ref[i * VIS + 2 * p + 1, :, :D] = product[BLOCK:]
            dq = dq + lax.dot_general(self.keys[rows, :], ds, TN, preferred_element_type=f32)
        self.put(self.dq_ref, i, dq * INV_ROOT)

    def put(self, ref, i, transposed):
        tokens = pl.ds(pl.multiple_of(i * BLOCK, BLOCK), BLOCK)
        for h in range(transposed.shape[1] // D):
            part = slice(h * D, (h + 1) * D)
            ref[tokens, part] = transposed[:, part].astype(ref.dtype).T

    def run(self, between):
        @pl.loop(0, 3 * PER)
        def _(k):
            i = k // 3
            phase = k - 3 * i
            pl.when(phase == 0)(lambda: self.weigh(i))
            pl.when(phase == 1)(lambda: self.mix(i))
            pl.when(phase == 2)(lambda: self.back(i))
            between(k)


def listed(k, table):
    low = high = jnp.int32(0)
    for key, (first, last) in table.items():
        low, high = jnp.where(k == key, first, low), jnp.where(k == key, last, high)
    return low, high


def exchange_scratch(sems):
    bf16 = jnp.bfloat16
    return [
        pltpu.VMEM((SIDE, PER, BLOCK, 2 * D), bf16),
        pltpu.VMEM((SIDE, SIDE, CAP, BLOCK, 2 * D), bf16),
        pltpu.VMEM((SIDE, CAP, BLOCK, 2 * D), bf16),
        sems(SIDE),
        sems(SIDE),
        sems(SIDE),
        sems(CTX),
        sems(CTX),
        sems(SIDE),
        sems(SIDE),
        sems(SIDE),
        sems(2),
    ]


class Steps:
    def __init__(self, **steps):
        self.__dict__.update(steps)


def exchange(head, picks_ref, k_ref, v_ref, out_ref, scratch, lists):
    row, packed, relay, z_recv, up_send, down_send, far_recv, y_send, relay_recv, relay_send, keep_sem, in_sem = scratch
    me, y, z = coords()
    columns = pl.ds(head * D, D)
    mine_in = (
        pltpu.make_async_copy(k_ref.at[:, :, columns], row.at[z, :, :, pl.ds(0, D)], in_sem.at[0]),
        pltpu.make_async_copy(v_ref.at[:, :, columns], row.at[z, :, :, pl.ds(D, D)], in_sem.at[1]),
    )

    def load():
        for copy in mine_in:
            copy.start()

    def loaded():
        for copy in mine_in:
            copy.wait()

    def z_copy(zs, to, sems):
        return pltpu.make_async_remote_copy(
            src_ref=row.at[zs],
            dst_ref=row.at[zs],
            send_sem=sems.at[zs],
            recv_sem=z_recv.at[zs],
            device_id=at(y, to),
            device_id_type=MESH,
        )

    def y_near(yd, zs):
        return pltpu.make_async_remote_copy(
            src_ref=packed.at[yd, zs],
            dst_ref=out_ref.at[far_at(y, zs)],
            send_sem=y_send.at[yd * SIDE + zs],
            recv_sem=far_recv.at[y * SIDE + zs],
            device_id=at(yd, z),
            device_id_type=MESH,
        )

    def y_far(yd, zs):
        return pltpu.make_async_remote_copy(
            src_ref=packed.at[yd, zs],
            dst_ref=relay.at[zs],
            send_sem=y_send.at[yd * SIDE + zs],
            recv_sem=relay_recv.at[zs],
            device_id=at(jnp.where(y == 0, SIDE - 1, 2), z),
            device_id_type=MESH,
        )

    def relay_copy(zs):
        return pltpu.make_async_remote_copy(
            src_ref=relay.at[zs],
            dst_ref=out_ref.at[far_at(3 - y, zs)],
            send_sem=relay_send.at[zs],
            recv_sem=far_recv.at[(3 - y) * SIDE + zs],
            device_id=at(5 - y, z),
            device_id_type=MESH,
        )

    def keep(zs):
        return pltpu.make_async_copy(row.at[zs], out_ref.at[pl.ds(zs * PER, PER)], keep_sem.at[zs])

    def wanted(zs):
        inside = (zs >= 0) & (zs < SIDE)
        return inside, inside & ((zs <= z) | (y < SIDE - 1))

    def pack(yd, zs):
        first = (yd * SIDE + zs) * CAP
        if lists:
            blocks_ref, count_ref = lists[:2]
            picks_ref[first], picks_ref[first + 1] = chosen(
                blocks_ref, count_ref, yd * SIDE + z, y * SIDE + zs
            )
        for c in range(CAP):
            pick = picks_ref[first + c]
            block = row[zs, 0]
            for t in range(1, PER):
                block = jnp.where(pick == t, row[zs, t], block)
            packed[yd, zs, c] = block

    def step(n):
        zs, d = nth(n, z)
        inside, mine = wanted(zs)

        @pl.when(mine)
        def _():
            pl.when(d > 0)(lambda: z_copy(zs, z, up_send).wait_recv())
            pl.when((zs <= z) & (z < SIDE - 1))(lambda: z_copy(zs, z + 1, up_send).start())
            pl.when((zs >= z) & (z > 0) & (y < SIDE - 1))(
                lambda: z_copy(zs, z - 1, down_send).start()
            )
            keep(zs).start()

        @pl.when(inside)
        def _():
            @pl.loop(0, SIDE - 1 - y)
            def _(h):
                hop = jnp.where(y == 2, 1, jnp.where(h == 0, 2, jnp.where(h == 1, 1, 3)))
                yd = y + hop
                pack(yd, zs)
                pl.when(hop == 2)(lambda: y_far(yd, zs).start())
                pl.when(hop != 2)(lambda: y_near(yd, zs).start())

    def relay_step(n):
        zs, _ = nth(n, z)

        @pl.when((zs >= 0) & (zs < SIDE) & (y >= 2))
        def _():
            pltpu.make_async_remote_copy(
                src_ref=relay.at[zs],
                dst_ref=relay.at[zs],
                send_sem=relay_send.at[zs],
                recv_sem=relay_recv.at[zs],
                device_id=at(y, z),
                device_id_type=MESH,
            ).wait_recv()
            relay_copy(zs).start()

    def arrived():
        @pl.loop(0, y * SIDE)
        def _(n):
            pltpu.make_async_remote_copy(
                src_ref=packed.at[0, 0],
                dst_ref=out_ref.at[pl.ds(ROW + n * CAP, CAP)],
                send_sem=relay_send.at[0],
                recv_sem=far_recv.at[n],
                device_id=at(y, z),
                device_id_type=MESH,
            ).wait_recv()

        @pl.loop(0, SIDE)
        def _(zs):
            _, mine = wanted(zs)
            pl.when(mine)(lambda: keep(zs).wait())

    def sent():
        @pl.loop(0, SIDE)
        def _(zs):
            _, mine = wanted(zs)

            @pl.when(mine)
            def _():
                pl.when((zs <= z) & (z < SIDE - 1))(
                    lambda: z_copy(zs, z + 1, up_send).wait_send()
                )
                pl.when((zs >= z) & (z > 0) & (y < SIDE - 1))(
                    lambda: z_copy(zs, z - 1, down_send).wait_send()
                )

            @pl.loop(y + 1, SIDE)
            def _(yd):
                y_near(yd, zs).wait_send()

            pl.when(y >= 2)(lambda: relay_copy(zs).wait_send())

    return Steps(load=load, loaded=loaded, step=step, relay=relay_step, arrived=arrived, sent=sent)


def return_scratch(sems):
    bf16 = jnp.bfloat16
    return [
        pltpu.VMEM((SIDE * (SIDE - 1), CAP, BLOCK, 2 * D), bf16),
        pltpu.VMEM((SIDE, SIDE, CAP, BLOCK, 2 * D), bf16),
        pltpu.VMEM((SIDE, CAP, BLOCK, 2 * D), bf16),
        pltpu.VMEM((SIDE, PER, BLOCK, 2 * D), bf16),
        pltpu.VMEM((SIDE, PER, BLOCK, 2 * D), bf16),
        pltpu.VMEM((SIDE, PER, BLOCK, 2 * D), bf16),
        pltpu.VMEM((PER, BLOCK, 2 * D), jnp.float32),
        sems(CTX),
        sems(CTX),
        sems(SIDE),
        sems(SIDE),
        sems(2 * SIDE),
        sems(2 * SIDE),
        sems(2 * SIDE),
    ]


def give_back(picks_ref, slot_of, slots_ref, scratch):
    (far, landed, relay, running, from_left, from_right, total,
     y_send, y_recv, relay_send, relay_recv, z_send, left_recv, right_recv) = scratch
    me, y, z = coords()

    def gathered(e):
        out = jnp.zeros((BLOCK, 2 * D), jnp.float32)
        for r in range(PER):
            slot = slot_of[e * PER + r]
            got = slots_ref[jnp.maximum(slot, 0)]
            out = out + jnp.where(slot >= 0, got, jnp.zeros_like(got)).astype(jnp.float32)
        return out

    def y_near(ys, zs):
        return pltpu.make_async_remote_copy(
            src_ref=far.at[ys * SIDE + zs],
            dst_ref=landed.at[y, zs],
            send_sem=y_send.at[ys * SIDE + zs],
            recv_sem=y_recv.at[y * SIDE + zs],
            device_id=at(ys, z),
            device_id_type=MESH,
        )

    def y_far(ys, zs):
        return pltpu.make_async_remote_copy(
            src_ref=far.at[ys * SIDE + zs],
            dst_ref=relay.at[zs],
            send_sem=y_send.at[ys * SIDE + zs],
            recv_sem=relay_recv.at[zs],
            device_id=at(5 - y, z),
            device_id_type=MESH,
        )

    def relay_copy(zs):
        return pltpu.make_async_remote_copy(
            src_ref=relay.at[zs],
            dst_ref=landed.at[5 - y, zs],
            send_sem=relay_send.at[zs],
            recv_sem=y_recv.at[(5 - y) * SIDE + zs],
            device_id=at(3 - y, z),
            device_id_type=MESH,
        )

    def z_copy(zs, half, to, landing, sems):
        blocks = pl.ds(2 * half, 2)
        return pltpu.make_async_remote_copy(
            src_ref=running.at[zs, blocks],
            dst_ref=landing.at[zs, blocks],
            send_sem=z_send.at[2 * zs + half],
            recv_sem=sems.at[2 * zs + half],
            device_id=at(y, to),
            device_id_type=MESH,
        )

    def send(j):
        zs = target(j, z)

        @pl.loop(0, y)
        def _(h):
            hop = jnp.where(y == 1, 1, jnp.where(h == 0, 2, jnp.where(h == 1, 1, 3)))
            ys = y - hop
            for c in range(CAP):
                far[ys * SIDE + zs, c] = gathered(ROW + (ys * SIDE + zs) * CAP + c).astype(far.dtype)
            pl.when(hop == 2)(lambda: y_far(ys, zs).start())
            pl.when(hop != 2)(lambda: y_near(ys, zs).start())

    def pass_on(j):
        zs = target(j, z)

        @pl.when(y >= 2)
        def _():
            pltpu.make_async_remote_copy(
                src_ref=relay.at[zs],
                dst_ref=relay.at[zs],
                send_sem=relay_send.at[zs],
                recv_sem=relay_recv.at[zs],
                device_id=at(y, z),
                device_id_type=MESH,
            ).wait_recv()
            relay_copy(zs).start()

    def add_up(j):
        zs = target(j, z)

        @pl.when((zs <= z) | (y < SIDE - 1))
        def _():
            for t in range(PER):
                total[t] = gathered(zs * PER + t)

            @pl.loop(y + 1, SIDE)
            def _(yd):
                pltpu.make_async_remote_copy(
                    src_ref=landed.at[yd, zs],
                    dst_ref=landed.at[yd, zs],
                    send_sem=relay_send.at[0],
                    recv_sem=y_recv.at[yd * SIDE + zs],
                    device_id=at(y, z),
                    device_id_type=MESH,
                ).wait_recv()
                for t in range(PER):
                    low, high = landed[yd, zs, 0], landed[yd, zs, 1]
                    got = jnp.where(picks_ref[(yd * SIDE + zs) * CAP + 1] == t, high, jnp.zeros_like(high))
                    got = jnp.where(picks_ref[(yd * SIDE + zs) * CAP] == t, low, got)
                    total[t] += got.astype(jnp.float32)

            @pl.loop(0, 2)
            def _(half):
                blocks = pl.ds(2 * half, 2)

                @pl.when((zs <= z) & (z < SIDE - 1))
                def _():
                    z_copy(zs, half, z, from_right, right_recv).wait_recv()
                    total[blocks] += from_right[zs, blocks].astype(jnp.float32)

                @pl.when((zs >= z) & (z > 0) & (y < SIDE - 1))
                def _():
                    z_copy(zs, half, z, from_left, left_recv).wait_recv()
                    total[blocks] += from_left[zs, blocks].astype(jnp.float32)

                @pl.when(zs != z)
                def _():
                    running[zs, blocks] = total[blocks].astype(running.dtype)
                    pl.when(zs < z)(lambda: z_copy(zs, half, z - 1, from_right, right_recv).start())
                    pl.when(zs > z)(lambda: z_copy(zs, half, z + 1, from_left, left_recv).start())

    def sent():
        @pl.loop(0, SIDE)
        def _(zs):
            @pl.when((zs < z) | ((zs > z) & (y < SIDE - 1)))
            def _():
                for half in range(2):
                    z_copy(zs, half, z, from_right, right_recv).wait_send()

            @pl.loop(0, y)
            def _(ys):
                y_near(ys, zs).wait_send()

            pl.when(y >= 2)(lambda: relay_copy(zs).wait_send())

    return Steps(send=send, pass_on=pass_on, add_up=add_up, sent=sent, total=total)


N_ATTEND, N_EXCHANGE, N_RETURN = 13, 12, 14


def gather_and_attend(
    blocks_ref, count_ref, len_ref, k_ref, v_ref, q_ref, do_ref,
    held_0, held_1, picks, place, seen, slot_of, attn_ref, dq_ref, slots_ref, *scratch,
):
    _, y, z = coords()
    lists = (blocks_ref, count_ref, len_ref, place, seen, slot_of)
    attention = Attention(0, place, seen, q_ref, do_ref, held_0, attn_ref, dq_ref, slots_ref, scratch[:N_ATTEND])
    scratch = scratch[N_ATTEND:]
    first = exchange(0, picks, k_ref, v_ref, held_0, scratch[:N_EXCHANGE], lists)
    second = exchange(1, picks, k_ref, v_ref, held_1, scratch[N_EXCHANGE:], None)
    first.load()
    second.load()
    attention.start()
    barrier_neighbours(y, z)
    first.loaded()
    first.step(jnp.int32(0))
    tables(*lists)
    second.loaded()

    @pl.loop(1, STEPS)
    def _(n):
        first.step(n)
        first.relay(n - 1)

    second.step(jnp.int32(0))
    first.relay(jnp.int32(STEPS - 1))

    @pl.loop(1, 3)
    def _(n):
        second.step(n)
        second.relay(n - 1)

    first.arrived()
    attention.wait()

    def between(k):
        pl.loop(*listed(k, {0: (3, 5), 4: (5, 7)}))(second.step)
        pl.loop(*listed(k, {0: (2, 3), 2: (3, 5), 7: (5, 7)}))(second.relay)

    attention.run(between)
    second.arrived()
    first.sent()
    second.sent()


def attend_and_return(
    picks, slot_of, place, seen, q_ref, do_ref, held_ref, done_ref,
    gk_ref, gv_ref, attn_ref, dq_ref, slots_ref, *scratch,
):
    _, y, z = coords()
    attention = Attention(1, place, seen, q_ref, do_ref, held_ref, attn_ref, dq_ref, slots_ref, scratch[:N_ATTEND])
    scratch = scratch[N_ATTEND:]
    first = give_back(picks, slot_of, done_ref, scratch[:N_RETURN])
    second = give_back(picks, slot_of, slots_ref, scratch[N_RETURN:])
    attention.start()
    attention.load_held()
    barrier_neighbours(y, z)
    first.send(jnp.int32(0))
    attention.wait_all()

    def between(k):
        pl.loop(*listed(k, {4: (0, 1), 7: (1, 2), 10: (2, 3)}))(first.add_up)
        pl.loop(*listed(k, {1: (0, 1), 4: (1, 2), 7: (2, 3), 10: (3, 4)}))(first.pass_on)
        pl.loop(*listed(k, {1: (1, 2), 4: (2, 3), 7: (3, 4)}))(first.send)

    attention.run(between)
    second.send(jnp.int32(0))
    first.add_up(jnp.int32(SIDE - 1))

    @pl.loop(0, SIDE)
    def _(j):
        second.pass_on(j)
        pl.when(j < SIDE - 1)(lambda: second.send(j + 1))
        second.add_up(j)

    for part, lanes in ((first, slice(0, D)), (second, slice(D, 2 * D))):
        for t in range(PER):
            rows = pl.ds(t * BLOCK, BLOCK)
            gk_ref[rows, lanes] = part.total[t, :, :D].astype(gk_ref.dtype)
            gv_ref[rows, lanes] = part.total[t, :, D:].astype(gv_ref.dtype)
    first.sent()
    second.sent()


def body(query_states, key_states, value_state_rows, grad_out, vis_blocks, vis_count, vis_len):
    tokens, q_width = query_states.shape
    width = key_states.shape[1]
    lanes = q_width * D // width
    bf16 = jnp.bfloat16
    sems = lambda n: pltpu.SemaphoreType.DMA((n,))
    smem = pl.BlockSpec(memory_space=pltpu.SMEM)
    vmem = pl.BlockSpec(memory_space=pltpu.VMEM)
    hbm = pl.BlockSpec(memory_space=pltpu.HBM)
    shape = jax.ShapeDtypeStruct
    held = shape((HELD, BLOCK, 2 * D), bf16)
    half = shape((tokens, lanes), bf16)
    slots = shape((PER * VIS, BLOCK, 2 * D), bf16)
    whole = shape((tokens, width), bf16)

    def remote(n, mib):
        return pltpu.CompilerParams(collective_id=n, has_side_effects=True, vmem_limit_bytes=mib * MIB)

    keys = key_states.reshape(PER, BLOCK, width)
    values = value_state_rows.reshape(PER, BLOCK, width)

    sizes = (CTX * CAP, PER * VIS, PER * VIS, PER * HELD)
    _, held_1, picks, place, seen, slot_of, attn_0, dq_0, slots_0 = pl.pallas_call(
        gather_and_attend,
        out_shape=(held, held) + tuple(shape((n,), jnp.int32) for n in sizes) + (half, half, slots),
        in_specs=[smem] * 3 + [hbm] * 4,
        out_specs=(hbm,) * 2 + (smem,) * 4 + (vmem,) * 3,
        scratch_shapes=Attention.scratch(tokens, lanes) + 2 * exchange_scratch(sems),
        compiler_params=remote(0, 58),
    )(vis_blocks.T, vis_count, vis_len.T, keys, values, query_states, grad_out)
    grad_key, grad_value, attn_1, dq_1, _ = pl.pallas_call(
        attend_and_return,
        out_shape=(whole, whole, half, half, slots),
        in_specs=[smem] * 4 + [hbm] * 3 + [vmem],
        out_specs=(vmem,) * 5,
        scratch_shapes=Attention.scratch(tokens, lanes) + 2 * return_scratch(sems),
        compiler_params=remote(1, 48),
    )(picks, slot_of, place, seen, query_states, grad_out, held_1, slots_0)
    attention = jnp.concatenate([attn_0, attn_1], axis=1)
    grad_query = jnp.concatenate([dq_0, dq_1], axis=1)
    return attention, grad_query, grad_key, grad_value


def solution(mesh):
    rows = P(("dp", "ctx"), "head")
    return jax.shard_map(
        body,
        mesh=mesh,
        in_specs=(rows, rows, rows, rows, P("dp", None), P("dp"), P("dp", None)),
        out_specs=(rows, rows, rows, rows),
        check_vma=False,
    )
```

```python
import functools
import math

import jax
import jax.numpy as jnp
from jax import lax
from jax.experimental import pallas as pl
from jax.experimental.pallas import tpu as pltpu
from jax.sharding import PartitionSpec as P

D = 128
BLOCK = 128
PER = 4
SIDE = 4
CTX = SIDE * SIDE
VIS = 6
CAP = 2
ROW = SIDE * PER
HELD = ROW + CAP * SIDE * (SIDE - 1)
STEPS = 2 * SIDE - 1
PAIRS = [slice(p * 2 * BLOCK, (p + 1) * 2 * BLOCK) for p in range(VIS // 2)]
TN = (((0,), (0,)), ((), ()))
NEG = -1e30
INV_ROOT = 1.0 / math.sqrt(D)
EXP2_SCALE = INV_ROOT * math.log2(math.e)
MIB = 1 << 20
MESH = pl.DeviceIdType.MESH


def coords():
    me = lax.axis_index("ctx")
    return me, me // SIDE, lax.rem(me, SIDE)


def at(y, z):
    return {"ctx": lax.rem(y + SIDE, SIDE) * SIDE + z}


def barrier_neighbours(y, z):
    barrier = pltpu.get_barrier_semaphore()

    def greet(where):
        pl.semaphore_signal(barrier, inc=1, device_id=where, device_id_type=MESH)

    greet(at(y + 1, z))
    greet(at(y - 1, z))
    pl.when(z > 0)(lambda: greet(at(y, z - 1)))
    pl.when(z < SIDE - 1)(lambda: greet(at(y, z + 1)))
    pl.semaphore_wait(barrier, 2 + jnp.where(z > 0, 1, 0) + jnp.where(z < SIDE - 1, 1, 0))


def far_at(y, z):
    return pl.ds(ROW + (y * SIDE + z) * CAP, CAP)


def nth(n, z):
    d = (n + 1) // 2
    return z + jnp.where(lax.rem(n, 2) == 1, -d, d), d


def target(j, z):
    inner = jnp.where(j == 0, 3, jnp.where(j == 1, 0, jnp.where(j == 2, 2, 1)))
    return jnp.where(z == 0, 3 - j, jnp.where(z == 3, j, jnp.where(z == 1, inner, 3 - inner)))


class Part:
    def __init__(self, ref, base):
        self.ref, self.base = ref, base

    def __getitem__(self, n):
        return self.ref[self.base + n]

    def __setitem__(self, n, value):
        self.ref[self.base + n] = value


def parts(ref):
    bases = (0, CTX * CAP, CTX * CAP + PER * VIS, CTX * CAP + 2 * PER * VIS)
    return tuple(Part(ref, base) for base in bases)


def chosen(blocks_ref, count_ref, dst, src):
    low, high = jnp.int32(PER - 1), jnp.int32(0)
    for r in range(PER):
        row = dst * PER + r
        count = count_ref[row]
        for s in range(1, VIS):
            t = blocks_ref[s, row] - src * PER
            hit = (t >= 0) & (t < PER) & (s < count)
            low = jnp.minimum(low, jnp.where(hit, t, PER - 1))
            high = jnp.maximum(high, jnp.where(hit, t, 0))
    return low, high


def tables(blocks_ref, count_ref, len_ref, place, seen, slot_of):
    me, y, z = coords()

    @pl.loop(0, PER)
    def _(r):
        row = me * PER + r
        own = z * PER + r
        place[r * VIS] = own
        seen[r * VIS] = BLOCK

        @pl.loop(1, VIS)
        def _(s):
            block = blocks_ref[s, row]
            live = s < count_ref[row]
            src = block // PER
            t = block - src * PER
            low, _ = chosen(blocks_ref, count_ref, me, src)
            far = ROW + CAP * src + jnp.where(t == low, 0, 1)
            near = lax.rem(src, SIDE) * PER + t
            there = jnp.where(src // SIDE == y, near, far)
            place[r * VIS + s] = jnp.where(live, there, own)
            seen[r * VIS + s] = jnp.where(live, len_ref[s, row], 0)

    @pl.loop(0, HELD)
    def _(e):
        for r in range(PER):
            slot = jnp.int32(-1)
            for s in range(VIS):
                hit = (place[r * VIS + s] == e) & (seen[r * VIS + s] > 0)
                slot = jnp.where(hit, r * VIS + s, slot)
            slot_of[e * PER + r] = slot


class Attention:
    def __init__(self, head, place, seen, q_ref, do_ref, held_ref, attn_ref, dq_ref, slots_ref, scratch):
        self.place, self.seen = place, seen
        self.attn_ref, self.dq_ref, self.slots_ref = attn_ref, dq_ref, slots_ref
        (self.q, self.do, self.held, self.qs, self.dos, self.qt, self.dot, self.keys, self.values,
         self.scores, self.scale, self.delta, sem) = scratch
        lanes = self.q.shape[1]
        columns = pl.ds(head * lanes, lanes)
        self.loads = (
            pltpu.make_async_copy(q_ref.at[:, columns], self.q, sem.at[0]),
            pltpu.make_async_copy(do_ref.at[:, columns], self.do, sem.at[1]),
            pltpu.make_async_copy(held_ref, self.held, sem.at[2]),
        )

    @staticmethod
    def scratch(tokens, lanes):
        f32, bf16 = jnp.float32, jnp.bfloat16
        return [
            pltpu.VMEM((tokens, lanes), bf16),
            pltpu.VMEM((tokens, lanes), bf16),
            pltpu.VMEM((HELD, BLOCK, 2 * D), bf16),
            pltpu.VMEM((lanes, D), bf16),
            pltpu.VMEM((lanes, D), bf16),
            pltpu.VMEM((D, lanes), bf16),
            pltpu.VMEM((D, lanes), bf16),
            pltpu.VMEM((VIS * BLOCK, D), bf16),
            pltpu.VMEM((VIS * BLOCK, D), bf16),
            pltpu.VMEM((VIS * BLOCK, lanes), f32),
            pltpu.VMEM((1, lanes), f32),
            pltpu.VMEM((1, lanes), f32),
            pltpu.SemaphoreType.DMA((3,)),
        ]

    def start(self):
        for load in self.loads[:2]:
            load.start()

    def load_held(self):
        self.loads[2].start()

    def wait_all(self):
        for load in self.loads:
            load.wait()

    def wait(self):
        self.load_held()
        self.wait_all()

    def weigh(self, i):
        f32, bf16 = jnp.float32, jnp.bfloat16
        lanes = self.q.shape[1]
        tokens = pl.ds(pl.multiple_of(i * BLOCK, BLOCK), BLOCK)
        for h in range(lanes // D):
            part = slice(h * D, (h + 1) * D)
            q, do = self.q[tokens, part], self.do[tokens, part]
            self.qs[part, :] = q
            self.dos[part, :] = do
            self.qt[:, part] = q.T
            self.dot[:, part] = do.T
        for s in range(VIS):
            block = self.held[self.place[i * VIS + s]]
            rows = slice(s * BLOCK, (s + 1) * BLOCK)
            self.keys[rows, :] = block[:, :D]
            self.values[rows, :] = block[:, D:]

        key_pos = lax.broadcasted_iota(jnp.int32, (BLOCK, lanes), 0)
        query_pos = lax.broadcasted_iota(jnp.int32, (BLOCK, lanes), 1) & (BLOCK - 1)
        top = jnp.full((1, lanes), NEG, f32)
        for p, rows in enumerate(PAIRS):
            raw = jnp.dot(self.keys[rows, :], self.qt[...], preferred_element_type=f32)
            first = key_pos <= query_pos if p == 0 else key_pos < self.seen[i * VIS + 2 * p]
            second = key_pos < self.seen[i * VIS + 2 * p + 1]
            raw = jnp.where(jnp.concatenate([first, second], axis=0), raw, NEG)
            self.scores[rows, :] = raw
            top = jnp.maximum(top, jnp.max(raw, axis=0, keepdims=True))
        shift = top * EXP2_SCALE
        total = jnp.zeros((1, lanes), f32)
        for rows in PAIRS:
            w = jnp.exp2(self.scores[rows, :] * EXP2_SCALE - shift)
            self.scores[rows, :] = w
            total = total + jnp.sum(w, axis=0, keepdims=True)
        self.scale[...] = 1.0 / total

    def mix(self, i):
        f32, bf16 = jnp.float32, jnp.bfloat16
        lanes = self.q.shape[1]
        scale = self.scale[...]
        attn = jnp.zeros((D, lanes), f32)
        for p, rows in enumerate(PAIRS):
            probs = self.scores[rows, :] * scale
            self.scores[rows, :] = probs
            probs = probs.astype(bf16)
            product = jnp.dot(probs, self.dos[...], preferred_element_type=f32).astype(bf16)
            self.slots_ref[i * VIS + 2 * p, :, D:] = product[:BLOCK]
            self.slots_ref[i * VIS + 2 * p + 1, :, D:] = product[BLOCK:]
            attn = attn + lax.dot_general(self.values[rows, :], probs, TN, preferred_element_type=f32)
        self.delta[...] = jnp.sum(attn * self.dot[...].astype(f32), axis=0, keepdims=True)
        self.put(self.attn_ref, i, attn)

    def back(self, i):
        f32, bf16 = jnp.float32, jnp.bfloat16
        lanes = self.q.shape[1]
        delta = self.delta[...]
        dq = jnp.zeros((D, lanes), f32)
        for p, rows in enumerate(PAIRS):
            dprobs = jnp.dot(self.values[rows, :], self.dot[...], preferred_element_type=f32)
            ds = (self.scores[rows, :] * (dprobs - delta)).astype(bf16)
            product = (jnp.dot(ds, self.qs[...], preferred_element_type=f32) * INV_ROOT).astype(bf16)
            self.slots_ref[i * VIS + 2 * p, :, :D] = product[:BLOCK]
            self.slots_ref[i * VIS + 2 * p + 1, :, :D] = product[BLOCK:]
            dq = dq + lax.dot_general(self.keys[rows, :], ds, TN, preferred_element_type=f32)
        self.put(self.dq_ref, i, dq * INV_ROOT)

    def put(self, ref, i, transposed):
        tokens = pl.ds(pl.multiple_of(i * BLOCK, BLOCK), BLOCK)
        for h in range(transposed.shape[1] // D):
            part = slice(h * D, (h + 1) * D)
            ref[tokens, part] = transposed[:, part].astype(ref.dtype).T

    def run(self, between):
        @pl.loop(0, 3 * PER)
        def _(k):
            i = k // 3
            phase = k - 3 * i
            pl.when(phase == 0)(lambda: self.weigh(i))
            pl.when(phase == 1)(lambda: self.mix(i))
            pl.when(phase == 2)(lambda: self.back(i))
            between(k)


def listed(k, table):
    low = high = jnp.int32(0)
    for key, (first, last) in table.items():
        low, high = jnp.where(k == key, first, low), jnp.where(k == key, last, high)
    return low, high


def exchange_scratch(sems):
    bf16 = jnp.bfloat16
    return [
        pltpu.VMEM((SIDE, PER, BLOCK, 2 * D), bf16),
        pltpu.VMEM((SIDE, SIDE, CAP, BLOCK, 2 * D), bf16),
        pltpu.VMEM((SIDE, CAP, BLOCK, 2 * D), bf16),
        sems(SIDE),
        sems(SIDE),
        sems(SIDE),
        sems(CTX),
        sems(CTX),
        sems(SIDE),
        sems(SIDE),
        sems(SIDE),
        sems(2),
    ]


class Steps:
    def __init__(self, **steps):
        self.__dict__.update(steps)


def exchange(head, picks_ref, k_ref, v_ref, out_ref, scratch, lists):
    row, packed, relay, z_recv, up_send, down_send, far_recv, y_send, relay_recv, relay_send, keep_sem, in_sem = scratch
    me, y, z = coords()
    columns = pl.ds(head * D, D)
    mine_in = (
        pltpu.make_async_copy(k_ref.at[:, :, columns], row.at[z, :, :, pl.ds(0, D)], in_sem.at[0]),
        pltpu.make_async_copy(v_ref.at[:, :, columns], row.at[z, :, :, pl.ds(D, D)], in_sem.at[1]),
    )

    def load():
        for copy in mine_in:
            copy.start()

    def loaded():
        for copy in mine_in:
            copy.wait()

    def z_copy(zs, to, sems):
        return pltpu.make_async_remote_copy(
            src_ref=row.at[zs],
            dst_ref=row.at[zs],
            send_sem=sems.at[zs],
            recv_sem=z_recv.at[zs],
            device_id=at(y, to),
            device_id_type=MESH,
        )

    def y_near(yd, zs):
        return pltpu.make_async_remote_copy(
            src_ref=packed.at[yd, zs],
            dst_ref=out_ref.at[far_at(y, zs)],
            send_sem=y_send.at[yd * SIDE + zs],
            recv_sem=far_recv.at[y * SIDE + zs],
            device_id=at(yd, z),
            device_id_type=MESH,
        )

    def y_far(yd, zs):
        return pltpu.make_async_remote_copy(
            src_ref=packed.at[yd, zs],
            dst_ref=relay.at[zs],
            send_sem=y_send.at[yd * SIDE + zs],
            recv_sem=relay_recv.at[zs],
            device_id=at(jnp.where(y == 0, SIDE - 1, 2), z),
            device_id_type=MESH,
        )

    def relay_copy(zs):
        return pltpu.make_async_remote_copy(
            src_ref=relay.at[zs],
            dst_ref=out_ref.at[far_at(3 - y, zs)],
            send_sem=relay_send.at[zs],
            recv_sem=far_recv.at[(3 - y) * SIDE + zs],
            device_id=at(5 - y, z),
            device_id_type=MESH,
        )

    def keep(zs):
        return pltpu.make_async_copy(row.at[zs], out_ref.at[pl.ds(zs * PER, PER)], keep_sem.at[zs])

    def wanted(zs):
        inside = (zs >= 0) & (zs < SIDE)
        return inside, inside & ((zs <= z) | (y < SIDE - 1))

    def pack(yd, zs):
        first = (yd * SIDE + zs) * CAP
        if lists:
            blocks_ref, count_ref = lists[:2]
            picks_ref[first], picks_ref[first + 1] = chosen(
                blocks_ref, count_ref, yd * SIDE + z, y * SIDE + zs
            )
        for c in range(CAP):
            pick = picks_ref[first + c]
            block = row[zs, 0]
            for t in range(1, PER):
                block = jnp.where(pick == t, row[zs, t], block)
            packed[yd, zs, c] = block

    def step(n):
        zs, d = nth(n, z)
        inside, mine = wanted(zs)

        @pl.when(mine)
        def _():
            pl.when(d > 0)(lambda: z_copy(zs, z, up_send).wait_recv())
            pl.when((zs <= z) & (z < SIDE - 1))(lambda: z_copy(zs, z + 1, up_send).start())
            pl.when((zs >= z) & (z > 0) & (y < SIDE - 1))(
                lambda: z_copy(zs, z - 1, down_send).start()
            )
            keep(zs).start()

        @pl.when(inside)
        def _():
            @pl.loop(0, SIDE - 1 - y)
            def _(h):
                hop = jnp.where(y == 2, 1, jnp.where(h == 0, 2, jnp.where(h == 1, 1, 3)))
                yd = y + hop
                pack(yd, zs)
                pl.when(hop == 2)(lambda: y_far(yd, zs).start())
                pl.when(hop != 2)(lambda: y_near(yd, zs).start())

    def relay_step(n):
        zs, _ = nth(n, z)

        @pl.when((zs >= 0) & (zs < SIDE) & (y >= 2))
        def _():
            pltpu.make_async_remote_copy(
                src_ref=relay.at[zs],
                dst_ref=relay.at[zs],
                send_sem=relay_send.at[zs],
                recv_sem=relay_recv.at[zs],
                device_id=at(y, z),
                device_id_type=MESH,
            ).wait_recv()
            relay_copy(zs).start()

    def arrived():
        @pl.loop(0, y * SIDE)
        def _(n):
            pltpu.make_async_remote_copy(
                src_ref=packed.at[0, 0],
                dst_ref=out_ref.at[pl.ds(ROW + n * CAP, CAP)],
                send_sem=relay_send.at[0],
                recv_sem=far_recv.at[n],
                device_id=at(y, z),
                device_id_type=MESH,
            ).wait_recv()

        @pl.loop(0, SIDE)
        def _(zs):
            _, mine = wanted(zs)
            pl.when(mine)(lambda: keep(zs).wait())

    def sent():
        @pl.loop(0, SIDE)
        def _(zs):
            _, mine = wanted(zs)

            @pl.when(mine)
            def _():
                pl.when((zs <= z) & (z < SIDE - 1))(
                    lambda: z_copy(zs, z + 1, up_send).wait_send()
                )
                pl.when((zs >= z) & (z > 0) & (y < SIDE - 1))(
                    lambda: z_copy(zs, z - 1, down_send).wait_send()
                )

            @pl.loop(y + 1, SIDE)
            def _(yd):
                y_near(yd, zs).wait_send()

            pl.when(y >= 2)(lambda: relay_copy(zs).wait_send())

    return Steps(load=load, loaded=loaded, step=step, relay=relay_step, arrived=arrived, sent=sent)


def return_scratch(sems):
    bf16 = jnp.bfloat16
    return [
        pltpu.VMEM((SIDE * (SIDE - 1), CAP, BLOCK, 2 * D), bf16),
        pltpu.VMEM((SIDE, SIDE, CAP, BLOCK, 2 * D), bf16),
        pltpu.VMEM((SIDE, CAP, BLOCK, 2 * D), bf16),
        pltpu.VMEM((SIDE, PER, BLOCK, 2 * D), bf16),
        pltpu.VMEM((SIDE, PER, BLOCK, 2 * D), bf16),
        pltpu.VMEM((SIDE, PER, BLOCK, 2 * D), bf16),
        pltpu.VMEM((PER, BLOCK, 2 * D), jnp.float32),
        sems(CTX),
        sems(CTX),
        sems(SIDE),
        sems(SIDE),
        sems(2 * SIDE),
        sems(2 * SIDE),
        sems(2 * SIDE),
    ]


def give_back(picks_ref, slot_of, slots_ref, scratch):
    (far, landed, relay, running, from_left, from_right, total,
     y_send, y_recv, relay_send, relay_recv, z_send, left_recv, right_recv) = scratch
    me, y, z = coords()

    def gathered(e):
        out = jnp.zeros((BLOCK, 2 * D), jnp.float32)
        for r in range(PER):
            slot = slot_of[e * PER + r]
            got = slots_ref[jnp.maximum(slot, 0)]
            out = out + jnp.where(slot >= 0, got, jnp.zeros_like(got)).astype(jnp.float32)
        return out

    def y_near(ys, zs):
        return pltpu.make_async_remote_copy(
            src_ref=far.at[ys * SIDE + zs],
            dst_ref=landed.at[y, zs],
            send_sem=y_send.at[ys * SIDE + zs],
            recv_sem=y_recv.at[y * SIDE + zs],
            device_id=at(ys, z),
            device_id_type=MESH,
        )

    def y_far(ys, zs):
        return pltpu.make_async_remote_copy(
            src_ref=far.at[ys * SIDE + zs],
            dst_ref=relay.at[zs],
            send_sem=y_send.at[ys * SIDE + zs],
            recv_sem=relay_recv.at[zs],
            device_id=at(5 - y, z),
            device_id_type=MESH,
        )

    def relay_copy(zs):
        return pltpu.make_async_remote_copy(
            src_ref=relay.at[zs],
            dst_ref=landed.at[5 - y, zs],
            send_sem=relay_send.at[zs],
            recv_sem=y_recv.at[(5 - y) * SIDE + zs],
            device_id=at(3 - y, z),
            device_id_type=MESH,
        )

    def z_copy(zs, half, to, landing, sems):
        blocks = pl.ds(2 * half, 2)
        return pltpu.make_async_remote_copy(
            src_ref=running.at[zs, blocks],
            dst_ref=landing.at[zs, blocks],
            send_sem=z_send.at[2 * zs + half],
            recv_sem=sems.at[2 * zs + half],
            device_id=at(y, to),
            device_id_type=MESH,
        )

    def send(j):
        zs = target(j, z)

        @pl.loop(0, y)
        def _(h):
            hop = jnp.where(y == 1, 1, jnp.where(h == 0, 2, jnp.where(h == 1, 1, 3)))
            ys = y - hop
            for c in range(CAP):
                far[ys * SIDE + zs, c] = gathered(ROW + (ys * SIDE + zs) * CAP + c).astype(far.dtype)
            pl.when(hop == 2)(lambda: y_far(ys, zs).start())
            pl.when(hop != 2)(lambda: y_near(ys, zs).start())

    def pass_on(j):
        zs = target(j, z)

        @pl.when(y >= 2)
        def _():
            pltpu.make_async_remote_copy(
                src_ref=relay.at[zs],
                dst_ref=relay.at[zs],
                send_sem=relay_send.at[zs],
                recv_sem=relay_recv.at[zs],
                device_id=at(y, z),
                device_id_type=MESH,
            ).wait_recv()
            relay_copy(zs).start()

    def add_up(j):
        zs = target(j, z)

        @pl.when((zs <= z) | (y < SIDE - 1))
        def _():
            for t in range(PER):
                total[t] = gathered(zs * PER + t)

            @pl.loop(y + 1, SIDE)
            def _(yd):
                pltpu.make_async_remote_copy(
                    src_ref=landed.at[yd, zs],
                    dst_ref=landed.at[yd, zs],
                    send_sem=relay_send.at[0],
                    recv_sem=y_recv.at[yd * SIDE + zs],
                    device_id=at(y, z),
                    device_id_type=MESH,
                ).wait_recv()
                for t in range(PER):
                    low, high = landed[yd, zs, 0], landed[yd, zs, 1]
                    got = jnp.where(picks_ref[(yd * SIDE + zs) * CAP + 1] == t, high, jnp.zeros_like(high))
                    got = jnp.where(picks_ref[(yd * SIDE + zs) * CAP] == t, low, got)
                    total[t] += got.astype(jnp.float32)

            @pl.loop(0, 2)
            def _(half):
                blocks = pl.ds(2 * half, 2)

                @pl.when((zs <= z) & (z < SIDE - 1))
                def _():
                    z_copy(zs, half, z, from_right, right_recv).wait_recv()
                    total[blocks] += from_right[zs, blocks].astype(jnp.float32)

                @pl.when((zs >= z) & (z > 0) & (y < SIDE - 1))
                def _():
                    z_copy(zs, half, z, from_left, left_recv).wait_recv()
                    total[blocks] += from_left[zs, blocks].astype(jnp.float32)

                @pl.when(zs != z)
                def _():
                    running[zs, blocks] = total[blocks].astype(running.dtype)
                    pl.when(zs < z)(lambda: z_copy(zs, half, z - 1, from_right, right_recv).start())
                    pl.when(zs > z)(lambda: z_copy(zs, half, z + 1, from_left, left_recv).start())

    def sent():
        @pl.loop(0, SIDE)
        def _(zs):
            @pl.when((zs < z) | ((zs > z) & (y < SIDE - 1)))
            def _():
                for half in range(2):
                    z_copy(zs, half, z, from_right, right_recv).wait_send()

            @pl.loop(0, y)
            def _(ys):
                y_near(ys, zs).wait_send()

            pl.when(y >= 2)(lambda: relay_copy(zs).wait_send())

    return Steps(send=send, pass_on=pass_on, add_up=add_up, sent=sent, total=total)


N_ATTEND, N_EXCHANGE, N_RETURN = 13, 12, 14


def gather_and_attend(
    blocks_ref, count_ref, len_ref, k_ref, v_ref, q_ref, do_ref,
    held_0, held_1, table_ref, attn_ref, dq_ref, slots_ref, *scratch,
):
    picks, place, seen, slot_of = parts(table_ref)
    _, y, z = coords()
    lists = (blocks_ref, count_ref, len_ref, place, seen, slot_of)
    attention = Attention(0, place, seen, q_ref, do_ref, held_0, attn_ref, dq_ref, slots_ref, scratch[:N_ATTEND])
    scratch = scratch[N_ATTEND:]
    first = exchange(0, picks, k_ref, v_ref, held_0, scratch[:N_EXCHANGE], lists)
    second = exchange(1, picks, k_ref, v_ref, held_1, scratch[N_EXCHANGE:], None)
    first.load()
    second.load()
    attention.start()
    barrier_neighbours(y, z)
    first.loaded()
    first.step(jnp.int32(0))
    tables(*lists)
    second.loaded()

    @pl.loop(1, STEPS)
    def _(n):
        first.step(n)
        first.relay(n - 1)

    second.step(jnp.int32(0))
    first.relay(jnp.int32(STEPS - 1))

    @pl.loop(1, 3)
    def _(n):
        second.step(n)
        second.relay(n - 1)

    first.arrived()
    attention.wait()

    def between(k):
        pl.loop(*listed(k, {0: (3, 5), 4: (5, 7)}))(second.step)
        pl.loop(*listed(k, {0: (2, 3), 2: (3, 5), 7: (5, 7)}))(second.relay)

    attention.run(between)
    second.arrived()
    first.sent()
    second.sent()


def attend_and_return(
    table_ref, q_ref, do_ref, held_ref, done_ref,
    gk_ref, gv_ref, attn_ref, dq_ref, slots_ref, *scratch,
):
    picks, place, seen, slot_of = parts(table_ref)
    _, y, z = coords()
    attention = Attention(1, place, seen, q_ref, do_ref, held_ref, attn_ref, dq_ref, slots_ref, scratch[:N_ATTEND])
    scratch = scratch[N_ATTEND:]
    first = give_back(picks, slot_of, done_ref, scratch[:N_RETURN])
    second = give_back(picks, slot_of, slots_ref, scratch[N_RETURN:])
    attention.start()
    attention.load_held()
    barrier_neighbours(y, z)
    first.send(jnp.int32(0))
    attention.wait_all()

    def between(k):
        pl.loop(*listed(k, {4: (0, 1), 7: (1, 2), 10: (2, 3)}))(first.add_up)
        pl.loop(*listed(k, {1: (0, 1), 4: (1, 2), 7: (2, 3), 10: (3, 4)}))(first.pass_on)
        pl.loop(*listed(k, {1: (1, 2), 4: (2, 3), 7: (3, 4)}))(first.send)

    attention.run(between)
    second.send(jnp.int32(0))
    first.add_up(jnp.int32(SIDE - 1))

    @pl.loop(0, SIDE)
    def _(j):
        second.pass_on(j)
        pl.when(j < SIDE - 1)(lambda: second.send(j + 1))
        second.add_up(j)

    for part, lanes in ((first, slice(0, D)), (second, slice(D, 2 * D))):
        for t in range(PER):
            rows = pl.ds(t * BLOCK, BLOCK)
            gk_ref[rows, lanes] = part.total[t, :, :D].astype(gk_ref.dtype)
            gv_ref[rows, lanes] = part.total[t, :, D:].astype(gv_ref.dtype)
    first.sent()
    second.sent()


def body(query_states, key_states, value_state_rows, grad_out, vis_blocks, vis_count, vis_len):
    tokens, q_width = query_states.shape
    width = key_states.shape[1]
    lanes = q_width * D // width
    bf16 = jnp.bfloat16
    sems = lambda n: pltpu.SemaphoreType.DMA((n,))
    smem = pl.BlockSpec(memory_space=pltpu.SMEM)
    vmem = pl.BlockSpec(memory_space=pltpu.VMEM)
    hbm = pl.BlockSpec(memory_space=pltpu.HBM)
    shape = jax.ShapeDtypeStruct
    held = shape((HELD, BLOCK, 2 * D), bf16)
    half = shape((tokens, lanes), bf16)
    slots = shape((PER * VIS, BLOCK, 2 * D), bf16)
    whole = shape((tokens, width), bf16)

    def remote(n, mib):
        return pltpu.CompilerParams(collective_id=n, has_side_effects=True, vmem_limit_bytes=mib * MIB)

    keys = key_states.reshape(PER, BLOCK, width)
    values = value_state_rows.reshape(PER, BLOCK, width)

    table = shape((CTX * CAP + 2 * PER * VIS + PER * HELD,), jnp.int32)
    _, held_1, tables_out, attn_0, dq_0, slots_0 = pl.pallas_call(
        gather_and_attend,
        out_shape=(held, held, table, half, half, slots),
        in_specs=[smem] * 3 + [hbm] * 4,
        out_specs=(hbm,) * 2 + (smem,) + (vmem,) * 3,
        scratch_shapes=Attention.scratch(tokens, lanes) + 2 * exchange_scratch(sems),
        compiler_params=remote(0, 58),
    )(vis_blocks.T, vis_count, vis_len.T, keys, values, query_states, grad_out)
    grad_key, grad_value, attn_1, dq_1, _ = pl.pallas_call(
        attend_and_return,
        out_shape=(whole, whole, half, half, slots),
        in_specs=[smem] + [hbm] * 3 + [vmem],
        out_specs=(vmem,) * 5,
        scratch_shapes=Attention.scratch(tokens, lanes) + 2 * return_scratch(sems),
        compiler_params=remote(1, 48),
    )(tables_out, query_states, grad_out, held_1, slots_0)
    attention = jnp.concatenate([attn_0, attn_1], axis=1)
    grad_query = jnp.concatenate([dq_0, dq_1], axis=1)
    return attention, grad_query, grad_key, grad_value


def solution(mesh):
    rows = P(("dp", "ctx"), "head")
    return jax.shard_map(
        body,
        mesh=mesh,
        in_specs=(rows, rows, rows, rows, P("dp", None), P("dp"), P("dp", None)),
        out_specs=(rows, rows, rows, rows),
        check_vma=False,
    )
```
